32 devices in a mesh: dp: 8 (over z, y), head: 4 (over x, core).
Axes of the slice: x: 2, y: 2, z: 4, core: 2. Of those that a mesh axis runs over, the one named last changes fastest.
Arguments:
- node_rows: bfloat16 [4096, 768], P(('dp', 'head')), may hold values from -6 to 6
- output_grad: bfloat16 [4096, 768], P(('dp', 'head')), may hold values from -6 to 6
- weight_in: float32 [4, 768, 768], P(None, 'dp', 'head'), may hold values from -0.21875 to 0.21875
- first_in: float32 [4, 768, 768], P(None, 'dp', 'head'), may hold values from -0.0008544922 to 0.0008544922
- second_in: float32 [4, 768, 768], P(None, 'dp', 'head'), may hold values from 2.6260505e-10 to 1.0504202e-09
- weight_out: float32 [768, 768], P('head', 'dp'), may hold values from -0.875 to 0.875
- first_out: float32 [768, 768], P('head', 'dp'), may hold values from -0.0008544922 to 0.0008544922
- second_out: float32 [768, 768], P('head', 'dp'), may hold values from 2.6260505e-10 to 1.0504202e-09
- weight_down: float32 [768, 768], P('head', 'dp'), may hold values from -0.21875 to 0.21875
- first_down: float32 [768, 768], P('head', 'dp'), may hold values from -0.0008544922 to 0.0008544922
- second_down: float32 [768, 768], P('head', 'dp'), may hold values from 2.6260505e-10 to 1.0504202e-09
- vectors: float32 [9, 768], P(None, ('dp', 'head')), may hold values from -0.9 to 1.9
- first_vectors: float32 [9, 768], P(None, ('dp', 'head')), may hold values from -0.0008544922 to 0.0008544922
- second_vectors: float32 [9, 768], P(None, ('dp', 'head')), may hold values from 2.6260505e-10 to 1.0504202e-09
- bias_table: float32 [8192, 32], P('dp', 'head'), may hold values from -3 to 3
- first_table: float32 [8192, 32], P('dp', 'head'), may hold values from -0.0008544922 to 0.0008544922
- second_table: float32 [8192, 32], P('dp', 'head'), may hold values from 2.6260505e-10 to 1.0504202e-09
- big_counts: int32 [8], P('dp'), may hold values from 1 to 256, 1536 in all
- small_counts: int32 [8, 4], P('dp'), may hold values from 1 to 64, 160 in all within a row
- big_distance: int32 [8, 256, 256], P('dp'), may hold values from 0 to 511
- small_distance: int32 [32, 64, 64], P('dp'), may hold values from 0 to 511
- big_paths: int32 [5, 8, 256, 256], P(None, 'dp'), may hold values from 0 to 1535
- small_paths: int32 [5, 32, 64, 64], P(None, 'dp'), may hold values from 0 to 1535
- big_lengths: int32 [8, 256, 256], P('dp'), may hold values from 1 to 5
- small_lengths: int32 [32, 64, 64], P('dp'), may hold values from 1 to 5
Outputs:
- layer_out: bfloat16 [4096, 768], P(('dp', 'head'))
- input_grad: bfloat16 [4096, 768], P(('dp', 'head'))
- grad_norm: float32 [], replicated
- weight_in_new: float32 [4, 768, 768], P(None, 'dp', 'head')
- first_in_new: float32 [4, 768, 768], P(None, 'dp', 'head')
- second_in_new: float32 [4, 768, 768], P(None, 'dp', 'head')
- weight_out_new: float32 [768, 768], P('head', 'dp')
- first_out_new: float32 [768, 768], P('head', 'dp')
- second_out_new: float32 [768, 768], P('head', 'dp')
- weight_down_new: float32 [768, 768], P('head', 'dp')
- first_down_new: float32 [768, 768], P('head', 'dp')
- second_down_new: float32 [768, 768], P('head', 'dp')
- vectors_new: float32 [9, 768], P(None, ('dp', 'head'))
- first_vectors_new: float32 [9, 768], P(None, ('dp', 'head'))
- second_vectors_new: float32 [9, 768], P(None, ('dp', 'head'))
- bias_table_new: float32 [8192, 32], P('dp', 'head')
- first_table_new: float32 [8192, 32], P('dp', 'head')
- second_table_new: float32 [8192, 32], P('dp', 'head')
The draws below stay inside these ranges and needn't reach their ends.
Inputs may be any that keep to these rules, and one draw needn't show every extreme that they name: `big_counts`: at least one large bucket in all is full; all counts sum to 3/4 of all large slots. `small_counts`: one small bucket of each index of dp is full.
All inputs are finite; a program needn't handle non-finite values. No bound on the sum of `big_counts` on one device may be relied on, other than what follows from the above.
Results may differ from the reference program's by a relative error of at most 0.015.
Values may be sent and summed in bfloat16 or wider, within the bound.
No kernel may reach another device: no remote copies, remote signals or barrier semaphores. Data moves between devices by JAX's collectives and lax.ppermute only.
A program may use at most 576 MiB of HBM per device.

```python
import math
import jax
import jax.numpy as jnp
import numpy as np
from jax import lax

D = 768
HEADS = 32
HEAD_DIM = 24
NDIST = 512
NTYPE = 1536
STEPS = 5
VECS = 9
ADAM_STEP = 10
WBIG = 256
WSMALL = 64
BIGB = 1
NSB = 4
TOK_DEV = 512
TOKENS = 4096
TAB = 8192
N_DP = 8


def draw_vectors(key, part):
    row_index = lax.broadcasted_iota(jnp.int32, (VECS, D), 0)
    is_gain = (row_index == 0) | (row_index == 2)
    noise = jnp.clip(0.35 * jax.random.normal(key, (VECS, D), jnp.float32), -0.9, 0.9)
    return jnp.where(is_gain, 1.0 + noise, noise)


def with_ends(values, own_key, low, top_value):
    shape = values.shape
    index_at = [jax.random.randint(jax.random.fold_in(own_key, axis), (), 0, shape[axis]) for axis in range(len(shape))]
    values = values.at[tuple(index_at)].set(low)
    longest = shape.index(max(shape))
    index_at[longest] = (index_at[longest] + 1) % shape[longest]
    return values.at[tuple(index_at)].set(top_value)


def level_of(own_key, shape, pieces, least, high):
    gain = 1.0
    for position, shards_of in pieces:
        heights = jax.random.uniform(jax.random.fold_in(jax.random.fold_in(own_key, 6), position), (shards_of,), jnp.float32, least / len(pieces), high / len(pieces))
        gain = gain * jnp.repeat(jnp.exp(heights), shape[position] // shards_of).reshape((-1,) + (1,) * (len(shape) - 1 - position))
    return gain


def length_profile(number_of, total, most, lean):
    weights = [(1 << 20) // math.isqrt(grade ** lean) + 1 for grade in range(2, number_of + 1)]
    rest, given = total - most - (number_of - 1), [1] * (number_of - 1)
    while rest > 0:
        candidates = [i for i in range(number_of - 1) if given[i] < most]
        mass, budget = sum([weights[i] for i in candidates]), rest
        for i in candidates:
            extra = min(most - given[i], max(1, budget * weights[i] // mass), rest)
            given[i] = given[i] + extra
            rest = rest - extra
    return np.array([most] + given)


def uneven_parts(stream_key, number_of, total, reach, skew):
    if number_of == 2:
        one = jax.random.randint(stream_key, (), max(1, total - reach), min(reach, total - 1) + 1)
        return jnp.stack([one, total - one])
    tallies = jnp.asarray(length_profile(number_of, total, reach, skew), jnp.int32)
    twos = (number_of - 1) // 2
    source_of, taker = tallies[1:1 + 2 * twos:2], tallies[2:2 + 2 * twos:2]
    slack = jnp.minimum(source_of - 1, reach - taker)
    passed = jax.random.randint(jax.random.fold_in(stream_key, 1), (twos,), 0, 1 << 20) % (slack + 1)
    tallies = tallies.at[1:1 + 2 * twos:2].set(source_of - passed).at[2:2 + 2 * twos:2].set(taker + passed)
    return tallies[jax.random.permutation(jax.random.fold_in(stream_key, 2), number_of)]


def gaussian(own_key, shape, width, reach, cuts=(), held_as=jnp.bfloat16):
    drawn = jax.random.normal(own_key, shape, jnp.float32) * width
    if len(cuts) > 0:
        drawn = level_of(own_key, shape, cuts, -0.22, 0.18) * drawn
    return jnp.clip(drawn, min=-reach, max=reach).astype(held_as)


def setup_inputs(seed: int = 0) -> dict:
    key_of = jax.random.split(jax.random.key(seed), 26)
    return {
        "node_rows": gaussian(key_of[0], (TOKENS, D), 1.0, 6.0, ((0, 32),)),
        "output_grad": gaussian(key_of[1], (TOKENS, D), 1.0, 6.0, ((0, 32),)),
        "weight_in": gaussian(key_of[2], (4, D, D), D ** -0.5, 0.21875, ((1, 8), (2, 4)), jnp.float32),
        "first_in": gaussian(key_of[3], (4, D, D), (0.11 / (6 * D * D + VECS * D + TAB * HEADS) ** 0.5), 0.0008544922, ((1, 8), (2, 4)), jnp.float32),
        "second_in": jnp.clip(jnp.exp(math.log(1.0504201952699077e-09) - 1.3862944 * jax.random.uniform(key_of[4], (4, D, D), jnp.float32) ** level_of(key_of[4], (4, D, D), ((1, 8), (2, 4)), -0.2, 0.2)), 2.6260504881747693e-10, 1.0504201952699077e-09),
        "weight_out": gaussian(key_of[5], (D, D), (D // 16) ** -0.5, 0.875, ((0, 4), (1, 8)), jnp.float32),
        "first_out": gaussian(key_of[6], (D, D), (0.11 / (6 * D * D + VECS * D + TAB * HEADS) ** 0.5), 0.0008544922, ((0, 4), (1, 8)), jnp.float32),
        "second_out": jnp.clip(jnp.exp(math.log(1.0504201952699077e-09) - 1.3862944 * jax.random.uniform(key_of[7], (D, D), jnp.float32) ** level_of(key_of[7], (D, D), ((0, 4), (1, 8)), -0.2, 0.2)), 2.6260504881747693e-10, 1.0504201952699077e-09),
        "weight_down": gaussian(key_of[8], (D, D), D ** -0.5, 0.21875, ((0, 4), (1, 8)), jnp.float32),
        "first_down": gaussian(key_of[9], (D, D), (0.11 / (6 * D * D + VECS * D + TAB * HEADS) ** 0.5), 0.0008544922, ((0, 4), (1, 8)), jnp.float32),
        "second_down": jnp.clip(jnp.exp(math.log(1.0504201952699077e-09) - 1.3862944 * jax.random.uniform(key_of[10], (D, D), jnp.float32) ** level_of(key_of[10], (D, D), ((0, 4), (1, 8)), -0.2, 0.2)), 2.6260504881747693e-10, 1.0504201952699077e-09),
        "vectors": draw_vectors(jax.random.fold_in(key_of[25], 71), 0),
        "first_vectors": gaussian(key_of[12], (VECS, D), (0.11 / (6 * D * D + VECS * D + TAB * HEADS) ** 0.5), 0.0008544922, ((1, 32),), jnp.float32),
        "second_vectors": jnp.clip(jnp.exp(math.log(1.0504201952699077e-09) - 1.3862944 * jax.random.uniform(key_of[13], (VECS, D), jnp.float32) ** level_of(key_of[13], (VECS, D), ((1, 32),), -0.2, 0.2)), 2.6260504881747693e-10, 1.0504201952699077e-09),
        "bias_table": gaussian(key_of[14], (TAB, HEADS), 0.5, 3.0, ((0, 8), (1, 4)), jnp.float32),
        "first_table": gaussian(key_of[15], (TAB, HEADS), (0.11 / (6 * D * D + VECS * D + TAB * HEADS) ** 0.5), 0.0008544922, ((0, 8), (1, 4)), jnp.float32),
        "second_table": jnp.clip(jnp.exp(math.log(1.0504201952699077e-09) - 1.3862944 * jax.random.uniform(key_of[16], (TAB, HEADS), jnp.float32) ** level_of(key_of[16], (TAB, HEADS), ((0, 8), (1, 4)), -0.2, 0.2)), 2.6260504881747693e-10, 1.0504201952699077e-09),
        "big_counts": uneven_parts(key_of[17], N_DP * BIGB, N_DP * BIGB * WBIG * 3 // 4, WBIG, 0).astype(jnp.int32),
        "small_counts": jax.vmap(lambda own: uneven_parts(own, NSB, NSB * WSMALL * 5 // 8, WSMALL, 2))(jax.random.split(key_of[18], N_DP)).reshape((N_DP, NSB)).astype(jnp.int32),
        "big_distance": with_ends(jax.random.randint(key_of[19], (N_DP * BIGB, WBIG, WBIG), 0, NDIST), jax.random.fold_in(key_of[19], 1), 0, NDIST - 1).astype(jnp.int32),
        "small_distance": with_ends(jax.random.randint(key_of[20], (N_DP * NSB, WSMALL, WSMALL), 0, NDIST), jax.random.fold_in(key_of[20], 1), 0, NDIST - 1).astype(jnp.int32),
        "big_paths": with_ends(jax.random.randint(key_of[21], (STEPS, N_DP * BIGB, WBIG, WBIG), 0, NTYPE), jax.random.fold_in(key_of[21], 1), 0, NTYPE - 1).astype(jnp.int32),
        "small_paths": with_ends(jax.random.randint(key_of[22], (STEPS, N_DP * NSB, WSMALL, WSMALL), 0, NTYPE), jax.random.fold_in(key_of[22], 1), 0, NTYPE - 1).astype(jnp.int32),
        "big_lengths": with_ends(jax.random.randint(key_of[23], (N_DP * BIGB, WBIG, WBIG), 1, STEPS + 1), jax.random.fold_in(key_of[23], 1), 1, STEPS).astype(jnp.int32),
        "small_lengths": with_ends(jax.random.randint(key_of[24], (N_DP * NSB, WSMALL, WSMALL), 1, STEPS + 1), jax.random.fold_in(key_of[24], 1), 1, STEPS).astype(jnp.int32),
    }


NORM_EPSILON = 1e-05
NEGATIVE_FILL = -1e+30
BETA_FIRST = 0.9
BETA_SECOND = 0.95
ADAM_EPSILON = 1e-08
RATE_MATRIX = 0.02
RATE_OUTPUT = 0.05
RATE_VECTOR = 0.15
WEIGHT_DECAY = 0.01
CLIP_NORM = 1.0

@jax.custom_vjp
def low(v):
    return lax.optimization_barrier(v.astype(jnp.bfloat16)).astype(jnp.float32)

@jax.custom_vjp
def low_back(v):
    return v

def low_keep(v):
    return (low(v), None)

def low_pass(kept, grad):
    return (grad,)

def back_keep(v):
    return (v, None)

def back_low(kept, grad):
    return (low(grad),)
low.defvjp(low_keep, low_pass)
low_back.defvjp(back_keep, back_low)

def exact_dot(left, right):
    return jnp.dot(left, right, precision=lax.Precision.HIGHEST)

def norm_rows(values, norm_gain, norm_shift):
    center = values - lax.optimization_barrier(jnp.mean(values, axis=-1, keepdims=True))
    spread = lax.optimization_barrier(jnp.mean(center * center, axis=-1, keepdims=True))
    return center * lax.rsqrt(spread + NORM_EPSILON) * norm_gain + norm_shift

def pair_bias(table, dist_block, path_block, length_block):
    bias_total = jnp.take(table, dist_block, axis=0)
    edge_bias = jnp.zeros_like(bias_total)
    for hop_step in range(STEPS):
        looked = jnp.take(table, NDIST + hop_step * NTYPE + path_block[hop_step], axis=0)
        edge_bias = edge_bias + jnp.where((length_block > hop_step)[..., None], looked, 0.0)
    bias_total = bias_total + edge_bias / length_block[..., None].astype(jnp.float32)
    return jnp.transpose(bias_total, (0, 3, 1, 2))

def block_math(table, query_block, key_block, value_block, count_block, dist_block, path_block, length_block):
    raw_scores = jnp.einsum('bqhd,bkhd->bhqk', query_block, key_block, precision=lax.Precision.HIGHEST) * HEAD_DIM ** (-0.5)
    raw_scores = raw_scores + pair_bias(table, dist_block, path_block, length_block)
    bucket_width = key_block.shape[1]
    key_valid = jnp.arange(bucket_width)[None, :] < count_block[:, None]
    raw_scores = low_back(jnp.where(key_valid[:, None, None, :], raw_scores, NEGATIVE_FILL))
    prob_low = low(jax.nn.softmax(raw_scores, axis=-1))
    return jnp.einsum('bhqk,bkhd->bqhd', prob_low, value_block, precision=lax.Precision.HIGHEST)

def attend_part(queries, keys, values, table, counts, distance, paths, lengths, per_block):
    bucket_width = distance.shape[-1]
    block_total = counts.shape[0] // per_block

    def head_shape(tensor):
        return tensor.reshape(block_total, per_block, bucket_width, HEADS, HEAD_DIM)
    block_items = (head_shape(queries), head_shape(keys), head_shape(values), counts.reshape(block_total, per_block), distance.reshape(block_total, per_block, bucket_width, bucket_width), jnp.moveaxis(paths.reshape(STEPS, block_total, per_block, bucket_width, bucket_width), 1, 0), lengths.reshape(block_total, per_block, bucket_width, bucket_width))
    checked = jax.checkpoint(block_math)

    def one_block(items_now):
        return checked(table, *items_now)
    mixed_out = lax.map(one_block, block_items)
    return mixed_out.reshape(queries.shape[0], HEADS * HEAD_DIM)

def layer(inputs, weights, integer_data):
    weight_in, weight_out, weight_down, vectors, bias_table = weights
    big_count, small_count, big_dist, small_dist, big_path, small_path, big_len, small_len = integer_data
    proj_in = low(weight_in)
    proj_out = low(weight_out)
    proj_down = low(weight_down)
    table = low(bias_table)
    normed_one = low(norm_rows(inputs, vectors[0], vectors[1]))
    queries = low(low_back(exact_dot(normed_one, proj_in[0]) + vectors[4]))
    keys = low(low_back(exact_dot(normed_one, proj_in[1])))
    values = low(low_back(exact_dot(normed_one, proj_in[2]) + vectors[5]))
    big_rows = BIGB * WBIG
    big_out = attend_part(queries[:big_rows], keys[:big_rows], values[:big_rows], table, big_count, big_dist, big_path, big_len, BIGB)
    small_out = attend_part(queries[big_rows:], keys[big_rows:], values[big_rows:], table, small_count, small_dist, small_path, small_len, 4)
    heads_out = low(low_back(jnp.concatenate([big_out, small_out], axis=0)))
    hidden = inputs + low_back(exact_dot(heads_out, proj_out)) + vectors[6]
    normed_two = low(norm_rows(hidden, vectors[2], vectors[3]))
    pre_act = low_back(exact_dot(normed_two, proj_in[3]) + vectors[7])
    activation = low(jax.nn.gelu(pre_act, approximate=False))
    return hidden + exact_dot(activation, proj_down) + vectors[8]

def adamw_update(weight, first_moment, second_moment, gradient, learn_rate):
    first_new = BETA_FIRST * first_moment + (1.0 - BETA_FIRST) * gradient
    second_new = BETA_SECOND * second_moment + (1.0 - BETA_SECOND) * gradient * gradient
    first_hat = first_new / (1.0 - BETA_FIRST ** ADAM_STEP)
    second_hat = second_new / (1.0 - BETA_SECOND ** ADAM_STEP)
    weight_new = weight - learn_rate * (first_hat / (jnp.sqrt(second_hat) + ADAM_EPSILON) + WEIGHT_DECAY * weight)
    return (weight_new, first_new, second_new)

def reference(node_rows, output_grad, weight_in, first_in, second_in, weight_out, first_out, second_out, weight_down, first_down, second_down, vectors, first_vectors, second_vectors, bias_table, first_table, second_table, big_counts, small_counts, big_distance, small_distance, big_paths, small_paths, big_lengths, small_lengths):
    params = (weight_in, weight_out, weight_down, vectors, bias_table)
    group_items = (node_rows.reshape(N_DP, TOK_DEV, D), output_grad.reshape(N_DP, TOK_DEV, D), big_counts.reshape(N_DP, BIGB), small_counts, big_distance.reshape(N_DP, BIGB, WBIG, WBIG), small_distance.reshape(N_DP, NSB, WSMALL, WSMALL), jnp.moveaxis(big_paths.reshape(STEPS, N_DP, BIGB, WBIG, WBIG), 1, 0), jnp.moveaxis(small_paths.reshape(STEPS, N_DP, NSB, WSMALL, WSMALL), 1, 0), big_lengths.reshape(N_DP, BIGB, WBIG, WBIG), small_lengths.reshape(N_DP, NSB, WSMALL, WSMALL))

    def group_step(totals, items_now):
        rows_in, rows_grad = (items_now[0], items_now[1])
        integer_data = items_now[2:]

        def forward(inputs, weights):
            return layer(inputs, weights, integer_data)
        result, pull_back = jax.vjp(forward, rows_in.astype(jnp.float32), params)
        grad_inputs, grad_params = pull_back(rows_grad.astype(jnp.float32))
        totals = jax.tree.map(jnp.add, totals, grad_params)
        return (totals, (result.astype(jnp.bfloat16), grad_inputs.astype(jnp.bfloat16)))
    zero_grads = jax.tree.map(jnp.zeros_like, params)
    grads, (layer_out, input_grad) = lax.scan(group_step, zero_grads, group_items)
    square_total = jnp.zeros((), jnp.float32)
    for gradient in grads:
        square_total = square_total + jnp.sum(gradient * gradient)
    grad_norm = jnp.sqrt(square_total)
    clip_factor = CLIP_NORM / jnp.maximum(grad_norm, CLIP_NORM)
    new_in = adamw_update(weight_in, first_in, second_in, grads[0] * clip_factor, RATE_MATRIX)
    new_out = adamw_update(weight_out, first_out, second_out, grads[1] * clip_factor, RATE_OUTPUT)
    new_down = adamw_update(weight_down, first_down, second_down, grads[2] * clip_factor, RATE_MATRIX)
    new_vectors = adamw_update(vectors, first_vectors, second_vectors, grads[3] * clip_factor, RATE_VECTOR)
    new_table = adamw_update(bias_table, first_table, second_table, grads[4] * clip_factor, RATE_VECTOR)
    return (layer_out.reshape(TOKENS, D), input_grad.reshape(TOKENS, D), grad_norm, new_in[0], new_in[1], new_in[2], new_out[0], new_out[1], new_out[2], new_down[0], new_down[1], new_down[2], new_vectors[0], new_vectors[1], new_vectors[2], new_table[0], new_table[1], new_table[2])
```

```python
import jax
import jax.numpy as jnp
from jax import lax
from jax.experimental import pallas as pl
from jax.experimental.pallas import tpu as pltpu
from jax.sharding import PartitionSpec as P

HEAD_DIM = 24
NDIST = 512
NTYPE = 1536
STEPS = 5
ADAM_STEP = 10

NORM_EPSILON = 1e-05
NEGATIVE_FILL = -1e30
BETA_FIRST = 0.9
BETA_SECOND = 0.95
ADAM_EPSILON = 1e-08
RATE_MATRIX = 0.02
RATE_OUTPUT = 0.05
RATE_VECTOR = 0.15
WEIGHT_DECAY = 0.01
CLIP_NORM = 1.0

LANES = 128
SUB = 8
FIRST = [0] + [(NDIST + n * NTYPE) // LANES for n in range(STEPS)]
CHUNKS = [NDIST // LANES] + [NTYPE // LANES] * STEPS
LOOKUPS = STEPS + 1
SCALE = HEAD_DIM**-0.5
BF = jnp.bfloat16
F32 = jnp.float32
VMEM_BYTES = 48 << 20

NN = (((1,), (0,)), ((), ()))
NT = (((1,), (1,)), ((), ()))
TN = (((0,), (0,)), ((), ()))


def dot(left, right, dims):
    return lax.dot_general(left, right, dims, preferred_element_type=F32)


def kernel_call(body, outs, name, flops, nbytes, n_in=0, in_specs=None):
    return pl.pallas_call(
        body,
        out_shape=outs,
        in_specs=in_specs or [pl.BlockSpec(memory_space=pltpu.VMEM)] * n_in,
        name=name,
        compiler_params=pltpu.CompilerParams(vmem_limit_bytes=VMEM_BYTES),
        cost_estimate=pl.CostEstimate(flops=flops, bytes_accessed=nbytes, transcendentals=0),
    )


def pair_block(big, small, block, half, is_small):
    distance, paths, lengths = small if is_small else big
    rows = pl.ds(SUB * block, SUB)
    if is_small:

        def two(ref, *lead):
            return jnp.concatenate([ref[(*lead, 2 * half, rows)], ref[(*lead, 2 * half + 1, rows)]], axis=1)

        index = [two(distance)] + [two(paths, n) for n in range(STEPS)]
        return index, two(lengths)
    lanes = slice(LANES * half, LANES * half + LANES)
    index = [distance[0, rows, lanes]] + [paths[n, 0, rows, lanes] for n in range(STEPS)]
    return index, lengths[0, rows, lanes]


def each_block(big, small, step):
    width, narrow = big[0].shape[1], small[0].shape[1]
    halves, pairs = width // LANES, small[0].shape[0] // 2

    def big_step(block, carry):
        for half in range(halves):
            index, lengths = pair_block(big, small, block, half, False)
            step(index, lengths, (half * width + SUB * block) * SUB)
        return carry

    lax.fori_loop(0, width // SUB, big_step, 0)

    def small_step(block, carry):
        for pair in range(pairs):
            index, lengths = pair_block(big, small, block, pair, True)
            step(index, lengths, (halves * width + pair * narrow + SUB * block) * SUB)
        return carry

    lax.fori_loop(0, narrow // SUB, small_step, 0)


def hop_weights(lengths):
    inverse = 1.0 / lengths.astype(F32)
    return [None] + [jnp.where(lengths > n, inverse, 0.0) for n in range(STEPS)]


def pick(items, high):
    bit = 1
    while len(items) > 1:
        odd = (high & bit) != 0
        items = [
            jnp.where(odd, items[k + 1], items[k]) if k + 1 < len(items) else items[k]
            for k in range(0, len(items), 2)
        ]
        bit *= 2
    return items[0]


def bias_body(table, bd, bp, bl, sd, sp, sl, out):
    def step(index, lengths, base):
        weights = hop_weights(lengths)
        total = [None] * SUB
        for t in range(LOOKUPS):
            chunks = [table[SUB * (FIRST[t] + k) : SUB * (FIRST[t] + k + 1), :] for k in range(CHUNKS[t])]
            low, high = index[t] & (LANES - 1), index[t] >> 7
            for s in range(SUB):
                low_row = jnp.broadcast_to(low[s : s + 1], (SUB, LANES))
                high_row = jnp.broadcast_to(high[s : s + 1], (SUB, LANES))
                found = [
                    jnp.take_along_axis(c, low_row, axis=1, mode="promise_in_bounds") for c in chunks
                ]
                value = pick(found, high_row)
                if t > 0:
                    value = value * jnp.broadcast_to(weights[t][s : s + 1], (SUB, LANES))
                total[s] = value if total[s] is None else total[s] + value
        for s in range(SUB):
            out[pl.ds(base + SUB * s, SUB), :] = total[s]

    each_block((bd, bp, bl), (sd, sp, sl), step)


def scatter_body(grads, bd, bp, bl, sd, sp, sl, out):
    out[...] = jnp.zeros_like(out)
    sub = lax.broadcasted_iota(jnp.int32, (2 * SUB, LANES), 0)
    low_pattern = [(sub + 2 * SUB * k).astype(F32).astype(BF) for k in range(LANES // (2 * SUB))]
    upper = (sub >= SUB).astype(jnp.int32)
    high_pattern = [(2 * k + upper).astype(F32).astype(BF) for k in range(max(CHUNKS) // 2)]
    zero = jnp.zeros((2 * SUB, LANES), BF)

    def wide(row):
        return jnp.broadcast_to(row, (2 * SUB, LANES)).astype(BF)

    def step(index, lengths, base):
        weights = hop_weights(lengths)
        twice = []
        for s in range(SUB):
            g = grads[pl.ds(base + SUB * s, SUB), :]
            twice.append(jnp.concatenate([g, g], axis=0).astype(BF))
        for t in range(LOOKUPS):
            low, high = (index[t] & (LANES - 1)).astype(F32), (index[t] >> 7).astype(F32)
            left, right = [], []
            for s in range(SUB):
                low_row, high_row = wide(low[s : s + 1]), wide(high[s : s + 1])
                one = wide(weights[t][s : s + 1]) if t > 0 else jnp.ones((2 * SUB, LANES), BF)
                right.append(jnp.concatenate([jnp.where(low_row == p, one, zero) for p in low_pattern], axis=0))
                left.append(
                    jnp.concatenate(
                        [jnp.where(high_row == p, twice[s], zero) for p in high_pattern[: CHUNKS[t] // 2]],
                        axis=0,
                    )
                )
            part = dot(jnp.concatenate(left, axis=1), jnp.concatenate(right, axis=1), NT)
            out[SUB * FIRST[t] : SUB * (FIRST[t] + CHUNKS[t]), :] += part

    each_block((bd, bp, bl), (sd, sp, sl), step)


def norm_parts(values):
    center = values - jnp.mean(values, axis=-1, keepdims=True)
    spread = lax.rsqrt(jnp.mean(center * center, axis=-1, keepdims=True) + NORM_EPSILON)
    return center * spread, spread


def norm_back(scaled, xhat, spread):
    return spread * (
        scaled
        - jnp.mean(scaled, axis=-1, keepdims=True)
        - xhat * jnp.mean(scaled * xhat, axis=-1, keepdims=True)
    )


def head_lanes(head, width):
    lane = lax.broadcasted_iota(jnp.int32, (1, width), 1)
    return (lane >= head * HEAD_DIM) & (lane < (head + 1) * HEAD_DIM)


def forward_body(
    rows, gains, biases, weights, bias, big_counts, small_counts, normed, q, k, v, mixed, big_probs, small_probs
):
    width = big_probs.shape[1]
    narrow = (rows.shape[0] - width) // small_counts.shape[1]
    wide = 2 * narrow
    pairs = small_counts.shape[1] // 2
    columns = q.shape[1]
    heads = columns // HEAD_DIM
    halves = width // LANES
    xhat, _ = norm_parts(rows[...].astype(F32))
    normed[...] = (xhat * gains[0:1, :] + gains[1:2, :]).astype(BF)
    q[...] = (dot(normed[...], weights[0], NN) + biases[0:1, :]).astype(BF)
    k[...] = dot(normed[...], weights[1], NN).astype(BF)
    v[...] = (dot(normed[...], weights[2], NN) + biases[1:2, :]).astype(BF)
    mixed[...] = jnp.zeros_like(mixed)
    key = lax.broadcasted_iota(jnp.int32, (1, width), 1)
    big_live = key < big_counts[0]
    small_live = []
    for pair in range(pairs):
        row = lax.broadcasted_iota(jnp.int32, (wide, wide), 0)
        lane = lax.broadcasted_iota(jnp.int32, (wide, wide), 1)
        first = (row < narrow) & (lane < small_counts[0, 2 * pair])
        second = (row >= narrow) & (lane >= narrow) & (lane < narrow + small_counts[0, 2 * pair + 1])
        small_live.append(first | second)

    def attend(span, scores, live, mine):
        scores = jnp.where(live, scores, NEGATIVE_FILL)
        power = jnp.exp(scores - jnp.max(scores, axis=-1, keepdims=True))
        probs = power * (1.0 / jnp.sum(power, axis=-1, keepdims=True))
        out = dot(probs.astype(BF), v[span, :], NN)
        mixed[span, :] = jnp.where(mine, out.astype(BF), mixed[span, :])
        return probs

    def one_head(head, carry):
        mine = head_lanes(head, columns)
        span = slice(0, width)
        query = jnp.where(mine, q[span, :], 0.0)
        extra = jnp.concatenate(
            [bias[pl.ds(half * width * SUB + head, width, stride=SUB), :] for half in range(halves)], axis=1
        )
        scores = dot(query, k[span, :], NT) * SCALE + extra
        big_probs[head] = attend(span, scores, big_live, mine)
        for pair in range(pairs):
            span = slice(width + pair * wide, width + (pair + 1) * wide)
            query = jnp.where(mine, q[span, :], 0.0)
            at = (halves * width + pair * narrow) * SUB
            extra = bias[pl.ds(at + head, narrow, stride=SUB), :]
            scores = dot(query, k[span, :], NT) * SCALE + jnp.concatenate([extra, extra], axis=0)
            small_probs[head, pair] = attend(span, scores, small_live[pair], mine)
        return carry

    lax.fori_loop(0, heads, one_head, 0)


def backward_body(grad_heads, q, k, v, big_probs, small_probs, dq, dk, dv, score_rows):
    heads, width = big_probs.shape[:2]
    pairs, wide = small_probs.shape[1:3]
    narrow = wide // 2
    columns = q.shape[1]
    halves = width // LANES
    for ref in (dq, dk, dv):
        ref[...] = jnp.zeros_like(ref)

    def attend(span, probs, mine):
        upper = jnp.where(mine, grad_heads[span, :], 0.0)
        grad_probs = dot(upper, v[span, :], NT)
        inner = jnp.sum(probs * grad_probs, axis=-1, keepdims=True)
        grad_scores = (probs * (grad_probs - inner)).astype(BF)
        dv[span, :] = jnp.where(mine, dot(probs.astype(BF), upper, TN).astype(BF), dv[span, :])
        dq[span, :] = jnp.where(mine, (dot(grad_scores, k[span, :], NN) * SCALE).astype(BF), dq[span, :])
        dk[span, :] = jnp.where(mine, (dot(grad_scores, q[span, :], TN) * SCALE).astype(BF), dk[span, :])
        return grad_scores.astype(F32)

    def one_head(head, carry):
        mine = head_lanes(head, columns)
        span = slice(0, width)
        grad_scores = attend(span, big_probs[head], mine)
        for half in range(halves):
            score_rows[pl.ds(half * width * SUB + head, width, stride=SUB), :] = grad_scores[
                :, LANES * half : LANES * (half + 1)
            ]
        for pair in range(pairs):
            span = slice(width + pair * wide, width + (pair + 1) * wide)
            grad_scores = attend(span, small_probs[head, pair], mine)
            at = (halves * width + pair * narrow) * SUB
            score_rows[pl.ds(at + head, narrow, stride=SUB), :] = grad_scores[:narrow] + grad_scores[narrow:]
        return carry

    lax.fori_loop(0, heads, one_head, 0)


def middle_body(
    heads_in, rows, upper, gains, weights, layer_out, grad_hidden, grad_low, normed_low, grad_heads, act, grad_pre, sums, pre_sums
):
    parts, _, columns = heads_in.shape
    hidden = rows[...].astype(F32) + gains[2:3, :]
    for j in range(parts):
        hidden = hidden + dot(heads_in[j], weights[0, j], NT)
    xhat, spread = norm_parts(hidden)
    low = (xhat * gains[0:1, :] + gains[1:2, :]).astype(BF)
    normed_low[...] = low
    cotangent = upper[...]
    final = hidden + gains[4:5, :]
    grad_normed = jnp.zeros_like(hidden)
    for j in range(parts):
        pre = dot(low, weights[1, j], NN) + gains[3:4, j * columns : (j + 1) * columns]
        phi = 0.5 * (1.0 + lax.erf(pre * (0.5**0.5)))
        active = (pre * phi).astype(BF)
        act[j] = active
        final = final + dot(active, weights[2, j], NT)
        slope = phi + pre * jnp.exp(-0.5 * pre * pre) * (0.5 / jnp.pi) ** 0.5
        grad_j = dot(cotangent, weights[2, j], NN) * slope
        low_j = grad_j.astype(BF)
        grad_pre[j] = low_j
        pre_sums[j : j + 1, :] = jnp.sum(low_j.astype(F32), axis=0, keepdims=True)
        grad_normed = grad_normed + dot(low_j, weights[1, j], NT)
    layer_out[...] = final.astype(BF)
    wide = cotangent.astype(F32)
    grad = wide + norm_back(grad_normed * gains[0:1, :], xhat, spread)
    grad_hidden[...] = grad
    grad_small = grad.astype(BF)
    grad_low[...] = grad_small
    for j in range(parts):
        grad_heads[j] = dot(grad_small, weights[0, j], NN).astype(BF)
    sums[0:1, :] = jnp.sum(grad_normed * xhat, axis=0, keepdims=True)
    sums[1:2, :] = jnp.sum(grad_normed, axis=0, keepdims=True)
    sums[2:3, :] = jnp.sum(grad, axis=0, keepdims=True)
    sums[3:4, :] = jnp.sum(wide, axis=0, keepdims=True)


def adamw_update(weight, first_moment, second_moment, gradient, learn_rate):
    first_new = BETA_FIRST * first_moment + (1.0 - BETA_FIRST) * gradient
    second_new = BETA_SECOND * second_moment + (1.0 - BETA_SECOND) * gradient * gradient
    first_hat = first_new / (1.0 - BETA_FIRST**ADAM_STEP)
    second_hat = second_new / (1.0 - BETA_SECOND**ADAM_STEP)
    weight_new = weight - learn_rate * (
        first_hat / (jnp.sqrt(second_hat) + ADAM_EPSILON) + WEIGHT_DECAY * weight
    )
    return (weight_new, first_new, second_new)


def exchange(value, axis):
    return lax.all_to_all(value, axis, split_axis=0, concat_axis=0, tiled=True)


def spread_all(value, axis):
    size = lax.axis_size(axis)
    return exchange(jnp.broadcast_to(value[None], (size, *value.shape)), axis)


def struct(shape, dtype):
    return jax.ShapeDtypeStruct(shape, dtype)


def on_device(
    node_rows,
    output_grad,
    weight_in,
    first_in,
    second_in,
    weight_out,
    first_out,
    second_out,
    weight_down,
    first_down,
    second_down,
    vectors,
    first_vectors,
    second_vectors,
    bias_table,
    first_table,
    second_table,
    big_counts,
    small_counts,
    big_distance,
    small_distance,
    big_paths,
    small_paths,
    big_lengths,
    small_lengths,
):
    everyone = ("dp", "head")
    n_dp, n_head = lax.axis_size("dp"), lax.axis_size("head")
    head_index = lax.axis_index("head")
    shard_rows, columns = weight_in.shape[1], weight_in.shape[2]
    model = shard_rows * n_dp
    my_rows = node_rows.shape[0]
    group_rows = my_rows * n_head
    heads = columns // HEAD_DIM
    width, narrow = big_distance.shape[1], small_distance.shape[1]
    pairs = small_distance.shape[0] // 2
    pair_rows = width // LANES * width + pairs * narrow
    pair_count = pair_rows * LANES
    table_rows = bias_table.shape[0]
    ints = (big_distance, big_paths, big_lengths, small_distance, small_paths, small_lengths)

    def chunked(table):
        return table.T.reshape(heads, table_rows // LANES, LANES).transpose(1, 0, 2)

    def unchunked(value):
        return value.transpose(1, 0, 2).reshape(heads, table_rows).T

    with jax.named_scope("table_all"):
        table_all = spread_all(chunked(bias_table.astype(BF)), "dp")
    table_all = table_all.reshape(-1, LANES).astype(F32)
    with jax.named_scope("vectors_all"):
        all_vectors = spread_all(vectors, everyone).transpose(1, 0, 2).reshape(vectors.shape[0], -1)
    with jax.named_scope("rows_all"):
        rows_all = spread_all(node_rows, "head").reshape(group_rows, model)
    with jax.named_scope("weights_qkv"):
        weights_qkv = lax.all_gather(weight_in[:3].astype(BF), "dp", axis=1, tiled=True)
    local_rest = jnp.stack([weight_out.astype(BF).T, weight_in[3].astype(BF), weight_down.astype(BF).T])
    with jax.named_scope("weights_rest"):
        weights_rest = lax.all_gather(local_rest, everyone)
    weights_rest = (
        weights_rest.reshape(n_dp, n_head, 3, shard_rows, columns)
        .transpose(2, 1, 0, 3, 4)
        .reshape(3, n_head, model, columns)
    )
    with jax.named_scope("upper_all"):
        upper_all = spread_all(output_grad, "head").reshape(group_rows, model)

    bias = kernel_call(
        bias_body,
        struct((pair_rows * SUB, LANES), F32),
        "pair_bias",
        pair_count * 8 * 60 * 100,
        pair_count * 8 * 8,
        7,
    )(table_all, *ints)

    my_bias = lax.dynamic_slice_in_dim(all_vectors, head_index * columns, columns, 1)
    vmem, smem = pl.BlockSpec(memory_space=pltpu.VMEM), pl.BlockSpec(memory_space=pltpu.SMEM)
    low_half = struct((group_rows, columns), BF)
    normed_one, q, k, v, mixed, big_probs, small_probs = kernel_call(
        forward_body,
        (
            struct((group_rows, model), BF),
            low_half,
            low_half,
            low_half,
            low_half,
            struct((heads, width, width), F32),
            struct((heads, pairs, 2 * narrow, 2 * narrow), F32),
        ),
        "attend_forward",
        6 * group_rows * model * columns,
        10 << 20,
        in_specs=[vmem] * 5 + [smem] * 2,
    )(
        rows_all,
        all_vectors[:2],
        my_bias[4:6],
        weights_qkv,
        bias,
        big_counts,
        small_counts,
    )
    with jax.named_scope("mixed_rows"):
        mixed_rows = exchange(mixed.reshape(n_head, my_rows, columns), "head")

    mine = struct((my_rows, model), BF)
    split = struct((n_head, my_rows, columns), BF)
    gains = jnp.concatenate([all_vectors[2:4], all_vectors[6:9]], axis=0)
    layer_out, grad_hidden, grad_low, normed_two, grad_heads, act, grad_pre, sums, pre_sums = kernel_call(
        middle_body,
        (
            mine,
            struct((my_rows, model), F32),
            mine,
            mine,
            split,
            split,
            split,
            struct((4, model), F32),
            struct((n_head, columns), F32),
        ),
        "feed_forward",
        14 * my_rows * model * model,
        8 << 20,
        5,
    )(mixed_rows, node_rows, output_grad, gains, weights_rest)

    with jax.named_scope("grad_heads"):
        grad_heads = exchange(grad_heads, "head").reshape(group_rows, columns)
    with jax.named_scope("act_pre"):
        act_pre = exchange(jnp.stack([act, grad_pre], axis=1), "head")
    act_all = act_pre[:, 0].reshape(group_rows, columns)
    pre_all = act_pre[:, 1].reshape(group_rows, columns)
    with jax.named_scope("rows_two"):
        rows_two = spread_all(jnp.stack([normed_two, grad_low]), "head")
    normed_all = rows_two[:, 0].reshape(group_rows, model)
    low_all = rows_two[:, 1].reshape(group_rows, model)

    dq, dk, dv, score_rows = kernel_call(
        backward_body,
        (low_half, low_half, low_half, struct((pair_rows * SUB, LANES), F32)),
        "attend_backward",
        heads * pair_count * columns * 8,
        10 << 20,
        6,
    )(grad_heads, q, k, v, big_probs, small_probs)

    def outer(left, right):
        return dot(left, right, TN).astype(BF).reshape(n_dp, shard_rows, columns)

    with jax.named_scope("rest_grads"):
        rest_shards = exchange(
            jnp.stack([outer(low_all, mixed), outer(normed_all, pre_all), outer(upper_all, act_all)], axis=1), "dp"
        )
    with jax.named_scope("qkv_grads"):
        qkv_shards = exchange(
            jnp.stack([outer(normed_one, dq), outer(normed_one, dk), outer(normed_one, dv)], axis=1), "dp"
        )
    partial = (dot(dq, weights_qkv[0], NT) + dot(dk, weights_qkv[1], NT) + dot(dv, weights_qkv[2], NT)).astype(BF)
    with jax.named_scope("grad_normed_one"):
        grad_normed_one = exchange(partial.reshape(n_head, my_rows, model), "head")
    grad_normed_one = jnp.sum(grad_normed_one.astype(F32), axis=0)
    xhat, spread = norm_parts(node_rows.astype(F32))
    input_grad = (grad_hidden + norm_back(grad_normed_one * all_vectors[0], xhat, spread)).astype(BF)

    table_grad = kernel_call(
        scatter_body,
        struct((n_dp * table_rows // LANES * heads, LANES), F32),
        "table_scatter",
        pair_count * 8 * 60 * 100,
        pair_count * 8 * 8,
        7,
    )(score_rows, *ints)
    with jax.named_scope("table_grad"):
        table_shards = exchange(
            table_grad.astype(BF).reshape(n_dp, table_rows // LANES, heads, LANES), "dp"
        )

    def my_columns(values):
        return lax.dynamic_update_slice_in_dim(
            jnp.zeros((1, model), F32), values[None], head_index * columns, 1
        )

    vector_terms = jnp.concatenate(
        [
            jnp.sum(grad_normed_one * xhat, axis=0)[None],
            jnp.sum(grad_normed_one, axis=0)[None],
            sums[0:2],
            my_columns(jnp.sum(dq.astype(F32), axis=0)),
            my_columns(jnp.sum(dv.astype(F32), axis=0)),
            sums[2:3],
            pre_sums.reshape(1, model),
            sums[3:4],
        ]
    )
    with jax.named_scope("vector_grads"):
        vector_shards = exchange(
            vector_terms.reshape(vectors.shape[0], n_dp * n_head, -1).transpose(1, 0, 2), everyone
        )
    shard_vectors = jnp.sum(vector_shards, axis=0)
    shard_rest = jnp.sum(rest_shards.astype(F32), axis=0)
    shard_qkv = jnp.sum(qkv_shards.astype(F32), axis=0)
    shard_table = jnp.sum(table_shards.astype(F32), axis=0)
    square_part = (
        jnp.sum(shard_rest * shard_rest)
        + jnp.sum(shard_qkv * shard_qkv)
        + jnp.sum(shard_vectors * shard_vectors)
        + jnp.sum(shard_table * shard_table)
    )
    with jax.named_scope("squares"):
        squares = spread_all(jnp.broadcast_to(square_part, (LANES,)), everyone)
    grad_norm = jnp.sqrt(jnp.sum(squares[:, 0]))
    clip_factor = CLIP_NORM / jnp.maximum(grad_norm, CLIP_NORM)
    shard_in = jnp.concatenate([shard_qkv, shard_rest[1:2]], axis=0)
    new_in = adamw_update(weight_in, first_in, second_in, shard_in * clip_factor, RATE_MATRIX)
    new_out = adamw_update(weight_out, first_out, second_out, shard_rest[0].T * clip_factor, RATE_OUTPUT)
    new_down = adamw_update(weight_down, first_down, second_down, shard_rest[2].T * clip_factor, RATE_MATRIX)
    new_vectors = adamw_update(
        vectors, first_vectors, second_vectors, shard_vectors * clip_factor, RATE_VECTOR
    )
    new_table = adamw_update(
        bias_table, first_table, second_table, unchunked(shard_table) * clip_factor, RATE_VECTOR
    )
    return (layer_out, input_grad, grad_norm, *new_in, *new_out, *new_down, *new_vectors, *new_table)


def solution(mesh):
    rows = P(("dp", "head"), None)
    square = P(None, "dp", "head")
    across = P("head", "dp")
    thin = P(None, ("dp", "head"))
    table = P("dp", "head")
    return jax.shard_map(
        on_device,
        mesh=mesh,
        in_specs=(rows, rows)
        + (square,) * 3
        + (across,) * 6
        + (thin,) * 3
        + (table,) * 3
        + (P("dp"), P("dp", None))
        + (P("dp", None, None),) * 2
        + (P(None, "dp", None, None),) * 2
        + (P("dp", None, None),) * 2,
        out_specs=(rows, rows, P()) + (square,) * 3 + (across,) * 6 + (thin,) * 3 + (table,) * 3,
        check_vma=False,
    )
```

```python
import jax
import jax.numpy as jnp
from jax import lax
from jax.experimental import pallas as pl
from jax.experimental.pallas import tpu as pltpu
from jax.sharding import PartitionSpec as P

HEAD_DIM = 24
NDIST = 512
NTYPE = 1536
STEPS = 5
ADAM_STEP = 10

NORM_EPSILON = 1e-05
NEGATIVE_FILL = -1e30
BETA_FIRST = 0.9
BETA_SECOND = 0.95
ADAM_EPSILON = 1e-08
RATE_MATRIX = 0.02
RATE_OUTPUT = 0.05
RATE_VECTOR = 0.15
WEIGHT_DECAY = 0.01
CLIP_NORM = 1.0

LANES = 128
SUB = 8
FIRST = [0] + [(NDIST + n * NTYPE) // LANES for n in range(STEPS)]
CHUNKS = [NDIST // LANES] + [NTYPE // LANES] * STEPS
LOOKUPS = STEPS + 1
VECTOR_ROWS = 16
BIG_QUARTERS = (1, 3)
BIG_PARTS = len(BIG_QUARTERS)
FIXED = 8192.0
NOWHERE = 4095
SCALE = HEAD_DIM**-0.5
BF = jnp.bfloat16
F32 = jnp.float32
VMEM_BYTES = 56 << 20

NN = (((1,), (0,)), ((), ()))
NT = (((1,), (1,)), ((), ()))
TN = (((0,), (0,)), ((), ()))


def dot(left, right, dims):
    return lax.dot_general(left, right, dims, preferred_element_type=F32)


def inner_of(size):
    return 1 << ((size.bit_length() - 1) // 2)


def xor_order(size):
    inner = inner_of(size)
    return [a * inner + b for b in range(inner) for a in range(size // inner)]


def kernel_call(body, outs, name, micros, args, scratch=(), smem_in=(), placed=(), us_at=None, ready=(), limit=VMEM_BYTES):
    n_in, n_out = len(args), len(outs)
    moved = [i for i in range(n_in) if i not in smem_in and i not in ready]
    blocks = [out[0] if isinstance(out, tuple) else 0 for out in outs]
    shapes = [out[1] if isinstance(out, tuple) else out for out in outs]
    flat = [(i, k) for i in range(n_out) for k in range(max(blocks[i], 1))]
    n_sems = sum(args[i].shape[0] if i in placed else 1 for i in moved)

    def wrapped(*refs):
        given, results = refs[:n_in], refs[n_in : n_in + len(flat)]
        refs = refs[n_in + len(flat) :]
        held = dict(zip(moved, refs))
        made, refs = refs[len(moved) : len(moved) + n_out], refs[len(moved) + n_out :]
        rest, (in_sems, out_sems) = refs[:-2], refs[-2:]
        arriving, sem = {}, 0
        for i in moved:
            pieces = [(given[i], held[i])]
            if i in placed:
                size = args[i].shape[0]
                pieces = [
                    (given[i].at[k], held[i].at[given[us_at][1] ^ other]) for k, other in enumerate(xor_order(size))
                ]
            arriving[i] = [pltpu.make_async_copy(a, b, in_sems.at[sem + n]) for n, (a, b) in enumerate(pieces)]
            sem += len(pieces)
        leaving = [
            pltpu.make_async_copy(made[i].at[k] if blocks[i] else made[i], results[at], out_sems.at[at])
            for at, (i, k) in enumerate(flat)
        ]
        for i in moved:
            for copy in arriving[i]:
                copy.start()
        waiting, unsent = list(moved), list(range(n_out))

        def need(*which):
            for i in which:
                if i in waiting:
                    waiting.remove(i)
                    for copy in arriving[i]:
                        copy.wait()

        def done(*which):
            for i in which:
                if i in unsent:
                    unsent.remove(i)
                    for at, (j, _) in enumerate(flat):
                        if i == j:
                            leaving[at].start()

        body(need, done, *[held.get(i, given[i]) for i in range(n_in)], *made, *rest)
        need(*moved)
        done(*range(n_out))
        for copy in leaving:
            copy.wait()

    anywhere, smem = pl.BlockSpec(memory_space=pl.ANY), pl.BlockSpec(memory_space=pltpu.SMEM)
    vmem = pl.BlockSpec(memory_space=pltpu.VMEM)
    return pl.pallas_call(
        wrapped,
        out_shape=tuple(shapes[i] for i, _ in flat),
        in_specs=[smem if i in smem_in else vmem if i in ready else anywhere for i in range(n_in)],
        out_specs=tuple([anywhere] * len(flat)),
        scratch_shapes=[pltpu.VMEM(args[i].shape, args[i].dtype) for i in moved]
        + [pltpu.VMEM((n, *o.shape) if n else o.shape, o.dtype) for n, o in zip(blocks, shapes)]
        + list(scratch)
        + [pltpu.SemaphoreType.DMA((n_sems,)), pltpu.SemaphoreType.DMA((len(flat),))],
        name=name,
        compiler_params=pltpu.CompilerParams(vmem_limit_bytes=limit),
        cost_estimate=pl.CostEstimate(flops=int(micros * 1e9), bytes_accessed=1 << 20, transcendentals=0),
    )(*args)


def big_block(refs, block, half):
    distance, paths, lengths = refs
    rows, lanes = pl.ds(SUB * block, SUB), slice(LANES * half, LANES * half + LANES)
    return [distance[0, rows, lanes]] + [paths[n, 0, rows, lanes] for n in range(STEPS)], lengths[0, rows, lanes]


def small_block(refs, block, pair):
    distance, paths, lengths = refs
    rows = pl.ds(SUB * block, SUB)

    def two(ref, *lead):
        return jnp.concatenate([ref[(*lead, 2 * pair, rows)], ref[(*lead, 2 * pair + 1, rows)]], axis=1)

    return [two(distance)] + [two(paths, n) for n in range(STEPS)], two(lengths)


def each_block(load, refs, first, count, sides, group, step):
    def some(at, carry):
        blocks = [first + at * group + u for u in range(group)]
        step([(*load(refs, block, side), block, side) for block in blocks for side in range(sides)])
        return carry

    lax.fori_loop(0, count // group, some, 0)


def bias_body(part, need, done, table, *refs):
    small, refs = (refs[:3], refs[3:]) if part == 0 else (None, refs)
    big, outs, words = refs[:3], refs[3:-1], refs[-1]
    need(0)
    heads, count = words.shape[:2]
    for k in range(count):
        low = jnp.round(table[SUB * 2 * k : SUB * (2 * k + 1), :].astype(F32) * FIXED).astype(jnp.int32)
        high = jnp.round(table[SUB * (2 * k + 1) : SUB * (2 * k + 2), :].astype(F32) * FIXED).astype(jnp.int32)
        word = (high << 16) | (low & 0xFFFF)
        for h in range(heads):
            words[h, k] = jnp.broadcast_to(word[h : h + 1], (SUB, LANES))

    def step(store):
        def run(parts):
            for index, lengths, block, side in parts:
                share = (1.0 / FIXED) / lengths.astype(F32)
                first, edges = [None] * heads, [None] * heads
                for t in range(LOOKUPS):
                    code = index[t]
                    lane = code & (LANES - 1)
                    odd = [(code & bit) != 0 for bit in (256, 512, 1024)]
                    shift = ((code >> 3) & 16) ^ 16
                    live = lengths > t - 1
                    for h in range(heads):
                        found = [
                            jnp.take_along_axis(words[h, FIRST[t] // 2 + k], lane, axis=1, mode="promise_in_bounds")
                            for k in range(CHUNKS[t] // 2)
                        ]
                        level = 0
                        while len(found) > 1:
                            found = [
                                jnp.where(odd[level], found[k + 1], found[k]) if k + 1 < len(found) else found[k]
                                for k in range(0, len(found), 2)
                            ]
                            level += 1
                        value = (found[0] << shift) >> 16
                        if t == 0:
                            first[h] = value
                        else:
                            value = jnp.where(live, value, 0)
                            edges[h] = value if edges[h] is None else edges[h] + value
                for h in range(heads):
                    value = first[h].astype(F32) * (1.0 / FIXED) + edges[h].astype(F32) * share
                    store(h, side, block, value)

        return run

    if small:

        def store_small(h, side, block, value):
            outs[0][h, side, pl.ds(SUB * block, SUB), :] = value

        need(1, 2, 3)
        each_block(small_block, small, 0, small[0].shape[1] // SUB, small[0].shape[0] // 2, 1, step(store_small))
        done(0)
    need(*range(1, 7 if small else 4))
    out = outs[-1]
    count = out.shape[2] // SUB
    first_block = big[0].shape[1] // SUB // sum(BIG_QUARTERS) * sum(BIG_QUARTERS[:part])

    def store_big(h, side, block, value):
        out[h, side, pl.ds(SUB * (block - first_block), SUB), :] = value

    each_block(big_block, big, first_block, count, big[0].shape[2] // LANES, 1, step(store_big))


def scatter_body(need, done, small_grads, sd, sp, sl, big_grads, bd, bp, bl, out, total):
    total[...] = jnp.zeros_like(total)
    sub = lax.broadcasted_iota(jnp.int32, (2 * SUB, LANES), 0)
    low_pattern = [(sub + 2 * SUB * k).astype(F32).astype(BF) for k in range(LANES // (2 * SUB))]
    upper = (sub >= SUB).astype(jnp.int32)
    high_pattern = [(2 * k + upper).astype(F32).astype(BF) for k in range(max(CHUNKS) // 2)]
    zero, one = jnp.zeros((2 * SUB, LANES), BF), jnp.ones((2 * SUB, LANES), BF)

    def twice(value):
        return jnp.concatenate([value, value], axis=0).astype(BF)

    def step(grads, side_rows):
        def run(parts):
            whole, shared = [], []
            for index, lengths, block, side in parts:
                inverse = 1.0 / lengths.astype(F32)
                for s in range(SUB):
                    g = grads[pl.ds((side * side_rows + SUB * block + s) * SUB, SUB), :]
                    whole.append(twice(g))
                    shared.append(twice(g * jnp.broadcast_to(inverse[s : s + 1], (SUB, LANES))))
            for t in range(LOOKUPS):
                left, right = [], []
                for part, (index, lengths, _, _) in enumerate(parts):
                    code = index[t] if t == 0 else jnp.where(lengths > t - 1, index[t], NOWHERE)
                    for s in range(SUB):
                        spread = jnp.broadcast_to(code[s : s + 1], (SUB, LANES))
                        low = twice((spread & (LANES - 1)).astype(F32))
                        high = twice((spread >> 7).astype(F32))
                        source = (whole if t == 0 else shared)[SUB * part + s]
                        left.append(jnp.concatenate([jnp.where(low == p, one, zero) for p in low_pattern], axis=0))
                        right.append(
                            jnp.concatenate(
                                [jnp.where(high == p, source, zero) for p in high_pattern[: CHUNKS[t] // 2]], axis=0
                            )
                        )
                span = slice(SUB * FIRST[t], SUB * (FIRST[t] + CHUNKS[t]))
                total[:, span] += dot(jnp.concatenate(left, axis=1), jnp.concatenate(right, axis=1), NT)

        return run

    need(0, 1, 2, 3)
    narrow, width = sd.shape[1], bd.shape[1]
    each_block(small_block, (sd, sp, sl), 0, narrow // SUB, sd.shape[0] // 2, 2, step(small_grads, narrow))
    need(4, 5, 6, 7)
    each_block(big_block, (bd, bp, bl), 0, width // SUB, width // LANES, 2, step(big_grads, width))
    out[...] = total[...].T.astype(BF)


def whole_matrix(ref, k):
    if len(ref.shape) == 3:
        return ref[k]
    value = ref[:, k]
    return value.reshape(value.shape[0] * value.shape[1], value.shape[2])


def norm_parts(values):
    center = values - jnp.mean(values, axis=-1, keepdims=True)
    spread = lax.rsqrt(jnp.mean(center * center, axis=-1, keepdims=True) + NORM_EPSILON)
    return center * spread, spread


def norm_back(scaled, xhat, spread):
    return spread * (
        scaled
        - jnp.mean(scaled, axis=-1, keepdims=True)
        - xhat * jnp.mean(scaled * xhat, axis=-1, keepdims=True)
    )


def head_lanes(head, width):
    lane = lax.broadcasted_iota(jnp.int32, (1, width), 1)
    return (lane >= head * HEAD_DIM) & (lane < (head + 1) * HEAD_DIM)


def peer_block(me, r, rows):
    return pl.ds(pl.multiple_of((me[0] ^ r) * rows, rows), rows)


def forward_body(n_head, need, done, *refs):
    rows_in, refs = refs[:n_head], refs[n_head:]
    me, big_counts, small_counts, pieces, weights, small_bias = refs[:6]
    big_bias, refs = refs[6 : 6 + BIG_PARTS], refs[6 + BIG_PARTS :]
    normed, qkv, big_probs, small_probs, vectors, hidden_bias = refs[:6]
    mixed_out, mixed = refs[6 : 6 + n_head], refs[6 + n_head]
    block = rows_in[0].shape[1]
    need(*range(n_head), n_head + 3)
    n_vectors, size = vectors.shape[0], vectors.shape[1] // pieces.shape[0]
    for piece in range(pieces.shape[0]):
        vectors[:, piece * size : (piece + 1) * size] = pieces[piece, :n_vectors, :size]
    heads, width = big_probs.shape[:2]
    pairs, wide = small_probs.shape[1:3]
    narrow = wide // 2
    columns = qkv.shape[2]
    halves = width // LANES
    biases = [None] * 2
    for j in range(n_head):
        span = slice(j * columns, (j + 1) * columns)
        hidden_bias[j : j + 1, :] = vectors[7:8, span]
        for i in range(2):
            value = jnp.where(me[0] == j, vectors[4 + i : 5 + i, span], 0.0)
            biases[i] = value if j == 0 else biases[i] + value
    for r in range(n_head):
        xhat, _ = norm_parts(rows_in[r][0].astype(F32))
        normed[peer_block(me, r, block), :] = (xhat * vectors[0:1, :] + vectors[1:2, :]).astype(BF)
    done(0, 4, 5)
    need(n_head + 4)
    for k in range(3):
        value = dot(normed[...], whole_matrix(weights, k), NN)
        if k != 1:
            value = value + biases[k // 2]
        qkv[k] = value.astype(BF)
    done(1)
    need(*range(n_head + 5, n_head + 6 + BIG_PARTS))
    mixed[...] = jnp.zeros_like(mixed)
    big_live = lax.broadcasted_iota(jnp.int32, (1, width), 1) < big_counts[0]
    small_live = []
    row = lax.broadcasted_iota(jnp.int32, (wide, wide), 0)
    lane = lax.broadcasted_iota(jnp.int32, (wide, wide), 1)
    for pair in range(pairs):
        first = (row < narrow) & (lane < small_counts[0, 2 * pair])
        second = (row >= narrow) & (lane >= narrow) & (lane < narrow + small_counts[0, 2 * pair + 1])
        small_live.append(first | second)

    def attend(span, extra, live, mine):
        query = jnp.where(mine, qkv[0, span, :], 0.0)
        scores = jnp.where(live, dot(query, qkv[1, span, :], NT) * SCALE + extra, NEGATIVE_FILL)
        power = jnp.exp(scores - jnp.max(scores, axis=-1, keepdims=True))
        probs = power * (1.0 / jnp.sum(power, axis=-1, keepdims=True))
        out = dot(probs.astype(BF), qkv[2, span, :], NN)
        mixed[span, :] = jnp.where(mine, out.astype(BF), mixed[span, :])
        return probs

    def big_heads(at, carry):
        for head in (2 * at, 2 * at + 1):
            extra = jnp.concatenate(
                [jnp.concatenate([part[head, half] for part in big_bias], axis=0) for half in range(halves)], axis=1
            )
            big_probs[head] = attend(slice(0, width), extra, big_live, head_lanes(head, columns))
        return carry

    lax.fori_loop(0, heads // 2, big_heads, 0)
    done(2)

    def small_heads(at, carry):
        for head in (2 * at, 2 * at + 1):
            for pair in range(pairs):
                extra = small_bias[head, pair]
                extra = jnp.concatenate([extra, extra], axis=0)
                span = slice(width + pair * wide, width + (pair + 1) * wide)
                small_probs[head, pair] = attend(span, extra, small_live[pair], head_lanes(head, columns))
        return carry

    lax.fori_loop(0, heads // 2, small_heads, 0)
    done(3)
    for r in range(n_head):
        mixed_out[r][...] = mixed[peer_block(me, r, block), :]


def put_matrix(ref, k, value):
    if len(ref.shape) == 3:
        ref[k] = value
        return
    rows = ref.shape[2]
    for d in range(ref.shape[0]):
        ref[d, k] = value[d * rows : (d + 1) * rows]


def backward_body(n_head, need, done, *refs):
    need(*range(n_head), n_head + 1, n_head + 2)
    grads_in, refs = refs[:n_head], refs[n_head:]
    me, qkv, small_probs, big_probs, weights, small_rows, big_rows, dqkv, column_sums = refs[:9]
    rows_out, (grad_heads,) = refs[9 : 9 + n_head], refs[9 + n_head :]
    heads, width = big_probs.shape[:2]
    pairs, wide = small_probs.shape[1:3]
    narrow = wide // 2
    columns = qkv.shape[2]
    halves = width // LANES
    block = grads_in[0].shape[0]
    for r in range(n_head):
        grad_heads[peer_block(me, r, block), :] = grads_in[r][...]
    dqkv[...] = jnp.zeros_like(dqkv)

    def attend(span, probs, mine):
        upper = jnp.where(mine, grad_heads[span, :], 0.0)
        grad_probs = dot(upper, qkv[2, span, :], NT)
        inner = jnp.sum(probs * grad_probs, axis=-1, keepdims=True)
        wide_scores = probs * (grad_probs - inner)
        grad_scores = wide_scores.astype(BF)
        dq = (dot(grad_scores, qkv[1, span, :], NN) * SCALE).astype(BF)
        dk = (dot(grad_scores, qkv[0, span, :], TN) * SCALE).astype(BF)
        dv = dot(probs.astype(BF), upper, TN).astype(BF)
        for k, value in enumerate((dq, dk, dv)):
            dqkv[k, span, :] = jnp.where(mine, value, dqkv[k, span, :])
        return grad_scores.astype(F32)

    def small_heads(at, carry):
        for head in (2 * at, 2 * at + 1):
            for pair in range(pairs):
                span = slice(width + pair * wide, width + (pair + 1) * wide)
                grad_scores = attend(span, small_probs[head, pair], head_lanes(head, columns))
                small_rows[pl.ds(pair * narrow * SUB + head, narrow, stride=SUB), :] = (
                    grad_scores[:narrow] + grad_scores[narrow:]
                )
        return carry

    lax.fori_loop(0, heads // 2, small_heads, 0)
    done(0)
    need(n_head + 3)

    def big_heads(at, carry):
        for head in (2 * at, 2 * at + 1):
            grad_scores = attend(slice(0, width), big_probs[head], head_lanes(head, columns))
            for half in range(halves):
                big_rows[pl.ds(half * width * SUB + head, width, stride=SUB), :] = grad_scores[
                    :, LANES * half : LANES * (half + 1)
                ]
        return carry

    lax.fori_loop(0, heads // 2, big_heads, 0)
    done(1, 2)
    need(n_head + 4)
    column_sums[...] = jnp.zeros_like(column_sums)
    for i, k in enumerate((0, 2)):
        column_sums[i, pl.ds(me[0], 1), :] = jnp.sum(dqkv[k].astype(F32), axis=0, keepdims=True)
    for r in range(n_head):
        rows = peer_block(me, r, block)
        total = dot(dqkv[0, rows, :], whole_matrix(weights, 0), NT)
        total = total + dot(dqkv[1, rows, :], whole_matrix(weights, 1), NT)
        total = total + dot(dqkv[2, rows, :], whole_matrix(weights, 2), NT)
        rows_out[r][...] = total.astype(BF)


def middle_body(n_head, need, done, *refs):
    mixed, refs = refs[:n_head], refs[n_head:]
    me, rows, upper, vectors, hidden_bias = refs[:5]
    weights, refs = refs[5 : 5 + n_head], refs[5 + n_head :]
    layer_out, grad_hidden, sums, pre_sums, normed_grad, act_pre = refs[:6]
    grad_heads = refs[6:]
    need(*range(2 * n_head + 5))
    columns = mixed[0].shape[1]
    slot = parcel_slot(columns)
    hidden = rows[...].astype(F32) + vectors[6:7, :]
    for r in range(n_head):
        hidden = hidden + dot(mixed[r][...], whole_matrix(weights[r], 0), NT)
    xhat, spread = norm_parts(hidden)
    low = (xhat * vectors[2:3, :] + vectors[3:4, :]).astype(BF)
    normed_grad[0] = low
    cotangent = upper[...]
    final = hidden + vectors[8:9, :]
    grad_normed = jnp.zeros_like(hidden)
    for r in range(n_head):
        peer = me[0] ^ r
        into, down = whole_matrix(weights[r], 1), whole_matrix(weights[r], 2)
        pre = dot(low, into, NN) + hidden_bias[pl.ds(peer, 1), :]
        phi = 0.5 * (1.0 + lax.erf(pre * (0.5**0.5)))
        active = (pre * phi).astype(BF)
        final = final + dot(active, down, NT)
        slope = phi + pre * jnp.exp(-0.5 * pre * pre) * (0.5 / jnp.pi) ** 0.5
        low_grad = (dot(cotangent, down, NN) * slope).astype(BF)
        pre_sums[pl.ds(peer, 1), :] = jnp.sum(low_grad.astype(F32), axis=0, keepdims=True)
        grad_normed = grad_normed + dot(low_grad, into, NT)
        act_pre[peer, :, 0:columns] = active
        act_pre[peer, :, slot : slot + columns] = low_grad
    layer_out[...] = final.astype(BF)
    wide = cotangent.astype(F32)
    grad = wide + norm_back(grad_normed * vectors[2:3, :], xhat, spread)
    grad_hidden[...] = grad
    grad_small = grad.astype(BF)
    normed_grad[1] = grad_small
    for r in range(n_head):
        grad_heads[r][...] = dot(grad_small, whole_matrix(weights[r], 0), NN).astype(BF)
    sums[0:1, :] = jnp.sum(grad_normed * xhat, axis=0, keepdims=True)
    sums[1:2, :] = jnp.sum(grad_normed, axis=0, keepdims=True)
    sums[2:3, :] = jnp.sum(grad, axis=0, keepdims=True)
    sums[3:4, :] = jnp.sum(wide, axis=0, keepdims=True)


def parcel_slot(columns):
    return (columns + LANES - 1) // LANES * LANES


def weight_grads_body(n_head, need, done, *refs):
    given, mixed, refs = refs[:n_head], refs[n_head : 2 * n_head], refs[2 * n_head :]
    me, act_pre, normed_one, dqkv = refs[:4]
    normed_grad, out = refs[4 : 4 + n_head], refs[-1]
    columns = mixed[0].shape[1]
    slot = parcel_slot(columns)

    def all_rows(pick):
        return jnp.concatenate([pick(me[0] ^ r) for r in range(n_head)], axis=0)

    need(2 * n_head + 2, 2 * n_head + 3)
    for k in range(3):
        put_matrix(out, k, dot(normed_one[...], dqkv[k], TN).astype(BF))
    need(*range(2 * n_head), 2 * n_head + 1, *range(2 * n_head + 4, 3 * n_head + 4))
    heads_out = jnp.concatenate([m[...] for m in mixed], axis=0)
    put_matrix(out, 3, dot(jnp.concatenate([n[1] for n in normed_grad], axis=0), heads_out, TN).astype(BF))
    grad_pre = all_rows(lambda p: act_pre[p, :, slot : slot + columns])
    put_matrix(out, 4, dot(jnp.concatenate([n[0] for n in normed_grad], axis=0), grad_pre, TN).astype(BF))
    cotangent = jnp.concatenate([g[1] for g in given], axis=0)
    put_matrix(out, 5, dot(cotangent, all_rows(lambda p: act_pre[p, :, 0:columns]), TN).astype(BF))


def merge_body(need, done, *refs):
    parts, out = refs[:-1], refs[-1]
    need(*range(len(parts)))
    value = parts[0][...].astype(F32)
    for part in parts[1:]:
        value = value + part[...].astype(F32)
    out[...] = value.astype(BF)


def input_body(n_head, n_vectors, need, done, *refs):
    parts, refs = refs[:n_head], refs[n_head:]
    me, rows, grad_hidden, vectors, sums, column_sums, pre_sums, table_grad, input_grad, parcel, terms = refs
    need(*range(n_head), *range(n_head + 1, n_head + 8))
    grad_normed = parts[0][...].astype(F32)
    for part in parts[1:]:
        grad_normed = grad_normed + part[...].astype(F32)
    xhat, spread = norm_parts(rows[...].astype(F32))
    input_grad[...] = (grad_hidden[...] + norm_back(grad_normed * vectors[0:1, :], xhat, spread)).astype(BF)
    done(0)
    columns = column_sums.shape[2]
    terms[...] = jnp.zeros_like(terms)
    terms[0:1, :] = jnp.sum(grad_normed * xhat, axis=0, keepdims=True)
    terms[1:2, :] = jnp.sum(grad_normed, axis=0, keepdims=True)
    terms[2:4, :] = sums[0:2, :]
    terms[6:7, :] = sums[2:3, :]
    terms[8:9, :] = sums[3:4, :]
    for j in range(n_head):
        span = slice(j * columns, (j + 1) * columns)
        for i in range(2):
            terms[4 + i : 5 + i, span] = column_sums[i, j : j + 1, :]
        terms[7:8, span] = pre_sums[j : j + 1, :]
    inner, outer, height, _ = parcel.shape
    lanes, height = vectors.shape[1] // (inner * outer), height - VECTOR_ROWS
    parcel[:, :, :VECTOR_ROWS, :] = jnp.zeros((inner, outer, VECTOR_ROWS, LANES), BF)
    for d in range(inner * outer):
        at = me[1] ^ d
        a, b = at % inner, at // inner
        parcel[a, b, :VECTOR_ROWS, 0:lanes] = terms[:, d * lanes : (d + 1) * lanes].astype(BF)
        parcel[a, b, VECTOR_ROWS:, :] = table_grad[d * height : (d + 1) * height, :]


def adamw_update(weight, first_moment, second_moment, gradient, learn_rate):
    first_new = BETA_FIRST * first_moment + (1.0 - BETA_FIRST) * gradient
    second_new = BETA_SECOND * second_moment + (1.0 - BETA_SECOND) * gradient * gradient
    first_hat = first_new / (1.0 - BETA_FIRST**ADAM_STEP)
    second_hat = second_new / (1.0 - BETA_SECOND**ADAM_STEP)
    weight_new = weight - learn_rate * (
        first_hat / (jnp.sqrt(second_hat) + ADAM_EPSILON) + WEIGHT_DECAY * weight
    )
    return (weight_new, first_new, second_new)


def shard_body(need, done, arrived, shards, squares):
    need(0)
    value = arrived[0].astype(F32)
    for d in range(1, arrived.shape[0]):
        value = value + arrived[d].astype(F32)
    shards[...] = value
    squares[...] = jnp.broadcast_to(jnp.sum(value * value).reshape(1, 1), squares.shape)


def told_body(need, done, *refs):
    parts, (squares, shard, told) = refs[:-3], refs[-3:]
    need(*range(len(parts) + 1))
    value = parts[0][...].astype(F32)
    for part in parts[1:]:
        value = value + part[...].astype(F32)
    table = value[VECTOR_ROWS:]
    shard[...] = table
    here = jnp.sum(table * table).reshape(1, 1) + squares[0:1, 0:1]
    row = lax.broadcasted_iota(jnp.int32, (VECTOR_ROWS, LANES), 0)
    lane = lax.broadcasted_iota(jnp.int32, (VECTOR_ROWS, LANES), 1)
    message = jnp.where((row == VECTOR_ROWS - 1) & (lane == 0), here, value[:VECTOR_ROWS])
    told[...] = jnp.broadcast_to(message[None], told.shape)


def update_body(n_head, n_vectors, need, done, *refs):
    need(1)
    me, told, shards, out_shard, down_shard, table_shard = refs[:6]
    params, outs = refs[6:21], refs[21:36]
    norm_out = refs[36]
    n_dp = told.shape[0] // n_head

    def merged(d):
        value = told[d * n_head]
        for j in range(1, n_head):
            value = value + told[d * n_head + j]
        return value

    row = lax.broadcasted_iota(jnp.int32, (VECTOR_ROWS, LANES), 0)

    def square(d, total):
        value = merged(d)
        return total + jnp.where(row < n_vectors, value * value, jnp.where(row == VECTOR_ROWS - 1, value, 0.0))

    total = lax.fori_loop(0, n_dp, square, jnp.zeros((VECTOR_ROWS, LANES), F32))
    grad_norm = jnp.sqrt(jnp.sum(total).reshape(1, 1))
    norm_out[...] = jnp.broadcast_to(grad_norm, norm_out.shape)
    factor = CLIP_NORM / jnp.maximum(grad_norm, CLIP_NORM)

    def update(at, gradient, rate, pick=...):
        weight, first, second = (ref[pick] for ref in params[3 * at : 3 * at + 3])
        for ref, value in zip(outs[3 * at : 3 * at + 3], adamw_update(weight, first, second, gradient * factor, rate)):
            ref[pick] = value

    for k in range(3):
        update(0, shards[k], RATE_MATRIX, k)
    update(0, shards[4], RATE_MATRIX, 3)
    update(1, out_shard[...], RATE_OUTPUT)
    update(2, down_shard[...], RATE_MATRIX)
    mine = merged(me[1])
    size = params[9].shape[1]
    gradient = jnp.zeros((n_vectors, size), F32)
    for j in range(n_head):
        gradient = jnp.where(me[0] == j, mine[:n_vectors, j * size : (j + 1) * size], gradient)
    update(3, gradient, RATE_VECTOR)
    heads = params[12].shape[0]
    for c in range(table_shard.shape[0] // heads):
        update(4, table_shard[c * heads : (c + 1) * heads, :], RATE_VECTOR, (slice(None), slice(c * LANES, (c + 1) * LANES)))


def exchange(value, axis):
    return lax.all_to_all(value, axis, split_axis=0, concat_axis=0, tiled=True)


def spread_all(value, axis):
    size = lax.axis_size(axis)
    return exchange(jnp.broadcast_to(value[None], (size, *value.shape)), axis)


def swap(values, n_head):
    return [values[0]] + [
        lax.ppermute(values[r], "head", [(i, i ^ r) for i in range(n_head)]) for r in range(1, n_head)
    ]


def struct(shape, dtype):
    return jax.ShapeDtypeStruct(shape, dtype)


def on_device(
    node_rows,
    output_grad,
    weight_in,
    first_in,
    second_in,
    weight_out,
    first_out,
    second_out,
    weight_down,
    first_down,
    second_down,
    vectors,
    first_vectors,
    second_vectors,
    bias_table,
    first_table,
    second_table,
    big_counts,
    small_counts,
    big_distance,
    small_distance,
    big_paths,
    small_paths,
    big_lengths,
    small_lengths,
):
    everyone = ("dp", "head")
    n_dp, n_head = lax.axis_size("dp"), lax.axis_size("head")
    head_index, dp_index = lax.axis_index("head"), lax.axis_index("dp")
    me = head_index.reshape(1).astype(jnp.int32)
    shard_rows, columns = weight_in.shape[1], weight_in.shape[2]
    model = shard_rows * n_dp
    my_rows = node_rows.shape[0]
    group_rows = my_rows * n_head
    heads = columns // HEAD_DIM
    width, narrow = big_distance.shape[1], small_distance.shape[1]
    pairs = small_distance.shape[0] // 2
    table_chunks = bias_table.shape[0] // LANES
    all_chunks = table_chunks * n_dp
    n_vectors, shard_width = vectors.shape
    stacked = shard_rows % 16 == 0
    big_ints = (big_distance, big_paths, big_lengths)
    small_ints = (small_distance, small_paths, small_lengths)
    inner = inner_of(n_dp)
    outer = n_dp // inner
    dp_pairs = lambda k: [(i, i ^ k) for i in range(n_dp)]
    us = jnp.stack([head_index, dp_index]).astype(jnp.int32)
    lanes_used = model // n_dp

    def far_shards(value):
        return [value] + [lax.ppermute(value, "dp", dp_pairs(k)) for k in range(inner, n_dp, inner)]

    def near_shards(values):
        value = jnp.stack(values)
        return [value] + [lax.ppermute(value, "dp", dp_pairs(k)) for k in range(1, inner)]

    def to_head(value, r):
        return lax.ppermute(value, "head", [(i, i ^ r) for i in range(n_head)])

    far = n_head // 2
    near_heads = range(1, far)

    rest_sent = jnp.stack([weight_out.astype(BF).T, weight_in[3].astype(BF), weight_down.astype(BF).T])
    rest_sent, my_table = lax.optimization_barrier((rest_sent, bias_table))
    with jax.named_scope("rest_far"):
        rest_far = far_shards(rest_sent)
    table_sent = my_table.astype(BF).T.reshape(heads, table_chunks, LANES).transpose(1, 0, 2)
    with jax.named_scope("table_all"):
        table_all = spread_all(table_sent, "dp").reshape(all_chunks * heads, LANES)
    given = {0: jnp.stack([node_rows, output_grad])}
    with jax.named_scope("rows_far"):
        given[far] = to_head(given[0], far)
    qkv_sent = weight_in[:3].astype(BF)
    vectors_sent = jnp.pad(vectors, ((0, VECTOR_ROWS - n_vectors), (0, LANES - shard_width)))
    table_all, vectors_sent, qkv_sent, *rest_far = lax.optimization_barrier(
        (table_all, vectors_sent, qkv_sent, *rest_far)
    )
    with jax.named_scope("vectors_all"):
        vector_pieces = spread_all(vectors_sent, everyone)
    with jax.named_scope("rest_near"):
        rest_near = near_shards(rest_far)
    with jax.named_scope("qkv_far"):
        qkv_far = far_shards(qkv_sent)

    def pair_bias(part, table, ints):
        rows = width // sum(BIG_QUARTERS) * BIG_QUARTERS[part]
        big_range = struct((heads, width // LANES, rows, LANES), F32)
        return kernel_call(
            lambda *refs: bias_body(part, *refs),
            ([struct((heads, pairs, narrow, LANES), F32)] if part == 0 else []) + [big_range],
            "pair_bias",
            12 if part == 0 else 20,
            (table, *ints),
            [pltpu.VMEM((heads, all_chunks // 2, SUB, LANES), jnp.int32)],
        )

    small_bias, *big_bias = pair_bias(0, table_all, (*small_ints, *big_ints))
    held = lax.optimization_barrier((small_bias, vector_pieces, table_all, given[far], *rest_near, *qkv_far))
    (small_bias, vector_pieces, table_all, given[far]), held = held[:4], held[4:]
    rest_near, qkv_far = held[:inner], held[inner:]
    weights_rest = jnp.concatenate(rest_near)
    with jax.named_scope("qkv_near"):
        qkv_near = near_shards(qkv_far)
    if not stacked:
        order = jnp.argsort(jnp.array(xor_order(n_dp), jnp.int32) ^ dp_index)
        weights_rest = weights_rest[order].transpose(1, 0, 2, 3).reshape(3, model, columns)
    weights_held = {0: weights_rest}
    with jax.named_scope("rest_far_head"):
        weights_held[far] = to_head(weights_rest, far)
    with jax.named_scope("rows_near"):
        for r in near_heads:
            given[r], given[far + r] = to_head(given[0], r), to_head(given[far], r)
    for part in range(1, BIG_PARTS):
        big_bias += pair_bias(part, table_all, big_ints)
    held = lax.optimization_barrier((big_bias[-1], *qkv_near, *[given[r] for r in range(n_head)]))
    big_bias[-1], qkv_near, given = held[0], held[1 : 1 + inner], held[1 + inner :]
    with jax.named_scope("rest_near_head"):
        for r in near_heads:
            weights_held[r] = to_head(weights_held[0], r)
    weights_attend = jnp.concatenate(qkv_near)
    if not stacked:
        weights_attend = weights_attend[order].transpose(1, 0, 2, 3).reshape(3, model, columns)

    block = struct((my_rows, columns), BF)
    rows_block = struct((my_rows, model), BF)
    normed_one, qkv, big_probs, small_probs, all_vectors, hidden_bias, *mixed = kernel_call(
        lambda *refs: forward_body(n_head, *refs),
        [
            struct((group_rows, model), BF),
            struct((3, group_rows, columns), BF),
            struct((heads, width, width), F32),
            struct((heads, pairs, 2 * narrow, 2 * narrow), F32),
            struct((n_vectors, model), F32),
            struct((n_head, columns), F32),
            *[block] * n_head,
        ],
        "attend_forward",
        12,
        (*given, us, big_counts, small_counts, vector_pieces, weights_attend, small_bias, *big_bias),
        [pltpu.VMEM((group_rows, columns), BF)],
        range(n_head, n_head + 3),
        (n_head + 4,) if stacked else (),
        n_head,
    )
    with jax.named_scope("mixed_rows"):
        mixed_rows = swap(mixed, n_head)
    mixed_rows[0], *held = lax.optimization_barrier((mixed_rows[0], *[weights_held[r] for r in range(far + 1)]))
    weights_held.update(enumerate(held))
    with jax.named_scope("rest_near_head"):
        for r in near_heads:
            weights_held[far + r] = to_head(weights_held[far], r)
    weights_rest = [weights_held[r] for r in range(n_head)]

    layer_out, grad_hidden, sums, pre_sums, normed_grad, act_pre, *grad_heads = kernel_call(
        lambda *refs: middle_body(n_head, *refs),
        [
            rows_block,
            struct((my_rows, model), F32),
            struct((4, model), F32),
            struct((n_head, columns), F32),
            struct((2, my_rows, model), BF),
            struct((n_head, my_rows, 2 * parcel_slot(columns)), BF),
            *[block] * n_head,
        ],
        "feed_forward",
        6,
        (*mixed_rows, us, node_rows, output_grad, all_vectors, hidden_bias, *weights_rest),
        (),
        (n_head,),
        range(n_head + 5, 2 * n_head + 5) if stacked else (),
        n_head,
    )
    with jax.named_scope("grad_heads"):
        grad_heads = swap(grad_heads, n_head)
    with jax.named_scope("act_pre"):
        act_pre = exchange(act_pre, "head")
    with jax.named_scope("normed_grad"):
        rows_held = {0: normed_grad}
        for r in (far, *range(1, far)):
            rows_held[r] = lax.ppermute(normed_grad, "head", [(i, i ^ r) for i in range(n_head)])

    small_rows, big_rows, dqkv, column_sums, *rows_sent = kernel_call(
        lambda *refs: backward_body(n_head, *refs),
        [
            struct((pairs * narrow * SUB, LANES), F32),
            struct((width // LANES * width * SUB, LANES), F32),
            struct((3, group_rows, columns), BF),
            struct((2, n_head, columns), F32),
            *[rows_block] * n_head,
        ],
        "attend_backward",
        14,
        (*grad_heads, us, qkv, small_probs, big_probs, weights_attend),
        [pltpu.VMEM((group_rows, columns), BF)],
        (n_head,),
        (n_head + 4,) if stacked else (),
        n_head,
    )
    small_rows, *arrived = lax.optimization_barrier((small_rows, *[rows_held[r] for r in range(1, far + 1)]))
    rows_held.update(zip(range(1, far + 1), arrived))
    with jax.named_scope("normed_grad"):
        for r in range(1, far):
            rows_held[far + r] = lax.ppermute(rows_held[far], "head", [(i, i ^ r) for i in range(n_head)])
    (weight_grads,) = kernel_call(
        lambda *refs: weight_grads_body(n_head, *refs),
        [struct((n_dp, 6, shard_rows, columns) if stacked else (6, model, columns), BF)],
        "weight_grads",
        6,
        (*given, *mixed, us, act_pre, normed_one, dqkv, *[rows_held[r] for r in range(n_head)]),
        (),
        (2 * n_head,),
    )
    if not stacked:
        weight_grads = weight_grads.reshape(6, n_dp, shard_rows, columns).transpose(1, 0, 2, 3)
    weight_grads, small_rows, *rows_sent = lax.optimization_barrier((weight_grads, small_rows, *rows_sent))
    with jax.named_scope("weight_grads"):
        weights_arrived = exchange(weight_grads, "dp")
    with jax.named_scope("grad_normed_one"):
        rows_back = swap(rows_sent, n_head)
    (table_grad,) = kernel_call(
        scatter_body,
        [struct((all_chunks * heads, LANES), BF)],
        "table_scatter",
        40,
        (small_rows, *small_ints, big_rows, *big_ints),
        [pltpu.VMEM((LANES, all_chunks * heads), F32)],
    )
    table_grad, *rows_back = lax.optimization_barrier((table_grad, *rows_back))
    table_rows = table_chunks * heads
    block = struct((outer, VECTOR_ROWS + table_rows, LANES), BF)
    input_grad, *inner_sent = kernel_call(
        lambda *refs: input_body(n_head, n_vectors, *refs),
        [rows_block, (inner, block)],
        "input_grad",
        3,
        (*rows_back, us, node_rows, grad_hidden, all_vectors, sums, column_sums, pre_sums, table_grad),
        [pltpu.VMEM((VECTOR_ROWS, model), F32)],
        (n_head,),
    )
    with jax.named_scope("table_inner"):
        arrived = [inner_sent[0]] + [lax.ppermute(inner_sent[k], "dp", dp_pairs(k)) for k in range(1, inner)]
    weights_arrived, *arrived = lax.optimization_barrier((weights_arrived, *arrived))
    outer_sent = kernel_call(
        merge_body,
        [(outer, struct(block.shape[1:], BF))],
        "merge_table",
        1,
        tuple(arrived),
    )
    with jax.named_scope("table_outer"):
        parts = [outer_sent[0]] + [
            lax.ppermute(outer_sent[k], "dp", dp_pairs(k * inner)) for k in range(1, outer)
        ]
    shards, squares = kernel_call(
        shard_body,
        [struct((6, shard_rows, columns), F32), struct((1, LANES), F32)],
        "shard_sums",
        3,
        (weights_arrived,),
    )
    table_shard, told = kernel_call(
        told_body,
        [struct((table_rows, LANES), F32), struct((n_dp * n_head, VECTOR_ROWS, LANES), F32)],
        "table_sums",
        1,
        (*parts, squares),
    )
    with jax.named_scope("squares"):
        told = exchange(told, everyone)
    params = (weight_in, first_in, second_in, weight_out, first_out, second_out)
    params += (weight_down, first_down, second_down, vectors, first_vectors, second_vectors)
    params += (bias_table.T, first_table.T, second_table.T)
    *updated, grad_norm = kernel_call(
        lambda *refs: update_body(n_head, n_vectors, *refs),
        [*[struct(p.shape, F32) for p in params], struct((1, LANES), F32)],
        "update",
        3,
        (us, told, shards, shards[3].T, shards[5].T, table_shard, *params),
        (),
        (0,),
        ready=range(2, 21),
        limit=16 << 20,
    )
    updated = updated[:12] + [value.T for value in updated[12:]]
    return (layer_out, input_grad, grad_norm[0, 0], *updated)


def solution(mesh):
    rows = P(("dp", "head"), None)
    square = P(None, "dp", "head")
    across = P("head", "dp")
    thin = P(None, ("dp", "head"))
    table = P("dp", "head")
    return jax.shard_map(
        on_device,
        mesh=mesh,
        in_specs=(rows, rows)
        + (square,) * 3
        + (across,) * 6
        + (thin,) * 3
        + (table,) * 3
        + (P("dp"), P("dp", None))
        + (P("dp", None, None),) * 2
        + (P(None, "dp", None, None),) * 2
        + (P("dp", None, None),) * 2,
        out_specs=(rows, rows, P()) + (square,) * 3 + (across,) * 6 + (thin,) * 3 + (table,) * 3,
        check_vma=False,
    )
```

```python
import jax
import jax.numpy as jnp
from jax import lax
from jax.experimental import pallas as pl
from jax.experimental.pallas import tpu as pltpu
from jax.sharding import PartitionSpec as P

HEAD_DIM = 24
NDIST = 512
NTYPE = 1536
STEPS = 5
ADAM_STEP = 10

NORM_EPSILON = 1e-05
NEGATIVE_FILL = -1e30
BETA_FIRST = 0.9
BETA_SECOND = 0.95
ADAM_EPSILON = 1e-08
RATE_MATRIX = 0.02
RATE_OUTPUT = 0.05
RATE_VECTOR = 0.15
WEIGHT_DECAY = 0.01
CLIP_NORM = 1.0

LANES = 128
SUB = 8
FIRST = [0] + [(NDIST + n * NTYPE) // LANES for n in range(STEPS)]
CHUNKS = [NDIST // LANES] + [NTYPE // LANES] * STEPS
LOOKUPS = STEPS + 1
VECTOR_ROWS = 16
BIG_QUARTERS = (1, 3)
BIG_PARTS = len(BIG_QUARTERS)
MESSAGE_ROWS = 8
PIECES = 3
PIECE_ROWS = 16
FIXED = 8192.0
NOWHERE = 4095
SCALE = HEAD_DIM**-0.5
BF = jnp.bfloat16
F32 = jnp.float32
VMEM_BYTES = 56 << 20

NN = (((1,), (0,)), ((), ()))
NT = (((1,), (1,)), ((), ()))
TN = (((0,), (0,)), ((), ()))


def dot(left, right, dims):
    return lax.dot_general(left, right, dims, preferred_element_type=F32)


def inner_of(size):
    return 1 << ((size.bit_length() - 1) // 2)


def xor_order(size):
    inner = inner_of(size)
    return [a * inner + b for b in range(inner) for a in range(size // inner)]


def kernel_call(body, outs, name, micros, args, scratch=(), smem_in=(), placed=(), us_at=None, ready=(), limit=VMEM_BYTES):
    n_in, n_out = len(args), len(outs)
    moved = [i for i in range(n_in) if i not in smem_in and i not in ready]
    blocks = [out[0] if isinstance(out, tuple) else 0 for out in outs]
    shapes = [out[1] if isinstance(out, tuple) else out for out in outs]
    flat = [(i, k) for i in range(n_out) for k in range(max(blocks[i], 1))]
    n_sems = sum(args[i].shape[0] if i in placed else 1 for i in moved)

    def wrapped(*refs):
        given, results = refs[:n_in], refs[n_in : n_in + len(flat)]
        refs = refs[n_in + len(flat) :]
        held = dict(zip(moved, refs))
        made, refs = refs[len(moved) : len(moved) + n_out], refs[len(moved) + n_out :]
        rest, (in_sems, out_sems) = refs[:-2], refs[-2:]
        arriving, sem = {}, 0
        for i in moved:
            pieces = [(given[i], held[i])]
            if i in placed:
                size = args[i].shape[0]
                pieces = [
                    (given[i].at[k], held[i].at[given[us_at][1] ^ other]) for k, other in enumerate(xor_order(size))
                ]
            arriving[i] = [pltpu.make_async_copy(a, b, in_sems.at[sem + n]) for n, (a, b) in enumerate(pieces)]
            sem += len(pieces)
        leaving = [
            pltpu.make_async_copy(made[i].at[k] if blocks[i] else made[i], results[at], out_sems.at[at])
            for at, (i, k) in enumerate(flat)
        ]
        for i in moved:
            for copy in arriving[i]:
                copy.start()
        waiting, unsent = list(moved), list(range(n_out))

        def need(*which):
            for i in which:
                if i in waiting:
                    waiting.remove(i)
                    for copy in arriving[i]:
                        copy.wait()

        def done(*which):
            for i in which:
                if i in unsent:
                    unsent.remove(i)
                    for at, (j, _) in enumerate(flat):
                        if i == j:
                            leaving[at].start()

        body(need, done, *[held.get(i, given[i]) for i in range(n_in)], *made, *rest)
        need(*moved)
        done(*range(n_out))
        for copy in leaving:
            copy.wait()

    anywhere, smem = pl.BlockSpec(memory_space=pl.ANY), pl.BlockSpec(memory_space=pltpu.SMEM)
    vmem = pl.BlockSpec(memory_space=pltpu.VMEM)
    return pl.pallas_call(
        wrapped,
        out_shape=tuple(shapes[i] for i, _ in flat),
        in_specs=[smem if i in smem_in else vmem if i in ready else anywhere for i in range(n_in)],
        out_specs=tuple([anywhere] * len(flat)),
        scratch_shapes=[pltpu.VMEM(args[i].shape, args[i].dtype) for i in moved]
        + [pltpu.VMEM((n, *o.shape) if n else o.shape, o.dtype) for n, o in zip(blocks, shapes)]
        + list(scratch)
        + [pltpu.SemaphoreType.DMA((n_sems,)), pltpu.SemaphoreType.DMA((len(flat),))],
        name=name,
        compiler_params=pltpu.CompilerParams(vmem_limit_bytes=limit),
        cost_estimate=pl.CostEstimate(flops=int(micros * 1e9), bytes_accessed=1 << 20, transcendentals=0),
    )(*args)


def big_block(refs, block, half):
    distance, paths, lengths = refs
    rows, lanes = pl.ds(SUB * block, SUB), slice(LANES * half, LANES * half + LANES)
    return [distance[0, rows, lanes]] + [paths[n, 0, rows, lanes] for n in range(STEPS)], lengths[0, rows, lanes]


def small_block(refs, block, pair):
    distance, paths, lengths = refs
    rows = pl.ds(SUB * block, SUB)

    def two(ref, *lead):
        return jnp.concatenate([ref[(*lead, 2 * pair, rows)], ref[(*lead, 2 * pair + 1, rows)]], axis=1)

    return [two(distance)] + [two(paths, n) for n in range(STEPS)], two(lengths)


def each_block(load, refs, first, count, sides, group, step):
    def some(at, carry):
        blocks = [first + at * group + u for u in range(group)]
        step([(*load(refs, block, side), block, side) for block in blocks for side in range(sides)])
        return carry

    lax.fori_loop(0, count // group, some, 0)


def bias_body(part, need, done, table, *refs):
    small, refs = (refs[:3], refs[3:]) if part == 0 else (None, refs)
    big, outs, words = refs[:3], refs[3:-1], refs[-1]
    need(0)
    heads, count = words.shape[:2]
    for k in range(count):
        low = jnp.round(table[SUB * 2 * k : SUB * (2 * k + 1), :].astype(F32) * FIXED).astype(jnp.int32)
        high = jnp.round(table[SUB * (2 * k + 1) : SUB * (2 * k + 2), :].astype(F32) * FIXED).astype(jnp.int32)
        word = (high << 16) | (low & 0xFFFF)
        for h in range(heads):
            words[h, k] = jnp.broadcast_to(word[h : h + 1], (SUB, LANES))

    def step(store):
        def run(parts):
            for index, lengths, block, side in parts:
                share = (1.0 / FIXED) / lengths.astype(F32)
                first, edges = [None] * heads, [None] * heads
                for t in range(LOOKUPS):
                    code = index[t]
                    lane = code & (LANES - 1)
                    odd = [(code & bit) != 0 for bit in (256, 512, 1024)]
                    shift = ((code >> 3) & 16) ^ 16
                    live = lengths > t - 1
                    for h in range(heads):
                        found = [
                            jnp.take_along_axis(words[h, FIRST[t] // 2 + k], lane, axis=1, mode="promise_in_bounds")
                            for k in range(CHUNKS[t] // 2)
                        ]
                        level = 0
                        while len(found) > 1:
                            found = [
                                jnp.where(odd[level], found[k + 1], found[k]) if k + 1 < len(found) else found[k]
                                for k in range(0, len(found), 2)
                            ]
                            level += 1
                        value = (found[0] << shift) >> 16
                        if t == 0:
                            first[h] = value
                        else:
                            value = jnp.where(live, value, 0)
                            edges[h] = value if edges[h] is None else edges[h] + value
                for h in range(heads):
                    value = first[h].astype(F32) * (1.0 / FIXED) + edges[h].astype(F32) * share
                    store(h, side, block, value)

        return run

    if small:

        def store_small(h, side, block, value):
            outs[0][h, side, pl.ds(SUB * block, SUB), :] = value

        need(1, 2, 3)
        each_block(small_block, small, 0, small[0].shape[1] // SUB, small[0].shape[0] // 2, 1, step(store_small))
        done(0)
    need(*range(1, 7 if small else 4))
    out = outs[-1]
    count = out.shape[2] // SUB
    first_block = big[0].shape[1] // SUB // sum(BIG_QUARTERS) * sum(BIG_QUARTERS[:part])

    def store_big(h, side, block, value):
        out[h, side, pl.ds(SUB * (block - first_block), SUB), :] = value

    each_block(big_block, big, first_block, count, big[0].shape[2] // LANES, 1, step(store_big))


def scatter_body(need, done, small_grads, sd, sp, sl, big_grads, bd, bp, bl, me, vector_rows, parcel, total):
    total[...] = jnp.zeros_like(total)
    sub = lax.broadcasted_iota(jnp.int32, (2 * SUB, LANES), 0)
    low_pattern = [(sub + 2 * SUB * k).astype(F32).astype(BF) for k in range(LANES // (2 * SUB))]
    upper = (sub >= SUB).astype(jnp.int32)
    high_pattern = [(2 * k + upper).astype(F32).astype(BF) for k in range(max(CHUNKS) // 2)]
    zero, one = jnp.zeros((2 * SUB, LANES), BF), jnp.ones((2 * SUB, LANES), BF)

    def twice(value):
        return jnp.concatenate([value, value], axis=0).astype(BF)

    def step(grads, side_rows):
        def run(parts):
            whole, shared = [], []
            for index, lengths, block, side in parts:
                inverse = 1.0 / lengths.astype(F32)
                for s in range(SUB):
                    g = grads[pl.ds((side * side_rows + SUB * block + s) * SUB, SUB), :]
                    whole.append(twice(g))
                    shared.append(twice(g * jnp.broadcast_to(inverse[s : s + 1], (SUB, LANES))))
            for t in range(LOOKUPS):
                left, right = [], []
                for part, (index, lengths, _, _) in enumerate(parts):
                    code = index[t] if t == 0 else jnp.where(lengths > t - 1, index[t], NOWHERE)
                    for s in range(SUB):
                        spread = jnp.broadcast_to(code[s : s + 1], (SUB, LANES))
                        low = twice((spread & (LANES - 1)).astype(F32))
                        high = twice((spread >> 7).astype(F32))
                        source = (whole if t == 0 else shared)[SUB * part + s]
                        left.append(jnp.concatenate([jnp.where(low == p, one, zero) for p in low_pattern], axis=0))
                        right.append(
                            jnp.concatenate(
                                [jnp.where(high == p, source, zero) for p in high_pattern[: CHUNKS[t] // 2]], axis=0
                            )
                        )
                span = slice(SUB * FIRST[t], SUB * (FIRST[t] + CHUNKS[t]))
                total[:, span] += dot(jnp.concatenate(left, axis=1), jnp.concatenate(right, axis=1), NT)

        return run

    need(0, 1, 2, 3)
    narrow, width = sd.shape[1], bd.shape[1]
    each_block(small_block, (sd, sp, sl), 0, narrow // SUB, sd.shape[0] // 2, 4, step(small_grads, narrow))
    need(4, 5, 6, 7)
    each_block(big_block, (bd, bp, bl), 0, width // SUB, width // LANES, 4, step(big_grads, width))
    need(9)
    inner, outer, height, _ = parcel.shape
    height -= VECTOR_ROWS
    parcel[:, :, :VECTOR_ROWS, :] = vector_rows[...]
    table = total[...].T.astype(BF)
    for d in range(inner * outer):
        at = me[1] ^ d
        parcel[at % inner, at // inner, VECTOR_ROWS:, :] = table[d * height : (d + 1) * height]


def attend_matrix(ref, k, model):
    if ref.shape[1] == model:
        return ref[k]
    rows = model // ref.shape[0]
    return ref[:, k * rows : (k + 1) * rows, :].reshape(model, ref.shape[2])


def whole_matrix(ref, k):
    if len(ref.shape) == 3:
        return ref[k]
    value = ref[:, k]
    return value.reshape(value.shape[0] * value.shape[1], value.shape[2])


def norm_parts(values):
    center = values - jnp.mean(values, axis=-1, keepdims=True)
    spread = lax.rsqrt(jnp.mean(center * center, axis=-1, keepdims=True) + NORM_EPSILON)
    return center * spread, spread


def norm_back(scaled, xhat, spread):
    return spread * (
        scaled
        - jnp.mean(scaled, axis=-1, keepdims=True)
        - xhat * jnp.mean(scaled * xhat, axis=-1, keepdims=True)
    )


def head_lanes(head, width):
    lane = lax.broadcasted_iota(jnp.int32, (1, width), 1)
    return (lane >= head * HEAD_DIM) & (lane < (head + 1) * HEAD_DIM)


def peer_block(me, r, rows):
    return pl.ds(pl.multiple_of((me[0] ^ r) * rows, rows), rows)


def forward_body(n_head, vector_row, need, done, *refs):
    rows_in, refs = refs[:n_head], refs[n_head:]
    me, big_counts, small_counts, weights, small_bias = refs[:5]
    big_bias, refs = refs[5 : 5 + BIG_PARTS], refs[5 + BIG_PARTS :]
    pieces = weights
    if vector_row == 0:
        pieces, refs = refs[0], refs[1:]
    normed, qkv, big_probs, small_probs, vectors, hidden_bias = refs[:6]
    mixed_out, (mixed, flat, stack) = refs[6 : 6 + n_head], refs[6 + n_head :]
    block = rows_in[0].shape[1]
    need(*range(n_head), n_head + 3)
    if vector_row == 0:
        need(n_head + 5 + BIG_PARTS)
    n_vectors, size = vectors.shape[0], vectors.shape[1] // pieces.shape[0]
    for d in range(pieces.shape[0]):
        parts = [pieces[d, pl.ds(vector_row + p * PIECE_ROWS, PIECE_ROWS), 0:size].astype(F32) for p in range(PIECES)]
        vectors[:, d * size : (d + 1) * size] = sum(parts[1:], parts[0])[:n_vectors]
    heads, width = big_probs.shape[:2]
    pairs, wide = small_probs.shape[1:3]
    narrow = wide // 2
    columns = qkv.shape[2]
    halves = width // LANES
    biases = [None] * 2
    for j in range(n_head):
        span = slice(j * columns, (j + 1) * columns)
        hidden_bias[j : j + 1, :] = vectors[7:8, span]
        for i in range(2):
            value = jnp.where(me[0] == j, vectors[4 + i : 5 + i, span], 0.0)
            biases[i] = value if j == 0 else biases[i] + value
    for r in range(n_head):
        xhat, _ = norm_parts(rows_in[r][0].astype(F32))
        normed[peer_block(me, r, block), :] = (xhat * vectors[0:1, :] + vectors[1:2, :]).astype(BF)
    done(0, 4, 5)
    for k in range(3):
        value = dot(normed[...], attend_matrix(weights, k, normed.shape[1]), NN)
        if k != 1:
            value = value + biases[k // 2]
        qkv[k] = value.astype(BF)
    done(1)
    need(*range(n_head + 4, n_head + 5 + BIG_PARTS))
    big_live = lax.broadcasted_iota(jnp.int32, (1, width), 1) < big_counts[0]
    small_live = []
    row = lax.broadcasted_iota(jnp.int32, (wide, wide), 0)
    lane = lax.broadcasted_iota(jnp.int32, (wide, wide), 1)
    for pair in range(pairs):
        first = (row < narrow) & (lane < small_counts[0, 2 * pair])
        second = (row >= narrow) & (lane >= narrow) & (lane < narrow + small_counts[0, 2 * pair + 1])
        small_live.append(first | second)

    def attend(span, extra, live, store):
        for head in range(heads):
            mine = head_lanes(head, columns)
            query = jnp.where(mine, qkv[0, span, :], 0.0)
            size = query.shape[0]
            scores = dot(query, qkv[1, span, :], NT) * SCALE + extra(head)
            scores = jnp.where(live, scores, NEGATIVE_FILL)
            power = jnp.exp(scores - jnp.max(scores, axis=-1, keepdims=True))
            probs = power * (1.0 / jnp.sum(power, axis=-1, keepdims=True))
            store(head, probs)
            rows = slice(head * size, (head + 1) * size)
            flat[:size, rows] = probs.astype(BF)
            stack[rows, :] = jnp.where(mine, qkv[2, span, :], 0.0)
        every = slice(0, heads * size)
        mixed[span, :] = dot(flat[:size, every], stack[every, :], NN).astype(BF)

    def big_extra(head):
        return jnp.concatenate(
            [jnp.concatenate([part[head, half] for part in big_bias], axis=0) for half in range(halves)], axis=1
        )

    def store_big(head, probs):
        big_probs[head] = probs

    attend(slice(0, width), big_extra, big_live, store_big)
    done(2)
    for pair in range(pairs):

        def small_extra(head, pair=pair):
            extra = small_bias[head, pair]
            return jnp.concatenate([extra, extra], axis=0)

        def store_small(head, probs, pair=pair):
            small_probs[head, pair] = probs

        span = slice(width + pair * wide, width + (pair + 1) * wide)
        attend(span, small_extra, small_live[pair], store_small)
    done(3)
    for r in range(n_head):
        mixed_out[r][...] = mixed[peer_block(me, r, block), :]


def put_matrix(ref, k, value):
    if len(ref.shape) == 3:
        ref[k] = value
        return
    rows = ref.shape[2]
    for d in range(ref.shape[0]):
        ref[d, k] = value[d * rows : (d + 1) * rows]


def backward_body(n_head, need, done, *refs):
    need(*range(n_head), n_head + 1, n_head + 2)
    grads_in, refs = refs[:n_head], refs[n_head:]
    me, qkv, small_probs, big_probs, weights, small_rows, big_rows, dqkv, column_sums = refs[:9]
    rows_out, (grad_heads, tall, flat, stacks) = refs[9 : 9 + n_head], refs[9 + n_head :]
    heads, width = big_probs.shape[:2]
    pairs, wide = small_probs.shape[1:3]
    narrow = wide // 2
    columns = qkv.shape[2]
    halves = width // LANES
    block = grads_in[0].shape[0]
    for r in range(n_head):
        grad_heads[peer_block(me, r, block), :] = grads_in[r][...]

    need(n_head + 3)

    def attend(span, all_probs, store):
        for head in range(heads):
            mine = head_lanes(head, columns)
            probs = all_probs(head)
            upper = jnp.where(mine, grad_heads[span, :], 0.0)
            size = upper.shape[0]
            grad_probs = dot(upper, qkv[2, span, :], NT)
            inner = jnp.sum(probs * grad_probs, axis=-1, keepdims=True)
            grad_scores = (probs * (grad_probs - inner)).astype(BF)
            rows = slice(head * size, (head + 1) * size)
            tall[0, rows, :size] = grad_scores
            tall[1, rows, :size] = probs.astype(BF)
            flat[:size, rows] = grad_scores
            stacks[0, rows, :] = jnp.where(mine, qkv[0, span, :], 0.0)
            stacks[1, rows, :] = jnp.where(mine, qkv[1, span, :], 0.0)
            stacks[2, rows, :] = upper
            store(head, grad_scores.astype(F32))
        every = slice(0, heads * size)
        dqkv[0, span, :] = (dot(flat[:size, every], stacks[1, every, :], NN) * SCALE).astype(BF)
        dqkv[1, span, :] = (dot(tall[0, every, :size], stacks[0, every, :], TN) * SCALE).astype(BF)
        dqkv[2, span, :] = dot(tall[1, every, :size], stacks[2, every, :], TN).astype(BF)

    for pair in range(pairs):

        def store_small(head, value, at=pair * narrow * SUB):
            small_rows[pl.ds(at + head, narrow, stride=SUB), :] = value[:narrow] + value[narrow:]

        span = slice(width + pair * wide, width + (pair + 1) * wide)
        attend(span, lambda head, pair=pair: small_probs[head, pair], store_small)
    done(0)

    def store_big(head, value):
        for half in range(halves):
            big_rows[pl.ds(half * width * SUB + head, width, stride=SUB), :] = value[
                :, LANES * half : LANES * (half + 1)
            ]

    attend(slice(0, width), lambda head: big_probs[head], store_big)
    done(1, 2)
    need(n_head + 4)
    column_sums[...] = jnp.zeros_like(column_sums)
    for i, k in enumerate((0, 2)):
        column_sums[i, pl.ds(me[0], 1), :] = jnp.sum(dqkv[k].astype(F32), axis=0, keepdims=True)
    for r in range(n_head):
        rows = peer_block(me, r, block)
        model = rows_out[r].shape[1]
        total = dot(dqkv[0, rows, :], attend_matrix(weights, 0, model), NT)
        total = total + dot(dqkv[1, rows, :], attend_matrix(weights, 1, model), NT)
        total = total + dot(dqkv[2, rows, :], attend_matrix(weights, 2, model), NT)
        rows_out[r][...] = total.astype(BF)


def middle_body(n_head, need, done, *refs):
    mixed, refs = refs[:n_head], refs[n_head:]
    me, rows, upper, vectors, hidden_bias = refs[:5]
    weights, refs = refs[5 : 5 + n_head], refs[5 + n_head :]
    layer_out, grad_hidden, sums, pre_sums, normed_grad, act_pre = refs[:6]
    grad_heads = refs[6:]
    need(*range(2 * n_head + 5))
    columns = mixed[0].shape[1]
    slot = parcel_slot(columns)
    hidden = rows[...].astype(F32) + vectors[6:7, :]
    for r in range(n_head):
        hidden = hidden + dot(mixed[r][...], whole_matrix(weights[r], 0), NT)
    xhat, spread = norm_parts(hidden)
    low = (xhat * vectors[2:3, :] + vectors[3:4, :]).astype(BF)
    normed_grad[0] = low
    cotangent = upper[...]
    final = hidden + vectors[8:9, :]
    grad_normed = jnp.zeros_like(hidden)
    for r in range(n_head):
        peer = me[0] ^ r
        into, down = whole_matrix(weights[r], 1), whole_matrix(weights[r], 2)
        pre = dot(low, into, NN) + hidden_bias[pl.ds(peer, 1), :]
        phi = 0.5 * (1.0 + lax.erf(pre * (0.5**0.5)))
        active = (pre * phi).astype(BF)
        final = final + dot(active, down, NT)
        slope = phi + pre * jnp.exp(-0.5 * pre * pre) * (0.5 / jnp.pi) ** 0.5
        low_grad = (dot(cotangent, down, NN) * slope).astype(BF)
        pre_sums[pl.ds(peer, 1), :] = jnp.sum(low_grad.astype(F32), axis=0, keepdims=True)
        grad_normed = grad_normed + dot(low_grad, into, NT)
        act_pre[peer, :, 0:columns] = active
        act_pre[peer, :, slot : slot + columns] = low_grad
    layer_out[...] = final.astype(BF)
    wide = cotangent.astype(F32)
    grad = wide + norm_back(grad_normed * vectors[2:3, :], xhat, spread)
    grad_hidden[...] = grad
    grad_small = grad.astype(BF)
    normed_grad[1] = grad_small
    for r in range(n_head):
        grad_heads[r][...] = dot(grad_small, whole_matrix(weights[r], 0), NN).astype(BF)
    sums[0:1, :] = jnp.sum(grad_normed * xhat, axis=0, keepdims=True)
    sums[1:2, :] = jnp.sum(grad_normed, axis=0, keepdims=True)
    sums[2:3, :] = jnp.sum(grad, axis=0, keepdims=True)
    sums[3:4, :] = jnp.sum(wide, axis=0, keepdims=True)


def parcel_slot(columns):
    return (columns + LANES - 1) // LANES * LANES


def weight_grads_body(n_head, need, done, *refs):
    given, mixed, refs = refs[:n_head], refs[n_head : 2 * n_head], refs[2 * n_head :]
    me, act_pre, normed_one, dqkv = refs[:4]
    normed_grad, out = refs[4 : 4 + n_head], refs[-1]
    columns = mixed[0].shape[1]
    slot = parcel_slot(columns)

    def all_rows(pick):
        return jnp.concatenate([pick(me[0] ^ r) for r in range(n_head)], axis=0)

    need(2 * n_head + 2, 2 * n_head + 3)
    for k in range(3):
        put_matrix(out, k, dot(normed_one[...], dqkv[k], TN).astype(BF))
    need(*range(2 * n_head), 2 * n_head + 1, *range(2 * n_head + 4, 3 * n_head + 4))
    heads_out = jnp.concatenate([m[...] for m in mixed], axis=0)
    put_matrix(out, 3, dot(jnp.concatenate([n[1] for n in normed_grad], axis=0), heads_out, TN).astype(BF))
    grad_pre = all_rows(lambda p: act_pre[p, :, slot : slot + columns])
    put_matrix(out, 4, dot(jnp.concatenate([n[0] for n in normed_grad], axis=0), grad_pre, TN).astype(BF))
    cotangent = jnp.concatenate([g[1] for g in given], axis=0)
    put_matrix(out, 5, dot(cotangent, all_rows(lambda p: act_pre[p, :, 0:columns]), TN).astype(BF))


def merge_body(need, done, *refs):
    parts, out = refs[:-1], refs[-1]
    need(*range(len(parts)))
    value = parts[0][...].astype(F32)
    for part in parts[1:]:
        value = value + part[...].astype(F32)
    out[...] = value.astype(BF)


def input_body(n_head, n_vectors, need, done, *refs):
    parts, refs = refs[:n_head], refs[n_head:]
    me, rows, grad_hidden, vectors, sums, column_sums, pre_sums, input_grad, vector_rows, terms = refs
    need(*range(n_head), *range(n_head + 1, n_head + 7))
    grad_normed = parts[0][...].astype(F32)
    for part in parts[1:]:
        grad_normed = grad_normed + part[...].astype(F32)
    xhat, spread = norm_parts(rows[...].astype(F32))
    input_grad[...] = (grad_hidden[...] + norm_back(grad_normed * vectors[0:1, :], xhat, spread)).astype(BF)
    done(0)
    columns = column_sums.shape[2]
    terms[...] = jnp.zeros_like(terms)
    terms[0:1, :] = jnp.sum(grad_normed * xhat, axis=0, keepdims=True)
    terms[1:2, :] = jnp.sum(grad_normed, axis=0, keepdims=True)
    terms[2:4, :] = sums[0:2, :]
    terms[6:7, :] = sums[2:3, :]
    terms[8:9, :] = sums[3:4, :]
    for j in range(n_head):
        span = slice(j * columns, (j + 1) * columns)
        for i in range(2):
            terms[4 + i : 5 + i, span] = column_sums[i, j : j + 1, :]
        terms[7:8, span] = pre_sums[j : j + 1, :]
    inner, outer = vector_rows.shape[:2]
    lanes = vectors.shape[1] // (inner * outer)
    vector_rows[...] = jnp.zeros_like(vector_rows)
    for d in range(inner * outer):
        at = me[1] ^ d
        vector_rows[at % inner, at // inner, :, 0:lanes] = terms[:, d * lanes : (d + 1) * lanes].astype(BF)


def adamw_update(weight, first_moment, second_moment, gradient, learn_rate):
    first_new = BETA_FIRST * first_moment + (1.0 - BETA_FIRST) * gradient
    second_new = BETA_SECOND * second_moment + (1.0 - BETA_SECOND) * gradient * gradient
    first_hat = first_new / (1.0 - BETA_FIRST**ADAM_STEP)
    second_hat = second_new / (1.0 - BETA_SECOND**ADAM_STEP)
    weight_new = weight - learn_rate * (
        first_hat / (jnp.sqrt(second_hat) + ADAM_EPSILON) + WEIGHT_DECAY * weight
    )
    return (weight_new, first_new, second_new)


def shard_body(need, done, arrived, shards, squares):
    need(0)
    value = arrived[0].astype(F32)
    for d in range(1, arrived.shape[0]):
        value = value + arrived[d].astype(F32)
    shards[...] = value
    squares[...] = jnp.broadcast_to(jnp.sum(value * value).reshape(1, 1), squares.shape)


def told_body(need, done, *refs):
    parts, (squares, shard, told) = refs[:-3], refs[-3:]
    need(*range(len(parts) + 1))
    value = parts[0][...].astype(F32)
    for part in parts[1:]:
        value = value + part[...].astype(F32)
    table = value[VECTOR_ROWS:]
    shard[...] = table
    here = jnp.sum(table * table).reshape(1, 1) + squares[0:1, 0:1]
    tail = value[MESSAGE_ROWS : MESSAGE_ROWS + 1]
    free = LANES // 4
    gap = jnp.zeros((1, LANES - free), F32)
    spill = [jnp.concatenate([gap, tail[:, q * free : (q + 1) * free]], axis=1) for q in range(3)]
    spill = jnp.concatenate(spill + [jnp.zeros((MESSAGE_ROWS - 3, LANES), F32)], axis=0)
    message = jnp.where(corner_mask(), here, value[:MESSAGE_ROWS] + spill)
    told[...] = jnp.broadcast_to(message[None], told.shape)


def corner_mask():
    row = lax.broadcasted_iota(jnp.int32, (MESSAGE_ROWS, LANES), 0)
    lane = lax.broadcasted_iota(jnp.int32, (MESSAGE_ROWS, LANES), 1)
    return (row == MESSAGE_ROWS - 1) & (lane == LANES - 1)


def update_body(n_head, n_vectors, need, done, *refs):
    need(1)
    me, told, shards, out_shard, down_shard, table_shard = refs[:6]
    params, outs = refs[6:21], refs[21:36]
    norm_out = refs[36]
    n_dp = told.shape[0] // n_head

    def merged(d):
        value = told[d * n_head]
        for j in range(1, n_head):
            value = value + told[d * n_head + j]
        return value

    corner = corner_mask()

    def square(d, total):
        value = merged(d)
        return total + jnp.where(corner, value, value * value)

    total = lax.fori_loop(0, n_dp, square, jnp.zeros((MESSAGE_ROWS, LANES), F32))
    grad_norm = jnp.sqrt(jnp.sum(total).reshape(1, 1))
    norm_out[...] = jnp.broadcast_to(grad_norm, norm_out.shape)
    factor = CLIP_NORM / jnp.maximum(grad_norm, CLIP_NORM)

    def update(at, gradient, rate, pick=...):
        weight, first, second = (ref[pick] for ref in params[3 * at : 3 * at + 3])
        for ref, value in zip(outs[3 * at : 3 * at + 3], adamw_update(weight, first, second, gradient * factor, rate)):
            ref[pick] = value

    for k in range(3):
        update(0, shards[k], RATE_MATRIX, k)
    update(0, shards[4], RATE_MATRIX, 3)
    update(1, out_shard[...], RATE_OUTPUT)
    update(2, down_shard[...], RATE_MATRIX)
    mine, free = merged(me[1]), LANES // 4
    tail = jnp.concatenate([mine[q : q + 1, LANES - free :] for q in range(3)], axis=1)
    mine = jnp.concatenate([mine[:, : LANES - free], tail], axis=0)
    size = params[9].shape[1]
    gradient = jnp.zeros((n_vectors, size), F32)
    for j in range(n_head):
        gradient = jnp.where(me[0] == j, mine[:n_vectors, j * size : (j + 1) * size], gradient)
    update(3, gradient, RATE_VECTOR)
    heads = params[12].shape[0]
    for c in range(table_shard.shape[0] // heads):
        update(4, table_shard[c * heads : (c + 1) * heads, :], RATE_VECTOR, (slice(None), slice(c * LANES, (c + 1) * LANES)))


def exchange(value, axis):
    return lax.all_to_all(value, axis, split_axis=0, concat_axis=0, tiled=True)


def spread_all(value, axis):
    size = lax.axis_size(axis)
    return exchange(jnp.broadcast_to(value[None], (size, *value.shape)), axis)


def swap(values, n_head):
    return [values[0]] + [
        lax.ppermute(values[r], "head", [(i, i ^ r) for i in range(n_head)]) for r in range(1, n_head)
    ]


def struct(shape, dtype):
    return jax.ShapeDtypeStruct(shape, dtype)


def on_device(
    node_rows,
    output_grad,
    weight_in,
    first_in,
    second_in,
    weight_out,
    first_out,
    second_out,
    weight_down,
    first_down,
    second_down,
    vectors,
    first_vectors,
    second_vectors,
    bias_table,
    first_table,
    second_table,
    big_counts,
    small_counts,
    big_distance,
    small_distance,
    big_paths,
    small_paths,
    big_lengths,
    small_lengths,
):
    everyone = ("dp", "head")
    n_dp, n_head = lax.axis_size("dp"), lax.axis_size("head")
    head_index, dp_index = lax.axis_index("head"), lax.axis_index("dp")
    me = head_index.reshape(1).astype(jnp.int32)
    shard_rows, columns = weight_in.shape[1], weight_in.shape[2]
    model = shard_rows * n_dp
    my_rows = node_rows.shape[0]
    group_rows = my_rows * n_head
    heads = columns // HEAD_DIM
    width, narrow = big_distance.shape[1], small_distance.shape[1]
    pairs = small_distance.shape[0] // 2
    table_chunks = bias_table.shape[0] // LANES
    all_chunks = table_chunks * n_dp
    n_vectors, shard_width = vectors.shape
    stacked = shard_rows % 16 == 0
    big_ints = (big_distance, big_paths, big_lengths)
    small_ints = (small_distance, small_paths, small_lengths)
    inner = inner_of(n_dp)
    outer = n_dp // inner
    dp_pairs = lambda k: [(i, i ^ k) for i in range(n_dp)]
    us = jnp.stack([head_index, dp_index]).astype(jnp.int32)
    lanes_used = model // n_dp

    def far_shards(value):
        return [value] + [lax.ppermute(value, "dp", dp_pairs(k)) for k in range(inner, n_dp, inner)]

    def near_shards(values):
        value = jnp.stack(values)
        return [value] + [lax.ppermute(value, "dp", dp_pairs(k)) for k in range(1, inner)]

    def to_head(value, r):
        return lax.ppermute(value, "head", [(i, i ^ r) for i in range(n_head)])

    far = n_head // 2
    near_heads = range(1, far)

    rest_sent = jnp.stack([weight_out.astype(BF).T, weight_in[3].astype(BF), weight_down.astype(BF).T])
    rest_sent, my_table = lax.optimization_barrier((rest_sent, bias_table))
    with jax.named_scope("rest_far"):
        rest_far = far_shards(rest_sent)
    table_sent = my_table.astype(BF).T.reshape(heads, table_chunks, LANES).transpose(1, 0, 2)
    with jax.named_scope("table_all"):
        table_all = spread_all(table_sent, "dp").reshape(all_chunks * heads, LANES)
    given = {0: jnp.stack([node_rows, output_grad])}
    with jax.named_scope("rows_far"):
        given[far] = to_head(given[0], far)
    qkv_sent = weight_in[:3].astype(BF)
    with jax.named_scope("vectors_head"):
        own_vectors = lax.dynamic_update_slice_in_dim(
            jnp.zeros((n_vectors, lanes_used), F32), vectors, head_index * shard_width, 1
        )
        step = far
        while step:
            own_vectors = own_vectors + to_head(own_vectors, step)
            step //= 2
    rest, pieces = own_vectors, []
    for _ in range(PIECES):
        piece = lax.reduce_precision(rest, 8, 7)
        rest = rest - piece
        pieces.append(jnp.pad(piece.astype(BF), ((0, PIECE_ROWS - n_vectors), (0, columns - lanes_used))))
    qkv_sent = jnp.concatenate([qkv_sent.reshape(3 * shard_rows, columns), *pieces])
    table_all, qkv_sent, *rest_far = lax.optimization_barrier((table_all, qkv_sent, *rest_far))
    with jax.named_scope("rest_near"):
        rest_near = near_shards(rest_far)
    with jax.named_scope("qkv_far"):
        qkv_far = far_shards(qkv_sent)

    def pair_bias(part, table, ints):
        rows = width // sum(BIG_QUARTERS) * BIG_QUARTERS[part]
        big_range = struct((heads, width // LANES, rows, LANES), F32)
        return kernel_call(
            lambda *refs: bias_body(part, *refs),
            ([struct((heads, pairs, narrow, LANES), F32)] if part == 0 else []) + [big_range],
            "pair_bias",
            12 if part == 0 else 20,
            (table, *ints),
            [pltpu.VMEM((heads, all_chunks // 2, SUB, LANES), jnp.int32)],
        )

    small_bias, *big_bias = pair_bias(0, table_all, (*small_ints, *big_ints))
    held = lax.optimization_barrier((small_bias, table_all, given[far], *rest_near, *qkv_far))
    (small_bias, table_all, given[far]), held = held[:3], held[3:]
    rest_near, qkv_far = held[:inner], held[inner:]
    weights_rest = jnp.concatenate(rest_near)
    with jax.named_scope("qkv_near"):
        qkv_near = near_shards(qkv_far)
    if not stacked:
        order = jnp.argsort(jnp.array(xor_order(n_dp), jnp.int32) ^ dp_index)
        weights_rest = weights_rest[order].transpose(1, 0, 2, 3).reshape(3, model, columns)
    weights_held = {0: weights_rest}
    with jax.named_scope("rest_far_head"):
        weights_held[far] = to_head(weights_rest, far)
    with jax.named_scope("rows_near"):
        for r in near_heads:
            given[r], given[far + r] = to_head(given[0], r), to_head(given[far], r)
    for part in range(1, BIG_PARTS):
        big_bias += pair_bias(part, table_all, big_ints)
    held = lax.optimization_barrier((big_bias[-1], *qkv_near, *[given[r] for r in range(n_head)]))
    big_bias[-1], qkv_near, given = held[0], held[1 : 1 + inner], held[1 + inner :]
    with jax.named_scope("rest_near_head"):
        for r in near_heads:
            weights_held[r] = to_head(weights_held[0], r)
    weights_attend = jnp.concatenate(qkv_near)
    vector_row, vector_pieces = 3 * shard_rows, ()
    if not stacked:
        weights_attend = weights_attend[order]
        vector_row, vector_pieces = 0, (weights_attend[:, 3 * shard_rows :],)
        weights_attend = weights_attend[:, : 3 * shard_rows].reshape(n_dp, 3, shard_rows, columns)
        weights_attend = weights_attend.transpose(1, 0, 2, 3).reshape(3, model, columns)

    block = struct((my_rows, columns), BF)
    rows_block = struct((my_rows, model), BF)
    normed_one, qkv, big_probs, small_probs, all_vectors, hidden_bias, *mixed = kernel_call(
        lambda *refs: forward_body(n_head, vector_row, *refs),
        [
            struct((group_rows, model), BF),
            struct((3, group_rows, columns), BF),
            struct((heads, width, width), F32),
            struct((heads, pairs, 2 * narrow, 2 * narrow), F32),
            struct((n_vectors, model), F32),
            struct((n_head, columns), F32),
            *[block] * n_head,
        ],
        "attend_forward",
        12,
        (*given, us, big_counts, small_counts, weights_attend, small_bias, *big_bias, *vector_pieces),
        [
            pltpu.VMEM((group_rows, columns), BF),
            pltpu.VMEM((width, heads * width), BF),
            pltpu.VMEM((heads * width, columns), BF),
        ],
        range(n_head, n_head + 3),
        (n_head + 3,) if stacked else (),
        n_head,
    )
    with jax.named_scope("mixed_rows"):
        mixed_rows = swap(mixed, n_head)
    mixed_rows[0], *held = lax.optimization_barrier((mixed_rows[0], *[weights_held[r] for r in range(far + 1)]))
    weights_held.update(enumerate(held))
    with jax.named_scope("rest_near_head"):
        for r in near_heads:
            weights_held[far + r] = to_head(weights_held[far], r)
    weights_rest = [weights_held[r] for r in range(n_head)]

    layer_out, grad_hidden, sums, pre_sums, normed_grad, act_pre, *grad_heads = kernel_call(
        lambda *refs: middle_body(n_head, *refs),
        [
            rows_block,
            struct((my_rows, model), F32),
            struct((4, model), F32),
            struct((n_head, columns), F32),
            struct((2, my_rows, model), BF),
            struct((n_head, my_rows, 2 * parcel_slot(columns)), BF),
            *[block] * n_head,
        ],
        "feed_forward",
        6,
        (*mixed_rows, us, node_rows, output_grad, all_vectors, hidden_bias, *weights_rest),
        (),
        (n_head,),
        range(n_head + 5, 2 * n_head + 5) if stacked else (),
        n_head,
    )
    with jax.named_scope("grad_heads"):
        grad_heads = swap(grad_heads, n_head)
    with jax.named_scope("act_pre"):
        act_pre = exchange(act_pre, "head")
    with jax.named_scope("normed_grad"):
        rows_held = {0: normed_grad}
        for r in (far, *range(1, far)):
            rows_held[r] = lax.ppermute(normed_grad, "head", [(i, i ^ r) for i in range(n_head)])

    small_rows, big_rows, dqkv, column_sums, *rows_sent = kernel_call(
        lambda *refs: backward_body(n_head, *refs),
        [
            struct((pairs * narrow * SUB, LANES), F32),
            struct((width // LANES * width * SUB, LANES), F32),
            struct((3, group_rows, columns), BF),
            struct((2, n_head, columns), F32),
            *[rows_block] * n_head,
        ],
        "attend_backward",
        14,
        (*grad_heads, us, qkv, small_probs, big_probs, weights_attend),
        [
            pltpu.VMEM((group_rows, columns), BF),
            pltpu.VMEM((2, heads * width, width), BF),
            pltpu.VMEM((width, heads * width), BF),
            pltpu.VMEM((3, heads * width, columns), BF),
        ],
        (n_head,),
        (n_head + 4,) if stacked else (),
        n_head,
    )
    small_rows, *arrived = lax.optimization_barrier((small_rows, *[rows_held[r] for r in range(1, far + 1)]))
    rows_held.update(zip(range(1, far + 1), arrived))
    with jax.named_scope("normed_grad"):
        for r in range(1, far):
            rows_held[far + r] = lax.ppermute(rows_held[far], "head", [(i, i ^ r) for i in range(n_head)])
    (weight_grads,) = kernel_call(
        lambda *refs: weight_grads_body(n_head, *refs),
        [struct((n_dp, 6, shard_rows, columns) if stacked else (6, model, columns), BF)],
        "weight_grads",
        6,
        (*given, *mixed, us, act_pre, normed_one, dqkv, *[rows_held[r] for r in range(n_head)]),
        (),
        (2 * n_head,),
    )
    if not stacked:
        weight_grads = weight_grads.reshape(6, n_dp, shard_rows, columns).transpose(1, 0, 2, 3)
    with jax.named_scope("grad_normed_one"):
        rows_back = swap(rows_sent, n_head)
    weight_grads, *rows_back = lax.optimization_barrier((weight_grads, *rows_back))
    with jax.named_scope("weight_grads"):
        weights_arrived = exchange(weight_grads, "dp")
    input_grad, vector_rows = kernel_call(
        lambda *refs: input_body(n_head, n_vectors, *refs),
        [rows_block, struct((inner, outer, VECTOR_ROWS, LANES), BF)],
        "input_grad",
        3,
        (*rows_back, us, node_rows, grad_hidden, all_vectors, sums, column_sums, pre_sums),
        [pltpu.VMEM((VECTOR_ROWS, model), F32)],
        (n_head,),
    )
    table_rows = table_chunks * heads
    block = struct((outer, VECTOR_ROWS + table_rows, LANES), BF)
    inner_sent = kernel_call(
        scatter_body,
        [(inner, block)],
        "table_scatter",
        40,
        (small_rows, *small_ints, big_rows, *big_ints, us, vector_rows),
        [pltpu.VMEM((LANES, all_chunks * heads), F32)],
        (8,),
    )
    with jax.named_scope("table_inner"):
        arrived = [inner_sent[0]] + [lax.ppermute(inner_sent[k], "dp", dp_pairs(k)) for k in range(1, inner)]
    outer_sent = kernel_call(
        merge_body,
        [(outer, struct(block.shape[1:], BF))],
        "merge_table",
        1,
        tuple(arrived),
    )
    weights_arrived, *outer_sent = lax.optimization_barrier((weights_arrived, *outer_sent))
    with jax.named_scope("table_outer"):
        parts = [outer_sent[0]] + [
            lax.ppermute(outer_sent[k], "dp", dp_pairs(k * inner)) for k in range(1, outer)
        ]
    shards, squares = kernel_call(
        shard_body,
        [struct((6, shard_rows, columns), F32), struct((1, LANES), F32)],
        "shard_sums",
        3,
        (weights_arrived,),
    )
    table_shard, told = kernel_call(
        told_body,
        [struct((table_rows, LANES), F32), struct((n_dp * n_head, MESSAGE_ROWS, LANES), F32)],
        "table_sums",
        1,
        (*parts, squares),
    )
    with jax.named_scope("squares"):
        told = exchange(told, everyone)
    params = (weight_in, first_in, second_in, weight_out, first_out, second_out)
    params += (weight_down, first_down, second_down, vectors, first_vectors, second_vectors)
    params += (bias_table.T, first_table.T, second_table.T)
    *updated, grad_norm = kernel_call(
        lambda *refs: update_body(n_head, n_vectors, *refs),
        [*[struct(p.shape, F32) for p in params], struct((1, LANES), F32)],
        "update",
        3,
        (us, told, shards, shards[3].T, shards[5].T, table_shard, *params),
        (),
        (0,),
        ready=range(2, 21),
        limit=16 << 20,
    )
    updated = updated[:12] + [value.T for value in updated[12:]]
    return (layer_out, input_grad, grad_norm[0, 0], *updated)


def solution(mesh):
    rows = P(("dp", "head"), None)
    square = P(None, "dp", "head")
    across = P("head", "dp")
    thin = P(None, ("dp", "head"))
    table = P("dp", "head")
    return jax.shard_map(
        on_device,
        mesh=mesh,
        in_specs=(rows, rows)
        + (square,) * 3
        + (across,) * 6
        + (thin,) * 3
        + (table,) * 3
        + (P("dp"), P("dp", None))
        + (P("dp", None, None),) * 2
        + (P(None, "dp", None, None),) * 2
        + (P("dp", None, None),) * 2,
        out_specs=(rows, rows, P()) + (square,) * 3 + (across,) * 6 + (thin,) * 3 + (table,) * 3,
        check_vma=False,
    )
```

```python
import jax
import jax.numpy as jnp
from jax import lax
from jax.experimental import pallas as pl
from jax.experimental.pallas import tpu as pltpu
from jax.sharding import PartitionSpec as P

HEAD_DIM = 24
NDIST = 512
NTYPE = 1536
STEPS = 5
ADAM_STEP = 10

NORM_EPSILON = 1e-05
NEGATIVE_FILL = -1e30
BETA_FIRST = 0.9
BETA_SECOND = 0.95
ADAM_EPSILON = 1e-08
RATE_MATRIX = 0.02
RATE_OUTPUT = 0.05
RATE_VECTOR = 0.15
WEIGHT_DECAY = 0.01
CLIP_NORM = 1.0

LANES = 128
SUB = 8
FIRST = [0] + [(NDIST + n * NTYPE) // LANES for n in range(STEPS)]
CHUNKS = [NDIST // LANES] + [NTYPE // LANES] * STEPS
LOOKUPS = STEPS + 1
VECTOR_ROWS = 16
BIG_QUARTERS = (1, 3)
BIG_PARTS = len(BIG_QUARTERS)
MESSAGE_ROWS = 8
PIECES = 3
PIECE_ROWS = 16
FIXED = 8192.0
SPLIT = 112
SPLIT_RECIPROCAL, SPLIT_SHIFT = 4682, 19
HIGHS = [-(-(n * LANES) // (2 * SPLIT)) * 2 for n in CHUNKS]
NOWHERE = 4095
SCALE = HEAD_DIM**-0.5
BF = jnp.bfloat16
F32 = jnp.float32
VMEM_BYTES = 56 << 20

NN = (((1,), (0,)), ((), ()))
NT = (((1,), (1,)), ((), ()))
TN = (((0,), (0,)), ((), ()))


def dot(left, right, dims):
    return lax.dot_general(left, right, dims, preferred_element_type=F32)


def inner_of(size):
    return 1 << ((size.bit_length() - 1) // 2)


def xor_order(size):
    inner = inner_of(size)
    return [a * inner + b for b in range(inner) for a in range(size // inner)]


def kernel_call(body, outs, name, micros, args, scratch=(), smem_in=(), placed=(), us_at=None, ready=(), limit=VMEM_BYTES, early=()):
    n_in, n_out = len(args), len(outs)
    moved = [i for i in range(n_in) if i not in smem_in and i not in ready]
    blocks = [out[0] if isinstance(out, tuple) else 0 for out in outs]
    shapes = [out[1] if isinstance(out, tuple) else out for out in outs]
    flat = [(i, k) for i in range(n_out) for k in range(max(blocks[i], 1))]
    n_sems = sum(args[i].shape[0] if i in placed else 1 for i in moved)

    def wrapped(*refs):
        given, results = refs[:n_in], refs[n_in : n_in + len(flat)]
        refs = refs[n_in + len(flat) :]
        held = dict(zip(moved, refs))
        made, refs = refs[len(moved) : len(moved) + n_out], refs[len(moved) + n_out :]
        rest, (in_sems, out_sems) = refs[:-2], refs[-2:]
        arriving, sem = {}, 0
        for i in moved:
            pieces = [(given[i], held[i])]
            if i in placed:
                size = args[i].shape[0]
                pieces = [
                    (given[i].at[k], held[i].at[given[us_at][1] ^ other]) for k, other in enumerate(xor_order(size))
                ]
            arriving[i] = [pltpu.make_async_copy(a, b, in_sems.at[sem + n]) for n, (a, b) in enumerate(pieces)]
            sem += len(pieces)
        leaving = [
            pltpu.make_async_copy(made[i].at[k] if blocks[i] else made[i], results[at], out_sems.at[at])
            for at, (i, k) in enumerate(flat)
        ]
        for i in [*early, *[i for i in moved if i not in early]]:
            for copy in arriving[i]:
                copy.start()
        waiting, unsent = list(moved), list(range(n_out))

        def need(*which):
            for i in which:
                if i in waiting:
                    waiting.remove(i)
                    for copy in arriving[i]:
                        copy.wait()

        def done(*which):
            for i in which:
                if i in unsent:
                    unsent.remove(i)
                    for at, (j, _) in enumerate(flat):
                        if i == j:
                            leaving[at].start()

        body(need, done, *[held.get(i, given[i]) for i in range(n_in)], *made, *rest)
        need(*moved)
        done(*range(n_out))
        for copy in leaving:
            copy.wait()

    anywhere, smem = pl.BlockSpec(memory_space=pl.ANY), pl.BlockSpec(memory_space=pltpu.SMEM)
    vmem = pl.BlockSpec(memory_space=pltpu.VMEM)
    return pl.pallas_call(
        wrapped,
        out_shape=tuple(shapes[i] for i, _ in flat),
        in_specs=[smem if i in smem_in else vmem if i in ready else anywhere for i in range(n_in)],
        out_specs=tuple([anywhere] * len(flat)),
        scratch_shapes=[pltpu.VMEM(args[i].shape, args[i].dtype) for i in moved]
        + [pltpu.VMEM((n, *o.shape) if n else o.shape, o.dtype) for n, o in zip(blocks, shapes)]
        + list(scratch)
        + [pltpu.SemaphoreType.DMA((n_sems,)), pltpu.SemaphoreType.DMA((len(flat),))],
        name=name,
        compiler_params=pltpu.CompilerParams(vmem_limit_bytes=limit),
        cost_estimate=pl.CostEstimate(flops=int(micros * 1e9), bytes_accessed=1 << 20, transcendentals=0),
    )(*args)


def big_block(refs, block, half):
    distance, paths, lengths = refs
    rows, lanes = pl.ds(SUB * block, SUB), slice(LANES * half, LANES * half + LANES)
    return [distance[0, rows, lanes]] + [paths[n, 0, rows, lanes] for n in range(STEPS)], lengths[0, rows, lanes]


def small_block(refs, block, pair):
    distance, paths, lengths = refs
    rows = pl.ds(SUB * block, SUB)

    def two(ref, *lead):
        return jnp.concatenate([ref[(*lead, 2 * pair, rows)], ref[(*lead, 2 * pair + 1, rows)]], axis=1)

    return [two(distance)] + [two(paths, n) for n in range(STEPS)], two(lengths)


def each_block(load, refs, first, count, sides, group, step):
    def some(at, carry):
        blocks = [first + at * group + u for u in range(group)]
        step([(*load(refs, block, side), block, side) for block in blocks for side in range(sides)])
        return carry

    lax.fori_loop(0, count // group, some, 0)


def bias_body(part, need, done, table, *refs):
    small, refs = (refs[:3], refs[3:]) if part == 0 else (None, refs)
    big, outs, words = refs[:3], refs[3:-1], refs[-1]
    need(0)
    heads, count = words.shape[:2]
    for k in range(count):
        low = jnp.round(table[SUB * 2 * k : SUB * (2 * k + 1), :].astype(F32) * FIXED).astype(jnp.int32)
        high = jnp.round(table[SUB * (2 * k + 1) : SUB * (2 * k + 2), :].astype(F32) * FIXED).astype(jnp.int32)
        word = (high << 16) | (low & 0xFFFF)
        for h in range(heads):
            words[h, k] = jnp.broadcast_to(word[h : h + 1], (SUB, LANES))

    def step(store):
        def run(parts):
            for index, lengths, block, side in parts:
                share = (1.0 / FIXED) / lengths.astype(F32)
                first, edges = [None] * heads, [None] * heads
                for t in range(LOOKUPS):
                    code = index[t]
                    lane = code & (LANES - 1)
                    odd = [(code & bit) != 0 for bit in (256, 512, 1024)]
                    shift = ((code >> 3) & 16) ^ 16
                    live = lengths > t - 1
                    for h in range(heads):
                        found = [
                            jnp.take_along_axis(words[h, FIRST[t] // 2 + k], lane, axis=1, mode="promise_in_bounds")
                            for k in range(CHUNKS[t] // 2)
                        ]
                        level = 0
                        while len(found) > 1:
                            found = [
                                jnp.where(odd[level], found[k + 1], found[k]) if k + 1 < len(found) else found[k]
                                for k in range(0, len(found), 2)
                            ]
                            level += 1
                        value = (found[0] << shift) >> 16
                        if t == 0:
                            first[h] = value
                        else:
                            value = jnp.where(live, value, 0)
                            edges[h] = value if edges[h] is None else edges[h] + value
                for h in range(heads):
                    value = first[h].astype(F32) * (1.0 / FIXED) + edges[h].astype(F32) * share
                    store(h, side, block, value)

        return run

    if small:

        def store_small(h, side, block, value):
            outs[0][h, side, pl.ds(SUB * block, SUB), :] = value

        need(1, 2, 3)
        each_block(small_block, small, 0, small[0].shape[1] // SUB, small[0].shape[0] // 2, 1, step(store_small))
        done(0)
    need(*range(1, 7 if small else 4))
    out = outs[-1]
    count = out.shape[2] // SUB
    first_block = big[0].shape[1] // SUB // sum(BIG_QUARTERS) * sum(BIG_QUARTERS[:part])

    def store_big(h, side, block, value):
        out[h, side, pl.ds(SUB * (block - first_block), SUB), :] = value

    each_block(big_block, big, first_block, count, big[0].shape[2] // LANES, 1, step(store_big))


def scatter_body(need, done, small_grads, sd, sp, sl, big_grads, bd, bp, bl, me, vector_rows, parcel, total):
    total[...] = jnp.zeros_like(total)
    sub = lax.broadcasted_iota(jnp.int32, (2 * SUB, LANES), 0)
    low_pattern = [(sub + 2 * SUB * k).astype(F32).astype(BF) for k in range(SPLIT // (2 * SUB))]
    upper = (sub >= SUB).astype(jnp.int32)
    high_pattern = [(2 * k + upper).astype(F32).astype(BF) for k in range(max(HIGHS) // 2)]
    zero, one = jnp.zeros((2 * SUB, LANES), BF), jnp.ones((2 * SUB, LANES), BF)

    def twice(value):
        return jnp.concatenate([value, value], axis=0).astype(BF)

    def step(grads, side_rows):
        def run(parts):
            whole, shared = [], []
            for index, lengths, block, side in parts:
                inverse = 1.0 / lengths.astype(F32)
                for s in range(SUB):
                    g = grads[pl.ds((side * side_rows + SUB * block + s) * SUB, SUB), :]
                    whole.append(twice(g))
                    shared.append(twice(g * jnp.broadcast_to(inverse[s : s + 1], (SUB, LANES))))
            for t in range(LOOKUPS):
                left, right = [], []
                for part, (index, lengths, _, _) in enumerate(parts):
                    high = index[t] * SPLIT_RECIPROCAL >> SPLIT_SHIFT
                    code = (high << 7) | (index[t] - high * SPLIT)
                    if t > 0:
                        code = jnp.where(lengths > t - 1, code, NOWHERE)
                    for s in range(SUB):
                        spread = jnp.broadcast_to(code[s : s + 1], (SUB, LANES))
                        low = twice((spread & (LANES - 1)).astype(F32))
                        high = twice((spread >> 7).astype(F32))
                        source = (whole if t == 0 else shared)[SUB * part + s]
                        left.append(jnp.concatenate([jnp.where(low == p, one, zero) for p in low_pattern], axis=0))
                        right.append(
                            jnp.concatenate(
                                [jnp.where(high == p, source, zero) for p in high_pattern[: HIGHS[t] // 2]], axis=0
                            )
                        )
                span = slice(0, SUB * HIGHS[t])
                total[t, :, span] += dot(jnp.concatenate(left, axis=1), jnp.concatenate(right, axis=1), NT)

        return run

    need(0, 1, 2, 3)
    narrow, width = sd.shape[1], bd.shape[1]
    each_block(small_block, (sd, sp, sl), 0, narrow // SUB, sd.shape[0] // 2, 4, step(small_grads, narrow))
    need(4, 5, 6, 7)
    each_block(big_block, (bd, bp, bl), 0, width // SUB, width // LANES, 4, step(big_grads, width))
    need(9)
    inner, outer, height, _ = parcel.shape
    height -= VECTOR_ROWS
    parcel[:, :, :VECTOR_ROWS, :] = vector_rows[...]
    chunks = []
    for t in range(LOOKUPS):
        rows = total[t, :, 0 : SUB * HIGHS[t]].T
        for c in range(CHUNKS[t]):
            first, last = c * LANES, (c + 1) * LANES
            pieces = []
            for high in range(first // SPLIT, (last - 1) // SPLIT + 1):
                start, end = max(first - high * SPLIT, 0), min(last - high * SPLIT, SPLIT)
                pieces.append(rows[SUB * high : SUB * (high + 1), start:end])
            chunks.append(jnp.concatenate(pieces, axis=1))
    table = jnp.concatenate(chunks, axis=0).astype(BF)
    for d in range(inner * outer):
        at = me[1] ^ d
        parcel[at % inner, at // inner, VECTOR_ROWS:, :] = table[d * height : (d + 1) * height]


def attend_matrix(ref, k, model):
    if ref.shape[1] == model:
        return ref[k]
    rows = model // ref.shape[0]
    return ref[:, k * rows : (k + 1) * rows, :].reshape(model, ref.shape[2])


def whole_matrix(ref, k):
    if len(ref.shape) == 3:
        return ref[k]
    value = ref[:, k]
    return value.reshape(value.shape[0] * value.shape[1], value.shape[2])


def norm_parts(values):
    center = values - jnp.mean(values, axis=-1, keepdims=True)
    spread = lax.rsqrt(jnp.mean(center * center, axis=-1, keepdims=True) + NORM_EPSILON)
    return center * spread, spread


def norm_back(scaled, xhat, spread):
    return spread * (
        scaled
        - jnp.mean(scaled, axis=-1, keepdims=True)
        - xhat * jnp.mean(scaled * xhat, axis=-1, keepdims=True)
    )


def head_lanes(head, width):
    lane = lax.broadcasted_iota(jnp.int32, (1, width), 1)
    return (lane >= head * HEAD_DIM) & (lane < (head + 1) * HEAD_DIM)


def peer_block(me, r, rows):
    return pl.ds(pl.multiple_of((me[0] ^ r) * rows, rows), rows)


def forward_body(n_head, vector_row, need, done, *refs):
    rows_in, refs = refs[:n_head], refs[n_head:]
    me, big_counts, small_counts, weights, small_bias = refs[:5]
    big_bias, refs = refs[5 : 5 + BIG_PARTS], refs[5 + BIG_PARTS :]
    pieces = weights
    if vector_row == 0:
        pieces, refs = refs[0], refs[1:]
    normed, qkv, big_probs, small_probs, vectors, hidden_bias = refs[:6]
    mixed_out, (mixed, flat, stack) = refs[6 : 6 + n_head], refs[6 + n_head :]
    block = rows_in[0].shape[1]
    need(*range(n_head), n_head + 3)
    if vector_row == 0:
        need(n_head + 5 + BIG_PARTS)
    n_vectors, size = vectors.shape[0], vectors.shape[1] // pieces.shape[0]
    for d in range(pieces.shape[0]):
        parts = [pieces[d, pl.ds(vector_row + p * PIECE_ROWS, PIECE_ROWS), 0:size].astype(F32) for p in range(PIECES)]
        vectors[:, d * size : (d + 1) * size] = sum(parts[1:], parts[0])[:n_vectors]
    heads, width = big_probs.shape[:2]
    pairs, wide = small_probs.shape[1:3]
    narrow = wide // 2
    columns = qkv.shape[2]
    halves = width // LANES
    biases = [None] * 2
    for j in range(n_head):
        span = slice(j * columns, (j + 1) * columns)
        hidden_bias[j : j + 1, :] = vectors[7:8, span]
        for i in range(2):
            value = jnp.where(me[0] == j, vectors[4 + i : 5 + i, span], 0.0)
            biases[i] = value if j == 0 else biases[i] + value
    for r in range(n_head):
        xhat, _ = norm_parts(rows_in[r][0].astype(F32))
        normed[peer_block(me, r, block), :] = (xhat * vectors[0:1, :] + vectors[1:2, :]).astype(BF)
    done(0, 4, 5)
    for k in range(3):
        value = dot(normed[...], attend_matrix(weights, k, normed.shape[1]), NN)
        if k != 1:
            value = value + biases[k // 2]
        qkv[k] = value.astype(BF)
    done(1)
    need(*range(n_head + 4, n_head + 5 + BIG_PARTS))
    big_live = lax.broadcasted_iota(jnp.int32, (1, width), 1) < big_counts[0]
    small_live = []
    row = lax.broadcasted_iota(jnp.int32, (wide, wide), 0)
    lane = lax.broadcasted_iota(jnp.int32, (wide, wide), 1)
    for pair in range(pairs):
        first = (row < narrow) & (lane < small_counts[0, 2 * pair])
        second = (row >= narrow) & (lane >= narrow) & (lane < narrow + small_counts[0, 2 * pair + 1])
        small_live.append(first | second)

    def attend(span, extra, live, store):
        for head in range(heads):
            mine = head_lanes(head, columns)
            query = jnp.where(mine, qkv[0, span, :], 0.0)
            size = query.shape[0]
            scores = dot(query, qkv[1, span, :], NT) * SCALE + extra(head)
            scores = jnp.where(live, scores, NEGATIVE_FILL)
            power = jnp.exp(scores - jnp.max(scores, axis=-1, keepdims=True))
            probs = power * (1.0 / jnp.sum(power, axis=-1, keepdims=True))
            store(head, probs)
            rows = slice(head * size, (head + 1) * size)
            flat[:size, rows] = probs.astype(BF)
            stack[rows, :] = jnp.where(mine, qkv[2, span, :], 0.0)
        every = slice(0, heads * size)
        mixed[span, :] = dot(flat[:size, every], stack[every, :], NN).astype(BF)

    def big_extra(head):
        return jnp.concatenate(
            [jnp.concatenate([part[head, half] for part in big_bias], axis=0) for half in range(halves)], axis=1
        )

    def store_big(head, probs):
        big_probs[head] = probs

    attend(slice(0, width), big_extra, big_live, store_big)
    done(2)
    for pair in range(pairs):

        def small_extra(head, pair=pair):
            extra = small_bias[head, pair]
            return jnp.concatenate([extra, extra], axis=0)

        def store_small(head, probs, pair=pair):
            small_probs[head, pair] = probs

        span = slice(width + pair * wide, width + (pair + 1) * wide)
        attend(span, small_extra, small_live[pair], store_small)
    done(3)
    for r in range(n_head):
        mixed_out[r][...] = mixed[peer_block(me, r, block), :]


def put_matrix(ref, k, value):
    if len(ref.shape) == 3:
        ref[k] = value
        return
    rows = ref.shape[2]
    for d in range(ref.shape[0]):
        ref[d, k] = value[d * rows : (d + 1) * rows]


def backward_body(n_head, need, done, *refs):
    need(*range(n_head), n_head + 1, n_head + 2)
    grads_in, refs = refs[:n_head], refs[n_head:]
    me, qkv, small_probs, big_probs, weights, small_rows, big_rows, dqkv, column_sums = refs[:9]
    rows_out, (grad_heads, tall, flat, stacks) = refs[9 : 9 + n_head], refs[9 + n_head :]
    heads, width = big_probs.shape[:2]
    pairs, wide = small_probs.shape[1:3]
    narrow = wide // 2
    columns = qkv.shape[2]
    halves = width // LANES
    block = grads_in[0].shape[0]
    for r in range(n_head):
        grad_heads[peer_block(me, r, block), :] = grads_in[r][...]

    need(n_head + 3)

    def attend(span, all_probs, store):
        for head in range(heads):
            mine = head_lanes(head, columns)
            probs = all_probs(head)
            upper = jnp.where(mine, grad_heads[span, :], 0.0)
            size = upper.shape[0]
            grad_probs = dot(upper, qkv[2, span, :], NT)
            inner = jnp.sum(probs * grad_probs, axis=-1, keepdims=True)
            grad_scores = (probs * (grad_probs - inner)).astype(BF)
            rows = slice(head * size, (head + 1) * size)
            tall[0, rows, :size] = grad_scores
            tall[1, rows, :size] = probs.astype(BF)
            flat[:size, rows] = grad_scores
            stacks[0, rows, :] = jnp.where(mine, qkv[0, span, :], 0.0)
            stacks[1, rows, :] = jnp.where(mine, qkv[1, span, :], 0.0)
            stacks[2, rows, :] = upper
            store(head, grad_scores.astype(F32))
        every = slice(0, heads * size)
        dqkv[0, span, :] = (dot(flat[:size, every], stacks[1, every, :], NN) * SCALE).astype(BF)
        dqkv[1, span, :] = (dot(tall[0, every, :size], stacks[0, every, :], TN) * SCALE).astype(BF)
        dqkv[2, span, :] = dot(tall[1, every, :size], stacks[2, every, :], TN).astype(BF)

    for pair in range(pairs):

        def store_small(head, value, at=pair * narrow * SUB):
            small_rows[pl.ds(at + head, narrow, stride=SUB), :] = value[:narrow] + value[narrow:]

        span = slice(width + pair * wide, width + (pair + 1) * wide)
        attend(span, lambda head, pair=pair: small_probs[head, pair], store_small)
    done(0)

    def store_big(head, value):
        for half in range(halves):
            big_rows[pl.ds(half * width * SUB + head, width, stride=SUB), :] = value[
                :, LANES * half : LANES * (half + 1)
            ]

    attend(slice(0, width), lambda head: big_probs[head], store_big)
    done(1, 2)
    need(n_head + 4)
    column_sums[...] = jnp.zeros_like(column_sums)
    for i, k in enumerate((0, 2)):
        column_sums[i, pl.ds(me[0], 1), :] = jnp.sum(dqkv[k].astype(F32), axis=0, keepdims=True)
    for r in range(n_head):
        rows = peer_block(me, r, block)
        model = rows_out[r].shape[1]
        total = dot(dqkv[0, rows, :], attend_matrix(weights, 0, model), NT)
        total = total + dot(dqkv[1, rows, :], attend_matrix(weights, 1, model), NT)
        total = total + dot(dqkv[2, rows, :], attend_matrix(weights, 2, model), NT)
        rows_out[r][...] = total.astype(BF)


def middle_body(n_head, need, done, *refs):
    mixed, refs = refs[:n_head], refs[n_head:]
    me, rows, upper, vectors, hidden_bias = refs[:5]
    weights, refs = refs[5 : 5 + n_head], refs[5 + n_head :]
    layer_out, grad_hidden, sums, pre_sums, normed_grad, act_pre = refs[:6]
    grad_heads = refs[6:]
    need(*range(n_head + 5))
    columns = mixed[0].shape[1]
    slot = parcel_slot(columns)
    hidden = rows[...].astype(F32) + vectors[6:7, :]
    for r in range(n_head):
        need(n_head + 5 + r)
        hidden = hidden + dot(mixed[r][...], whole_matrix(weights[r], 0), NT)
    xhat, spread = norm_parts(hidden)
    low = (xhat * vectors[2:3, :] + vectors[3:4, :]).astype(BF)
    normed_grad[0] = low
    cotangent = upper[...]
    final = hidden + vectors[8:9, :]
    grad_normed = jnp.zeros_like(hidden)
    for r in range(n_head):
        peer = me[0] ^ r
        into, down = whole_matrix(weights[r], 1), whole_matrix(weights[r], 2)
        pre = dot(low, into, NN) + hidden_bias[pl.ds(peer, 1), :]
        phi = 0.5 * (1.0 + lax.erf(pre * (0.5**0.5)))
        active = (pre * phi).astype(BF)
        final = final + dot(active, down, NT)
        slope = phi + pre * jnp.exp(-0.5 * pre * pre) * (0.5 / jnp.pi) ** 0.5
        low_grad = (dot(cotangent, down, NN) * slope).astype(BF)
        pre_sums[pl.ds(peer, 1), :] = jnp.sum(low_grad.astype(F32), axis=0, keepdims=True)
        grad_normed = grad_normed + dot(low_grad, into, NT)
        act_pre[peer, :, 0:columns] = active
        act_pre[peer, :, slot : slot + columns] = low_grad
    layer_out[...] = final.astype(BF)
    wide = cotangent.astype(F32)
    grad = wide + norm_back(grad_normed * vectors[2:3, :], xhat, spread)
    grad_hidden[...] = grad
    grad_small = grad.astype(BF)
    normed_grad[1] = grad_small
    for r in range(n_head):
        grad_heads[r][...] = dot(grad_small, whole_matrix(weights[r], 0), NN).astype(BF)
    sums[0:1, :] = jnp.sum(grad_normed * xhat, axis=0, keepdims=True)
    sums[1:2, :] = jnp.sum(grad_normed, axis=0, keepdims=True)
    sums[2:3, :] = jnp.sum(grad, axis=0, keepdims=True)
    sums[3:4, :] = jnp.sum(wide, axis=0, keepdims=True)


def parcel_slot(columns):
    return (columns + LANES - 1) // LANES * LANES


def weight_grads_body(n_head, need, done, *refs):
    given, mixed, refs = refs[:n_head], refs[n_head : 2 * n_head], refs[2 * n_head :]
    me, act_pre, normed_one, dqkv = refs[:4]
    normed_grad, out = refs[4 : 4 + n_head], refs[-1]
    columns = mixed[0].shape[1]
    slot = parcel_slot(columns)

    def all_rows(pick):
        return jnp.concatenate([pick(me[0] ^ r) for r in range(n_head)], axis=0)

    need(2 * n_head + 2, 2 * n_head + 3)
    for k in range(3):
        put_matrix(out, k, dot(normed_one[...], dqkv[k], TN).astype(BF))
    need(*range(2 * n_head), 2 * n_head + 1, *range(2 * n_head + 4, 3 * n_head + 4))
    heads_out = jnp.concatenate([m[...] for m in mixed], axis=0)
    put_matrix(out, 3, dot(jnp.concatenate([n[1] for n in normed_grad], axis=0), heads_out, TN).astype(BF))
    grad_pre = all_rows(lambda p: act_pre[p, :, slot : slot + columns])
    put_matrix(out, 4, dot(jnp.concatenate([n[0] for n in normed_grad], axis=0), grad_pre, TN).astype(BF))
    cotangent = jnp.concatenate([g[1] for g in given], axis=0)
    put_matrix(out, 5, dot(cotangent, all_rows(lambda p: act_pre[p, :, 0:columns]), TN).astype(BF))


def merge_body(need, done, *refs):
    parts, out = refs[:-1], refs[-1]
    need(*range(len(parts)))
    value = parts[0][...].astype(F32)
    for part in parts[1:]:
        value = value + part[...].astype(F32)
    out[...] = value.astype(BF)


def input_body(n_head, n_vectors, need, done, *refs):
    parts, refs = refs[:n_head], refs[n_head:]
    me, rows, grad_hidden, vectors, sums, column_sums, pre_sums, input_grad, vector_rows, terms = refs
    need(*range(n_head), *range(n_head + 1, n_head + 7))
    grad_normed = parts[0][...].astype(F32)
    for part in parts[1:]:
        grad_normed = grad_normed + part[...].astype(F32)
    xhat, spread = norm_parts(rows[...].astype(F32))
    input_grad[...] = (grad_hidden[...] + norm_back(grad_normed * vectors[0:1, :], xhat, spread)).astype(BF)
    done(0)
    columns = column_sums.shape[2]
    terms[...] = jnp.zeros_like(terms)
    terms[0:1, :] = jnp.sum(grad_normed * xhat, axis=0, keepdims=True)
    terms[1:2, :] = jnp.sum(grad_normed, axis=0, keepdims=True)
    terms[2:4, :] = sums[0:2, :]
    terms[6:7, :] = sums[2:3, :]
    terms[8:9, :] = sums[3:4, :]
    for j in range(n_head):
        span = slice(j * columns, (j + 1) * columns)
        for i in range(2):
            terms[4 + i : 5 + i, span] = column_sums[i, j : j + 1, :]
        terms[7:8, span] = pre_sums[j : j + 1, :]
    inner, outer = vector_rows.shape[:2]
    lanes = vectors.shape[1] // (inner * outer)
    vector_rows[...] = jnp.zeros_like(vector_rows)
    for d in range(inner * outer):
        at = me[1] ^ d
        vector_rows[at % inner, at // inner, :, 0:lanes] = terms[:, d * lanes : (d + 1) * lanes].astype(BF)


def adamw_update(weight, first_moment, second_moment, gradient, learn_rate):
    first_new = BETA_FIRST * first_moment + (1.0 - BETA_FIRST) * gradient
    second_new = BETA_SECOND * second_moment + (1.0 - BETA_SECOND) * gradient * gradient
    first_hat = first_new / (1.0 - BETA_FIRST**ADAM_STEP)
    second_hat = second_new / (1.0 - BETA_SECOND**ADAM_STEP)
    weight_new = weight - learn_rate * (
        first_hat / (jnp.sqrt(second_hat) + ADAM_EPSILON) + WEIGHT_DECAY * weight
    )
    return (weight_new, first_new, second_new)


def told_body(need, done, arrived, *refs):
    parts, (shards, shard, told) = refs[:-3], refs[-3:]
    need(0)
    rest = arrived[0].astype(F32)
    for d in range(1, arrived.shape[0]):
        rest = rest + arrived[d].astype(F32)
    shards[...] = rest
    done(0)
    need(*range(1, len(parts) + 1))
    value = parts[0][...].astype(F32)
    for part in parts[1:]:
        value = value + part[...].astype(F32)
    table = value[VECTOR_ROWS:]
    shard[...] = table
    here = jnp.sum(table * table).reshape(1, 1) + jnp.sum(rest * rest).reshape(1, 1)
    tail = value[MESSAGE_ROWS : MESSAGE_ROWS + 1]
    free = LANES // 4
    gap = jnp.zeros((1, LANES - free), F32)
    spill = [jnp.concatenate([gap, tail[:, q * free : (q + 1) * free]], axis=1) for q in range(3)]
    spill = jnp.concatenate(spill + [jnp.zeros((MESSAGE_ROWS - 3, LANES), F32)], axis=0)
    message = jnp.where(corner_mask(), here, value[:MESSAGE_ROWS] + spill)
    told[...] = jnp.broadcast_to(message[None], told.shape)


def corner_mask():
    row = lax.broadcasted_iota(jnp.int32, (MESSAGE_ROWS, LANES), 0)
    lane = lax.broadcasted_iota(jnp.int32, (MESSAGE_ROWS, LANES), 1)
    return (row == MESSAGE_ROWS - 1) & (lane == LANES - 1)


def update_body(n_head, n_vectors, need, done, *refs):
    need(1)
    me, told, shards, out_shard, down_shard, table_shard = refs[:6]
    params, outs = refs[6:21], refs[21:36]
    norm_out = refs[36]
    n_dp = told.shape[0] // n_head

    def merged(d):
        value = told[d * n_head]
        for j in range(1, n_head):
            value = value + told[d * n_head + j]
        return value

    corner = corner_mask()

    def square(d, total):
        value = merged(d)
        return total + jnp.where(corner, value, value * value)

    total = lax.fori_loop(0, n_dp, square, jnp.zeros((MESSAGE_ROWS, LANES), F32))
    grad_norm = jnp.sqrt(jnp.sum(total).reshape(1, 1))
    norm_out[...] = jnp.broadcast_to(grad_norm, norm_out.shape)
    factor = CLIP_NORM / jnp.maximum(grad_norm, CLIP_NORM)

    def update(at, gradient, rate, pick=...):
        weight, first, second = (ref[pick] for ref in params[3 * at : 3 * at + 3])
        for ref, value in zip(outs[3 * at : 3 * at + 3], adamw_update(weight, first, second, gradient * factor, rate)):
            ref[pick] = value

    for k in range(3):
        update(0, shards[k], RATE_MATRIX, k)
    update(0, shards[4], RATE_MATRIX, 3)
    update(1, out_shard[...], RATE_OUTPUT)
    update(2, down_shard[...], RATE_MATRIX)
    mine, free = merged(me[1]), LANES // 4
    tail = jnp.concatenate([mine[q : q + 1, LANES - free :] for q in range(3)], axis=1)
    mine = jnp.concatenate([mine[:, : LANES - free], tail], axis=0)
    size = params[9].shape[1]
    gradient = jnp.zeros((n_vectors, size), F32)
    for j in range(n_head):
        gradient = jnp.where(me[0] == j, mine[:n_vectors, j * size : (j + 1) * size], gradient)
    update(3, gradient, RATE_VECTOR)
    heads = params[12].shape[0]
    for c in range(table_shard.shape[0] // heads):
        update(4, table_shard[c * heads : (c + 1) * heads, :], RATE_VECTOR, (slice(None), slice(c * LANES, (c + 1) * LANES)))


def exchange(value, axis):
    return lax.all_to_all(value, axis, split_axis=0, concat_axis=0, tiled=True)


def spread_all(value, axis):
    size = lax.axis_size(axis)
    return exchange(jnp.broadcast_to(value[None], (size, *value.shape)), axis)


def swap(values, n_head):
    return [values[0]] + [
        lax.ppermute(values[r], "head", [(i, i ^ r) for i in range(n_head)]) for r in range(1, n_head)
    ]


def struct(shape, dtype):
    return jax.ShapeDtypeStruct(shape, dtype)


def on_device(
    node_rows,
    output_grad,
    weight_in,
    first_in,
    second_in,
    weight_out,
    first_out,
    second_out,
    weight_down,
    first_down,
    second_down,
    vectors,
    first_vectors,
    second_vectors,
    bias_table,
    first_table,
    second_table,
    big_counts,
    small_counts,
    big_distance,
    small_distance,
    big_paths,
    small_paths,
    big_lengths,
    small_lengths,
):
    everyone = ("dp", "head")
    n_dp, n_head = lax.axis_size("dp"), lax.axis_size("head")
    head_index, dp_index = lax.axis_index("head"), lax.axis_index("dp")
    me = head_index.reshape(1).astype(jnp.int32)
    shard_rows, columns = weight_in.shape[1], weight_in.shape[2]
    model = shard_rows * n_dp
    my_rows = node_rows.shape[0]
    group_rows = my_rows * n_head
    heads = columns // HEAD_DIM
    width, narrow = big_distance.shape[1], small_distance.shape[1]
    pairs = small_distance.shape[0] // 2
    table_chunks = bias_table.shape[0] // LANES
    all_chunks = table_chunks * n_dp
    n_vectors, shard_width = vectors.shape
    stacked = shard_rows % 16 == 0
    big_ints = (big_distance, big_paths, big_lengths)
    small_ints = (small_distance, small_paths, small_lengths)
    inner = inner_of(n_dp)
    outer = n_dp // inner
    dp_pairs = lambda k: [(i, i ^ k) for i in range(n_dp)]
    us = jnp.stack([head_index, dp_index]).astype(jnp.int32)
    lanes_used = model // n_dp

    def far_shards(value):
        return [value] + [lax.ppermute(value, "dp", dp_pairs(k)) for k in range(inner, n_dp, inner)]

    def near_shards(values):
        value = jnp.stack(values)
        return [value] + [lax.ppermute(value, "dp", dp_pairs(k)) for k in range(1, inner)]

    def to_head(value, r):
        return lax.ppermute(value, "head", [(i, i ^ r) for i in range(n_head)])

    far = n_head // 2
    near_heads = range(1, far)

    rest_sent = jnp.stack([weight_out.astype(BF).T, weight_in[3].astype(BF), weight_down.astype(BF).T])
    rest_sent, my_table = lax.optimization_barrier((rest_sent, bias_table))
    with jax.named_scope("rest_far"):
        rest_far = far_shards(rest_sent)
    table_sent = my_table.astype(BF).T.reshape(heads, table_chunks, LANES).transpose(1, 0, 2)
    with jax.named_scope("table_all"):
        table_all = spread_all(table_sent, "dp").reshape(all_chunks * heads, LANES)
    given = {0: jnp.stack([node_rows, output_grad])}
    with jax.named_scope("rows_far"):
        given[far] = to_head(given[0], far)
    qkv_sent = weight_in[:3].astype(BF)
    with jax.named_scope("vectors_head"):
        own_vectors = lax.dynamic_update_slice_in_dim(
            jnp.zeros((n_vectors, lanes_used), F32), vectors, head_index * shard_width, 1
        )
        step = far
        while step:
            own_vectors = own_vectors + to_head(own_vectors, step)
            step //= 2
    rest, pieces = own_vectors, []
    for _ in range(PIECES):
        piece = lax.reduce_precision(rest, 8, 7)
        rest = rest - piece
        pieces.append(jnp.pad(piece.astype(BF), ((0, PIECE_ROWS - n_vectors), (0, columns - lanes_used))))
    qkv_sent = jnp.concatenate([qkv_sent.reshape(3 * shard_rows, columns), *pieces])
    qkv_sent, *rest_far = lax.optimization_barrier((qkv_sent, *rest_far))
    with jax.named_scope("rest_near"):
        rest_near = near_shards(rest_far)
    with jax.named_scope("qkv_far"):
        qkv_far = far_shards(qkv_sent)

    def pair_bias(part, table, ints):
        rows = width // sum(BIG_QUARTERS) * BIG_QUARTERS[part]
        big_range = struct((heads, width // LANES, rows, LANES), F32)
        return kernel_call(
            lambda *refs: bias_body(part, *refs),
            ([struct((heads, pairs, narrow, LANES), F32)] if part == 0 else []) + [big_range],
            "pair_bias",
            12 if part == 0 else 20,
            (table, *ints),
            [pltpu.VMEM((heads, all_chunks // 2, SUB, LANES), jnp.int32)],
        )

    small_bias, *big_bias = pair_bias(0, table_all, (*small_ints, *big_ints))
    held = lax.optimization_barrier((small_bias, table_all, given[far], *rest_near, *qkv_far))
    (small_bias, table_all, given[far]), held = held[:3], held[3:]
    rest_near, qkv_far = held[:inner], held[inner:]
    weights_rest = jnp.concatenate(rest_near)
    with jax.named_scope("qkv_near"):
        qkv_near = near_shards(qkv_far)
    if not stacked:
        order = jnp.argsort(jnp.array(xor_order(n_dp), jnp.int32) ^ dp_index)
        weights_rest = weights_rest[order].transpose(1, 0, 2, 3).reshape(3, model, columns)
    weights_held = {0: weights_rest}
    with jax.named_scope("rest_far_head"):
        weights_held[far] = to_head(weights_rest, far)
    with jax.named_scope("rows_near"):
        for r in near_heads:
            given[r], given[far + r] = to_head(given[0], r), to_head(given[far], r)
    for part in range(1, BIG_PARTS):
        big_bias += pair_bias(part, table_all, big_ints)
    held = lax.optimization_barrier((big_bias[-1], *qkv_near, *[given[r] for r in range(n_head)]))
    big_bias[-1], qkv_near, given = held[0], held[1 : 1 + inner], held[1 + inner :]
    with jax.named_scope("rest_near_head"):
        for r in near_heads:
            weights_held[r] = to_head(weights_held[0], r)
    weights_attend = jnp.concatenate(qkv_near)
    vector_row, vector_pieces = 3 * shard_rows, ()
    if not stacked:
        weights_attend = weights_attend[order]
        vector_row, vector_pieces = 0, (weights_attend[:, 3 * shard_rows :],)
        weights_attend = weights_attend[:, : 3 * shard_rows].reshape(n_dp, 3, shard_rows, columns)
        weights_attend = weights_attend.transpose(1, 0, 2, 3).reshape(3, model, columns)

    block = struct((my_rows, columns), BF)
    rows_block = struct((my_rows, model), BF)
    normed_one, qkv, big_probs, small_probs, all_vectors, hidden_bias, *mixed = kernel_call(
        lambda *refs: forward_body(n_head, vector_row, *refs),
        [
            struct((group_rows, model), BF),
            struct((3, group_rows, columns), BF),
            struct((heads, width, width), F32),
            struct((heads, pairs, 2 * narrow, 2 * narrow), F32),
            struct((n_vectors, model), F32),
            struct((n_head, columns), F32),
            *[block] * n_head,
        ],
        "attend_forward",
        12,
        (*given, us, big_counts, small_counts, weights_attend, small_bias, *big_bias, *vector_pieces),
        [
            pltpu.VMEM((group_rows, columns), BF),
            pltpu.VMEM((width, heads * width), BF),
            pltpu.VMEM((heads * width, columns), BF),
        ],
        range(n_head, n_head + 3),
        (n_head + 3,) if stacked else (),
        n_head,
    )
    with jax.named_scope("mixed_rows"):
        mixed_rows = swap(mixed, n_head)
    mixed_rows[0], *held = lax.optimization_barrier((mixed_rows[0], *[weights_held[r] for r in range(far + 1)]))
    weights_held.update(enumerate(held))
    with jax.named_scope("rest_near_head"):
        for r in near_heads:
            weights_held[far + r] = to_head(weights_held[far], r)
    weights_rest = [weights_held[r] for r in range(n_head)]

    layer_out, grad_hidden, sums, pre_sums, normed_grad, act_pre, *grad_heads = kernel_call(
        lambda *refs: middle_body(n_head, *refs),
        [
            rows_block,
            struct((my_rows, model), F32),
            struct((4, model), F32),
            struct((n_head, columns), F32),
            struct((2, my_rows, model), BF),
            struct((n_head, my_rows, 2 * parcel_slot(columns)), BF),
            *[block] * n_head,
        ],
        "feed_forward",
        6,
        (*mixed_rows, us, node_rows, output_grad, all_vectors, hidden_bias, *weights_rest),
        (),
        (n_head,),
        range(n_head + 5, 2 * n_head + 5) if stacked else (),
        n_head,
    )
    with jax.named_scope("grad_heads"):
        grad_heads = swap(grad_heads, n_head)
    with jax.named_scope("act_pre"):
        act_pre = exchange(act_pre, "head")
    with jax.named_scope("normed_grad"):
        rows_held = {0: normed_grad}
        for r in (far, *range(1, far)):
            rows_held[r] = lax.ppermute(normed_grad, "head", [(i, i ^ r) for i in range(n_head)])

    small_rows, big_rows, dqkv, column_sums, *rows_sent = kernel_call(
        lambda *refs: backward_body(n_head, *refs),
        [
            struct((pairs * narrow * SUB, LANES), F32),
            struct((width // LANES * width * SUB, LANES), F32),
            struct((3, group_rows, columns), BF),
            struct((2, n_head, columns), F32),
            *[rows_block] * n_head,
        ],
        "attend_backward",
        14,
        (*grad_heads, us, qkv, small_probs, big_probs, weights_attend),
        [
            pltpu.VMEM((group_rows, columns), BF),
            pltpu.VMEM((2, heads * width, width), BF),
            pltpu.VMEM((width, heads * width), BF),
            pltpu.VMEM((3, heads * width, columns), BF),
        ],
        (n_head,),
        (n_head + 4,) if stacked else (),
        n_head,
    )
    small_rows, *arrived = lax.optimization_barrier((small_rows, *[rows_held[r] for r in range(1, far + 1)]))
    rows_held.update(zip(range(1, far + 1), arrived))
    with jax.named_scope("normed_grad"):
        for r in range(1, far):
            rows_held[far + r] = lax.ppermute(rows_held[far], "head", [(i, i ^ r) for i in range(n_head)])
    (weight_grads,) = kernel_call(
        lambda *refs: weight_grads_body(n_head, *refs),
        [struct((n_dp, 6, shard_rows, columns) if stacked else (6, model, columns), BF)],
        "weight_grads",
        6,
        (*given, *mixed, us, act_pre, normed_one, dqkv, *[rows_held[r] for r in range(n_head)]),
        (),
        (2 * n_head,),
        early=(2 * n_head + 2, 2 * n_head + 3),
    )
    if not stacked:
        weight_grads = weight_grads.reshape(6, n_dp, shard_rows, columns).transpose(1, 0, 2, 3)
    with jax.named_scope("grad_normed_one"):
        rows_back = swap(rows_sent, n_head)
    weight_grads, *rows_back = lax.optimization_barrier((weight_grads, *rows_back))
    with jax.named_scope("weight_grads"):
        weights_arrived = exchange(weight_grads, "dp")
    input_grad, vector_rows = kernel_call(
        lambda *refs: input_body(n_head, n_vectors, *refs),
        [rows_block, struct((inner, outer, VECTOR_ROWS, LANES), BF)],
        "input_grad",
        3,
        (*rows_back, us, node_rows, grad_hidden, all_vectors, sums, column_sums, pre_sums),
        [pltpu.VMEM((VECTOR_ROWS, model), F32)],
        (n_head,),
    )
    table_rows = table_chunks * heads
    block = struct((outer, VECTOR_ROWS + table_rows, LANES), BF)
    inner_sent = kernel_call(
        scatter_body,
        [(inner, block)],
        "table_scatter",
        40,
        (small_rows, *small_ints, big_rows, *big_ints, us, vector_rows),
        [pltpu.VMEM((LOOKUPS, SPLIT, SUB * max(HIGHS)), F32)],
        (8,),
    )
    with jax.named_scope("table_inner"):
        arrived = [inner_sent[0]] + [lax.ppermute(inner_sent[k], "dp", dp_pairs(k)) for k in range(1, inner)]
    outer_sent = kernel_call(
        merge_body,
        [(outer, struct(block.shape[1:], BF))],
        "merge_table",
        1,
        tuple(arrived),
    )
    with jax.named_scope("table_outer"):
        parts = [outer_sent[0]] + [
            lax.ppermute(outer_sent[k], "dp", dp_pairs(k * inner)) for k in range(1, outer)
        ]
    weights_arrived, *parts = lax.optimization_barrier((weights_arrived, *parts))
    shards, table_shard, told = kernel_call(
        told_body,
        [
            struct((6, shard_rows, columns), F32),
            struct((table_rows, LANES), F32),
            struct((n_dp * n_head, MESSAGE_ROWS, LANES), F32),
        ],
        "shard_sums",
        4,
        (weights_arrived, *parts),
    )
    with jax.named_scope("squares"):
        told = exchange(told, everyone)
    params = (weight_in, first_in, second_in, weight_out, first_out, second_out)
    params += (weight_down, first_down, second_down, vectors, first_vectors, second_vectors)
    params += (bias_table.T, first_table.T, second_table.T)
    *updated, grad_norm = kernel_call(
        lambda *refs: update_body(n_head, n_vectors, *refs),
        [*[struct(p.shape, F32) for p in params], struct((1, LANES), F32)],
        "update",
        3,
        (us, told, shards, shards[3].T, shards[5].T, table_shard, *params),
        (),
        (0,),
        ready=range(2, 21),
        limit=16 << 20,
    )
    updated = updated[:12] + [value.T for value in updated[12:]]
    return (layer_out, input_grad, grad_norm[0, 0], *updated)


def solution(mesh):
    rows = P(("dp", "head"), None)
    square = P(None, "dp", "head")
    across = P("head", "dp")
    thin = P(None, ("dp", "head"))
    table = P("dp", "head")
    return jax.shard_map(
        on_device,
        mesh=mesh,
        in_specs=(rows, rows)
        + (square,) * 3
        + (across,) * 6
        + (thin,) * 3
        + (table,) * 3
        + (P("dp"), P("dp", None))
        + (P("dp", None, None),) * 2
        + (P(None, "dp", None, None),) * 2
        + (P("dp", None, None),) * 2,
        out_specs=(rows, rows, P()) + (square,) * 3 + (across,) * 6 + (thin,) * 3 + (table,) * 3,
        check_vma=False,
    )
```

```python
import jax
import jax.numpy as jnp
from jax import lax
from jax.experimental import pallas as pl
from jax.experimental.pallas import tpu as pltpu
from jax.sharding import PartitionSpec as P

HEAD_DIM = 24
NDIST = 512
NTYPE = 1536
STEPS = 5
ADAM_STEP = 10

NORM_EPSILON = 1e-05
NEGATIVE_FILL = -1e30
BETA_FIRST = 0.9
BETA_SECOND = 0.95
ADAM_EPSILON = 1e-08
RATE_MATRIX = 0.02
RATE_OUTPUT = 0.05
RATE_VECTOR = 0.15
WEIGHT_DECAY = 0.01
CLIP_NORM = 1.0

LANES = 128
SUB = 8
FIRST = [0] + [(NDIST + n * NTYPE) // LANES for n in range(STEPS)]
CHUNKS = [NDIST // LANES] + [NTYPE // LANES] * STEPS
LOOKUPS = STEPS + 1
VECTOR_ROWS = 16
BIG_QUARTERS = (1, 3)
BIG_PARTS = len(BIG_QUARTERS)
MESSAGE_ROWS = 8
PRODUCTS = (STEPS - 1, STEPS)
PIECES = 3
PIECE_ROWS = 16
FIXED = 8192.0
SPLIT = 112
SPLIT_RECIPROCAL, SPLIT_SHIFT = 4682, 19
HIGHS = [-(-(n * LANES) // (2 * SPLIT)) * 2 for n in CHUNKS]
NOWHERE = 4095
SCALE = HEAD_DIM**-0.5
BF = jnp.bfloat16
F32 = jnp.float32
VMEM_BYTES = 56 << 20

NN = (((1,), (0,)), ((), ()))
NT = (((1,), (1,)), ((), ()))
TN = (((0,), (0,)), ((), ()))


def dot(left, right, dims):
    return lax.dot_general(left, right, dims, preferred_element_type=F32)


def inner_of(size):
    return 1 << ((size.bit_length() - 1) // 2)


def xor_order(size):
    inner = inner_of(size)
    return [a * inner + b for b in range(inner) for a in range(size // inner)]


def kernel_call(body, outs, name, micros, args, scratch=(), smem_in=(), placed=(), us_at=None, ready=(), limit=VMEM_BYTES, early=()):
    groups = [arg if isinstance(arg, list) else [arg] for arg in args]
    args = [struct((sum(a.shape[0] for a in g), *g[0].shape[1:]), g[0].dtype) if len(g) > 1 else g[0] for g in groups]
    starts = [sum(len(g) for g in groups[:i]) for i in range(len(groups) + 1)]
    n_in, n_out = len(args), len(outs)
    moved = [i for i in range(n_in) if i not in smem_in and i not in ready]
    blocks = [out[0] if isinstance(out, tuple) else 0 for out in outs]
    shapes = [out[1] if isinstance(out, tuple) else out for out in outs]
    flat = [(i, k) for i in range(n_out) for k in range(max(blocks[i], 1))]
    n_sems = sum(args[i].shape[0] if i in placed else 1 for i in moved)

    def wrapped(*refs):
        parts = [refs[starts[i] : starts[i + 1]] for i in range(n_in)]
        given, results = [p[0] for p in parts], refs[starts[-1] : starts[-1] + len(flat)]
        refs = refs[starts[-1] + len(flat) :]
        held = dict(zip(moved, refs))
        made, refs = refs[len(moved) : len(moved) + n_out], refs[len(moved) + n_out :]
        rest, (in_sems, out_sems) = refs[:-2], refs[-2:]
        arriving, sem = {}, 0
        for i in moved:
            pieces = [(given[i], held[i])]
            if i in placed:
                size = args[i].shape[0]
                each = size // len(parts[i])
                pieces = [
                    (parts[i][k // each].at[k % each], held[i].at[given[us_at][1] ^ other])
                    for k, other in enumerate(xor_order(size))
                ]
            arriving[i] = [pltpu.make_async_copy(a, b, in_sems.at[sem + n]) for n, (a, b) in enumerate(pieces)]
            sem += len(pieces)
        leaving = [
            pltpu.make_async_copy(made[i].at[k] if blocks[i] else made[i], results[at], out_sems.at[at])
            for at, (i, k) in enumerate(flat)
        ]
        for i in [*early, *[i for i in moved if i not in early]]:
            for copy in arriving[i]:
                copy.start()
        waiting, unsent = list(moved), list(range(n_out))

        def need(*which):
            for i in which:
                if i in waiting:
                    waiting.remove(i)
                    for copy in arriving[i]:
                        copy.wait()

        def done(*which):
            for i in which:
                if i in unsent:
                    unsent.remove(i)
                    for at, (j, _) in enumerate(flat):
                        if i == j:
                            leaving[at].start()

        body(need, done, *[held.get(i, given[i]) for i in range(n_in)], *made, *rest)
        need(*moved)
        done(*range(n_out))
        for copy in leaving:
            copy.wait()

    anywhere, smem = pl.BlockSpec(memory_space=pl.ANY), pl.BlockSpec(memory_space=pltpu.SMEM)
    vmem = pl.BlockSpec(memory_space=pltpu.VMEM)
    return pl.pallas_call(
        wrapped,
        out_shape=tuple(shapes[i] for i, _ in flat),
        in_specs=[
            smem if i in smem_in else vmem if i in ready else anywhere for i in range(n_in) for _ in groups[i]
        ],
        out_specs=tuple([anywhere] * len(flat)),
        scratch_shapes=[pltpu.VMEM(args[i].shape, args[i].dtype) for i in moved]
        + [pltpu.VMEM((n, *o.shape) if n else o.shape, o.dtype) for n, o in zip(blocks, shapes)]
        + list(scratch)
        + [pltpu.SemaphoreType.DMA((n_sems,)), pltpu.SemaphoreType.DMA((len(flat),))],
        name=name,
        compiler_params=pltpu.CompilerParams(vmem_limit_bytes=limit),
        cost_estimate=pl.CostEstimate(flops=int(micros * 1e9), bytes_accessed=1 << 20, transcendentals=0),
    )(*[part for group in groups for part in group])


def big_block(refs, block, half):
    distance, paths, lengths = refs
    rows, lanes = pl.ds(SUB * block, SUB), slice(LANES * half, LANES * half + LANES)
    return [distance[0, rows, lanes]] + [paths[n, 0, rows, lanes] for n in range(STEPS)], lengths[0, rows, lanes]


def small_block(refs, block, pair):
    distance, paths, lengths = refs
    rows = pl.ds(SUB * block, SUB)

    def two(ref, *lead):
        return jnp.concatenate([ref[(*lead, 2 * pair, rows)], ref[(*lead, 2 * pair + 1, rows)]], axis=1)

    return [two(distance)] + [two(paths, n) for n in range(STEPS)], two(lengths)


def each_block(load, refs, first, count, sides, group, step):
    def some(at, carry):
        blocks = [first + at * group + u for u in range(group)]
        step([(*load(refs, block, side), block, side) for block in blocks for side in range(sides)])
        return carry

    lax.fori_loop(0, count // group, some, 0)


def pick(items, high):
    bit = 1
    while len(items) > 1:
        odd = (high & bit) != 0
        items = [
            jnp.where(odd, items[k + 1], items[k]) if k + 1 < len(items) else items[k]
            for k in range(0, len(items), 2)
        ]
        bit *= 2
    return items[0]


def bias_body(part, need, done, table, *refs):
    small, refs = (refs[:3], refs[3:]) if part == 0 else (None, refs)
    big, outs, (words, rows_of, found_rows) = refs[:3], refs[3:-3], refs[-3:]
    need(0)
    heads, count = words.shape[:2]
    for k in range(count):
        low = jnp.round(table[SUB * 2 * k : SUB * (2 * k + 1), :].astype(F32) * FIXED).astype(jnp.int32)
        high = jnp.round(table[SUB * (2 * k + 1) : SUB * (2 * k + 2), :].astype(F32) * FIXED).astype(jnp.int32)
        word = (high << 16) | (low & 0xFFFF)
        for h in range(heads):
            words[h, k] = jnp.broadcast_to(word[h : h + 1], (SUB, LANES))

    for i, t in enumerate(PRODUCTS):
        chunk = [table[SUB * c : SUB * (c + 1), :].astype(F32) for c in range(FIRST[t], FIRST[t] + CHUNKS[t])]
        pairs_of = [jnp.concatenate(chunk[c : c + 2], axis=1) for c in range(0, CHUNKS[t], 2)]
        rows_of[i] = jnp.concatenate(pairs_of, axis=0).astype(BF)
    sub = lax.broadcasted_iota(jnp.int32, (2 * SUB, LANES), 0)
    patterns = [(sub + 2 * SUB * k).astype(F32).astype(BF) for k in range(LANES // SUB)]
    zero, one = jnp.zeros((2 * SUB, LANES), BF), jnp.ones((2 * SUB, LANES), BF)

    def product(i, code):
        spread = [jnp.broadcast_to(code[s : s + 1], (SUB, LANES)) for s in range(SUB)]
        hot = []
        for s in range(SUB):
            low = (spread[s] & (2 * LANES - 1)).astype(F32)
            low = jnp.concatenate([low, low], axis=0).astype(BF)
            hot.append(jnp.concatenate([jnp.where(low == p, one, zero) for p in patterns], axis=0))
        values = dot(rows_of[i], jnp.concatenate(hot, axis=1), NN)
        for s in range(SUB):
            lanes = slice(LANES * s, LANES * (s + 1))
            items = [values[heads * c : heads * (c + 1), lanes] for c in range(values.shape[0] // heads)]
            found_rows[i, pl.ds(s, heads, stride=SUB), :] = pick(items, spread[s] >> 8)

    def step(store):
        def run(parts):
            for index, lengths, block, side in parts:
                share = 1.0 / lengths.astype(F32)
                first, edges = [None] * heads, [None] * heads
                for i, t in enumerate(PRODUCTS):
                    product(i, index[t])
                for t in range(LOOKUPS):
                    if t in PRODUCTS:
                        continue
                    code = index[t]
                    lane = code & (LANES - 1)
                    odd = [(code & bit) != 0 for bit in (256, 512, 1024)]
                    shift = ((code >> 3) & 16) ^ 16
                    live = lengths > t - 1
                    for h in range(heads):
                        found = [
                            jnp.take_along_axis(words[h, FIRST[t] // 2 + k], lane, axis=1, mode="promise_in_bounds")
                            for k in range(CHUNKS[t] // 2)
                        ]
                        level = 0
                        while len(found) > 1:
                            found = [
                                jnp.where(odd[level], found[k + 1], found[k]) if k + 1 < len(found) else found[k]
                                for k in range(0, len(found), 2)
                            ]
                            level += 1
                        value = (found[0] << shift) >> 16
                        if t == 0:
                            first[h] = value
                        else:
                            value = jnp.where(live, value, 0)
                            edges[h] = value if edges[h] is None else edges[h] + value
                for h in range(heads):
                    edge = edges[h].astype(F32) * (1.0 / FIXED)
                    for i, t in enumerate(PRODUCTS):
                        edge = edge + jnp.where(lengths > t - 1, found_rows[i, SUB * h : SUB * (h + 1), :], 0.0)
                    store(h, side, block, first[h].astype(F32) * (1.0 / FIXED) + edge * share)

        return run

    if small:

        def store_small(h, side, block, value):
            outs[0][h, side, pl.ds(SUB * block, SUB), :] = value

        need(1, 2, 3)
        each_block(small_block, small, 0, small[0].shape[1] // SUB, small[0].shape[0] // 2, 1, step(store_small))
        done(0)
    need(*range(1, 7 if small else 4))
    out = outs[-1]
    count = out.shape[2] // SUB
    first_block = big[0].shape[1] // SUB // sum(BIG_QUARTERS) * sum(BIG_QUARTERS[:part])

    def store_big(h, side, block, value):
        out[h, side, pl.ds(SUB * (block - first_block), SUB), :] = value

    each_block(big_block, big, first_block, count, big[0].shape[2] // LANES, 1, step(store_big))


def scatter_body(need, done, small_grads, sd, sp, sl, big_grads, bd, bp, bl, me, vector_rows, parcel, total):
    total[...] = jnp.zeros_like(total)
    sub = lax.broadcasted_iota(jnp.int32, (2 * SUB, LANES), 0)
    low_pattern = [(sub + 2 * SUB * k).astype(F32).astype(BF) for k in range(SPLIT // (2 * SUB))]
    upper = (sub >= SUB).astype(jnp.int32)
    high_pattern = [(2 * k + upper).astype(F32).astype(BF) for k in range(max(HIGHS) // 2)]
    zero, one = jnp.zeros((2 * SUB, LANES), BF), jnp.ones((2 * SUB, LANES), BF)

    def twice(value):
        return jnp.concatenate([value, value], axis=0).astype(BF)

    def step(grads, side_rows):
        def run(parts):
            whole, shared = [], []
            for index, lengths, block, side in parts:
                inverse = 1.0 / lengths.astype(F32)
                for s in range(SUB):
                    g = grads[pl.ds((side * side_rows + SUB * block + s) * SUB, SUB), :]
                    whole.append(twice(g))
                    shared.append(twice(g * jnp.broadcast_to(inverse[s : s + 1], (SUB, LANES))))
            for t in range(LOOKUPS):
                left, right = [], []
                for part, (index, lengths, _, _) in enumerate(parts):
                    high = index[t] * SPLIT_RECIPROCAL >> SPLIT_SHIFT
                    code = (high << 7) | (index[t] - high * SPLIT)
                    if t > 0:
                        code = jnp.where(lengths > t - 1, code, NOWHERE)
                    for s in range(SUB):
                        spread = jnp.broadcast_to(code[s : s + 1], (SUB, LANES))
                        low = twice((spread & (LANES - 1)).astype(F32))
                        high = twice((spread >> 7).astype(F32))
                        source = (whole if t == 0 else shared)[SUB * part + s]
                        left.append(jnp.concatenate([jnp.where(low == p, one, zero) for p in low_pattern], axis=0))
                        right.append(
                            jnp.concatenate(
                                [jnp.where(high == p, source, zero) for p in high_pattern[: HIGHS[t] // 2]], axis=0
                            )
                        )
                span = slice(0, SUB * HIGHS[t])
                total[t, :, span] += dot(jnp.concatenate(left, axis=1), jnp.concatenate(right, axis=1), NT)

        return run

    need(0, 1, 2, 3)
    narrow, width = sd.shape[1], bd.shape[1]
    each_block(small_block, (sd, sp, sl), 0, narrow // SUB, sd.shape[0] // 2, 4, step(small_grads, narrow))
    need(4, 5, 6, 7)
    each_block(big_block, (bd, bp, bl), 0, width // SUB, width // LANES, 4, step(big_grads, width))
    need(9)
    inner, outer, height, _ = parcel.shape
    height -= VECTOR_ROWS
    parcel[:, :, :VECTOR_ROWS, :] = vector_rows[...]
    chunks = []
    for t in range(LOOKUPS):
        rows = total[t, :, 0 : SUB * HIGHS[t]].T
        for c in range(CHUNKS[t]):
            first, last = c * LANES, (c + 1) * LANES
            pieces = []
            for high in range(first // SPLIT, (last - 1) // SPLIT + 1):
                start, end = max(first - high * SPLIT, 0), min(last - high * SPLIT, SPLIT)
                pieces.append(rows[SUB * high : SUB * (high + 1), start:end])
            chunks.append(jnp.concatenate(pieces, axis=1))
    table = jnp.concatenate(chunks, axis=0).astype(BF)
    for d in range(inner * outer):
        at = me[1] ^ d
        parcel[at % inner, at // inner, VECTOR_ROWS:, :] = table[d * height : (d + 1) * height]


def attend_matrix(ref, k, model):
    if ref.shape[1] == model:
        return ref[k]
    rows = model // ref.shape[0]
    return ref[:, k * rows : (k + 1) * rows, :].reshape(model, ref.shape[2])


def whole_matrix(ref, k):
    if len(ref.shape) == 3:
        return ref[k]
    value = ref[:, k]
    return value.reshape(value.shape[0] * value.shape[1], value.shape[2])


def norm_parts(values):
    center = values - jnp.mean(values, axis=-1, keepdims=True)
    spread = lax.rsqrt(jnp.mean(center * center, axis=-1, keepdims=True) + NORM_EPSILON)
    return center * spread, spread


def norm_back(scaled, xhat, spread):
    return spread * (
        scaled
        - jnp.mean(scaled, axis=-1, keepdims=True)
        - xhat * jnp.mean(scaled * xhat, axis=-1, keepdims=True)
    )


def head_lanes(head, width):
    lane = lax.broadcasted_iota(jnp.int32, (1, width), 1)
    return (lane >= head * HEAD_DIM) & (lane < (head + 1) * HEAD_DIM)


def peer_block(me, r, rows):
    return pl.ds(pl.multiple_of((me[0] ^ r) * rows, rows), rows)


def forward_body(n_head, vector_row, need, done, *refs):
    rows_in, refs = refs[:n_head], refs[n_head:]
    me, big_counts, small_counts, weights, small_bias = refs[:5]
    big_bias, refs = refs[5 : 5 + BIG_PARTS], refs[5 + BIG_PARTS :]
    pieces = weights
    if vector_row == 0:
        pieces, refs = refs[0], refs[1:]
    normed, qkv, big_probs, small_probs, vectors, hidden_bias = refs[:6]
    mixed_out, (mixed, flat, stack) = refs[6 : 6 + n_head], refs[6 + n_head :]
    block = rows_in[0].shape[1]
    need(*range(n_head), n_head + 3)
    if vector_row == 0:
        need(n_head + 5 + BIG_PARTS)
    n_vectors, size = vectors.shape[0], vectors.shape[1] // pieces.shape[0]
    for d in range(pieces.shape[0]):
        parts = [pieces[d, pl.ds(vector_row + p * PIECE_ROWS, PIECE_ROWS), 0:size].astype(F32) for p in range(PIECES)]
        vectors[:, d * size : (d + 1) * size] = sum(parts[1:], parts[0])[:n_vectors]
    heads, width = big_probs.shape[:2]
    pairs, wide = small_probs.shape[1:3]
    narrow = wide // 2
    columns = qkv.shape[2]
    halves = width // LANES
    biases = [None] * 2
    for j in range(n_head):
        span = slice(j * columns, (j + 1) * columns)
        hidden_bias[j : j + 1, :] = vectors[7:8, span]
        for i in range(2):
            value = jnp.where(me[0] == j, vectors[4 + i : 5 + i, span], 0.0)
            biases[i] = value if j == 0 else biases[i] + value
    for r in range(n_head):
        xhat, _ = norm_parts(rows_in[r][0].astype(F32))
        normed[peer_block(me, r, block), :] = (xhat * vectors[0:1, :] + vectors[1:2, :]).astype(BF)
    done(0, 4, 5)
    for k in range(3):
        value = dot(normed[...], attend_matrix(weights, k, normed.shape[1]), NN)
        if k != 1:
            value = value + biases[k // 2]
        qkv[k] = value.astype(BF)
    done(1)
    need(*range(n_head + 4, n_head + 5 + BIG_PARTS))
    big_live = lax.broadcasted_iota(jnp.int32, (1, width), 1) < big_counts[0]
    small_live = []
    row = lax.broadcasted_iota(jnp.int32, (wide, wide), 0)
    lane = lax.broadcasted_iota(jnp.int32, (wide, wide), 1)
    for pair in range(pairs):
        first = (row < narrow) & (lane < small_counts[0, 2 * pair])
        second = (row >= narrow) & (lane >= narrow) & (lane < narrow + small_counts[0, 2 * pair + 1])
        small_live.append(first | second)

    def attend(span, extra, live, store):
        for head in range(heads):
            mine = head_lanes(head, columns)
            query = jnp.where(mine, qkv[0, span, :], 0.0)
            size = query.shape[0]
            scores = dot(query, qkv[1, span, :], NT) * SCALE + extra(head)
            scores = jnp.where(live, scores, NEGATIVE_FILL)
            power = jnp.exp(scores - jnp.max(scores, axis=-1, keepdims=True))
            probs = power * (1.0 / jnp.sum(power, axis=-1, keepdims=True))
            store(head, probs)
            rows = slice(head * size, (head + 1) * size)
            flat[:size, rows] = probs.astype(BF)
            stack[rows, :] = jnp.where(mine, qkv[2, span, :], 0.0)
        every = slice(0, heads * size)
        mixed[span, :] = dot(flat[:size, every], stack[every, :], NN).astype(BF)

    def big_extra(head):
        return jnp.concatenate(
            [jnp.concatenate([part[head, half] for part in big_bias], axis=0) for half in range(halves)], axis=1
        )

    def store_big(head, probs):
        big_probs[head] = probs

    attend(slice(0, width), big_extra, big_live, store_big)
    done(2)
    for pair in range(pairs):

        def small_extra(head, pair=pair):
            extra = small_bias[head, pair]
            return jnp.concatenate([extra, extra], axis=0)

        def store_small(head, probs, pair=pair):
            small_probs[head, pair] = probs

        span = slice(width + pair * wide, width + (pair + 1) * wide)
        attend(span, small_extra, small_live[pair], store_small)
    done(3)
    for r in range(n_head):
        mixed_out[r][...] = mixed[peer_block(me, r, block), :]


def put_matrix(ref, k, value):
    if len(ref.shape) == 3:
        ref[k] = value
        return
    rows = ref.shape[2]
    for d in range(ref.shape[0]):
        ref[d, k] = value[d * rows : (d + 1) * rows]


def backward_body(n_head, need, done, *refs):
    need(*range(n_head), n_head + 1, n_head + 2)
    grads_in, refs = refs[:n_head], refs[n_head:]
    me, qkv, small_probs, big_probs, weights, small_rows, big_rows, dqkv, column_sums = refs[:9]
    rows_out, (grad_heads, tall, flat, stacks) = refs[9 : 9 + n_head], refs[9 + n_head :]
    heads, width = big_probs.shape[:2]
    pairs, wide = small_probs.shape[1:3]
    narrow = wide // 2
    columns = qkv.shape[2]
    halves = width // LANES
    block = grads_in[0].shape[0]
    for r in range(n_head):
        grad_heads[peer_block(me, r, block), :] = grads_in[r][...]

    need(n_head + 3)

    def attend(span, all_probs, store):
        for head in range(heads):
            mine = head_lanes(head, columns)
            probs = all_probs(head)
            upper = jnp.where(mine, grad_heads[span, :], 0.0)
            size = upper.shape[0]
            grad_probs = dot(upper, qkv[2, span, :], NT)
            inner = jnp.sum(probs * grad_probs, axis=-1, keepdims=True)
            grad_scores = (probs * (grad_probs - inner)).astype(BF)
            rows = slice(head * size, (head + 1) * size)
            tall[0, rows, :size] = grad_scores
            tall[1, rows, :size] = probs.astype(BF)
            flat[:size, rows] = grad_scores
            stacks[0, rows, :] = jnp.where(mine, qkv[0, span, :], 0.0)
            stacks[1, rows, :] = jnp.where(mine, qkv[1, span, :], 0.0)
            stacks[2, rows, :] = upper
            store(head, grad_scores.astype(F32))
        every = slice(0, heads * size)
        dqkv[0, span, :] = (dot(flat[:size, every], stacks[1, every, :], NN) * SCALE).astype(BF)
        dqkv[1, span, :] = (dot(tall[0, every, :size], stacks[0, every, :], TN) * SCALE).astype(BF)
        dqkv[2, span, :] = dot(tall[1, every, :size], stacks[2, every, :], TN).astype(BF)

    for pair in range(pairs):

        def store_small(head, value, at=pair * narrow * SUB):
            small_rows[pl.ds(at + head, narrow, stride=SUB), :] = value[:narrow] + value[narrow:]

        span = slice(width + pair * wide, width + (pair + 1) * wide)
        attend(span, lambda head, pair=pair: small_probs[head, pair], store_small)
    done(0)

    def store_big(head, value):
        for half in range(halves):
            big_rows[pl.ds(half * width * SUB + head, width, stride=SUB), :] = value[
                :, LANES * half : LANES * (half + 1)
            ]

    attend(slice(0, width), lambda head: big_probs[head], store_big)
    done(1, 2)
    need(n_head + 4)
    column_sums[...] = jnp.zeros_like(column_sums)
    for i, k in enumerate((0, 2)):
        column_sums[i, pl.ds(me[0], 1), :] = jnp.sum(dqkv[k].astype(F32), axis=0, keepdims=True)
    for r in range(n_head):
        rows = peer_block(me, r, block)
        model = rows_out[r].shape[1]
        total = dot(dqkv[0, rows, :], attend_matrix(weights, 0, model), NT)
        total = total + dot(dqkv[1, rows, :], attend_matrix(weights, 1, model), NT)
        total = total + dot(dqkv[2, rows, :], attend_matrix(weights, 2, model), NT)
        rows_out[r][...] = total.astype(BF)


def middle_body(n_head, need, done, *refs):
    mixed, refs = refs[:n_head], refs[n_head:]
    me, rows, upper, vectors, hidden_bias = refs[:5]
    weights, refs = refs[5 : 5 + n_head], refs[5 + n_head :]
    layer_out, grad_hidden, sums, pre_sums, normed_grad, act_pre = refs[:6]
    grad_heads = refs[6:]
    need(*range(n_head + 5))
    columns = mixed[0].shape[1]
    slot = parcel_slot(columns)
    hidden = rows[...].astype(F32) + vectors[6:7, :]
    for r in range(n_head):
        need(n_head + 5 + r)
        hidden = hidden + dot(mixed[r][...], whole_matrix(weights[r], 0), NT)
    xhat, spread = norm_parts(hidden)
    low = (xhat * vectors[2:3, :] + vectors[3:4, :]).astype(BF)
    normed_grad[0] = low
    cotangent = upper[...]
    final = hidden + vectors[8:9, :]
    grad_normed = jnp.zeros_like(hidden)
    for r in range(n_head):
        peer = me[0] ^ r
        into, down = whole_matrix(weights[r], 1), whole_matrix(weights[r], 2)
        pre = dot(low, into, NN) + hidden_bias[pl.ds(peer, 1), :]
        phi = 0.5 * (1.0 + lax.erf(pre * (0.5**0.5)))
        active = (pre * phi).astype(BF)
        final = final + dot(active, down, NT)
        slope = phi + pre * jnp.exp(-0.5 * pre * pre) * (0.5 / jnp.pi) ** 0.5
        low_grad = (dot(cotangent, down, NN) * slope).astype(BF)
        pre_sums[pl.ds(peer, 1), :] = jnp.sum(low_grad.astype(F32), axis=0, keepdims=True)
        grad_normed = grad_normed + dot(low_grad, into, NT)
        act_pre[peer, :, 0:columns] = active
        act_pre[peer, :, slot : slot + columns] = low_grad
    layer_out[...] = final.astype(BF)
    wide = cotangent.astype(F32)
    grad = wide + norm_back(grad_normed * vectors[2:3, :], xhat, spread)
    grad_hidden[...] = grad
    grad_small = grad.astype(BF)
    normed_grad[1] = grad_small
    for r in range(n_head):
        grad_heads[r][...] = dot(grad_small, whole_matrix(weights[r], 0), NN).astype(BF)
    sums[0:1, :] = jnp.sum(grad_normed * xhat, axis=0, keepdims=True)
    sums[1:2, :] = jnp.sum(grad_normed, axis=0, keepdims=True)
    sums[2:3, :] = jnp.sum(grad, axis=0, keepdims=True)
    sums[3:4, :] = jnp.sum(wide, axis=0, keepdims=True)


def parcel_slot(columns):
    return (columns + LANES - 1) // LANES * LANES


def weight_grads_body(n_head, need, done, *refs):
    given, mixed, refs = refs[:n_head], refs[n_head : 2 * n_head], refs[2 * n_head :]
    me, act_pre, normed_one, dqkv = refs[:4]
    normed_grad, out = refs[4 : 4 + n_head], refs[-1]
    columns = mixed[0].shape[1]
    slot = parcel_slot(columns)

    def all_rows(pick):
        return jnp.concatenate([pick(me[0] ^ r) for r in range(n_head)], axis=0)

    need(2 * n_head + 2, 2 * n_head + 3)
    for k in range(3):
        put_matrix(out, k, dot(normed_one[...], dqkv[k], TN).astype(BF))
    need(*range(2 * n_head), 2 * n_head + 1, *range(2 * n_head + 4, 3 * n_head + 4))
    heads_out = jnp.concatenate([m[...] for m in mixed], axis=0)
    put_matrix(out, 3, dot(jnp.concatenate([n[1] for n in normed_grad], axis=0), heads_out, TN).astype(BF))
    grad_pre = all_rows(lambda p: act_pre[p, :, slot : slot + columns])
    put_matrix(out, 4, dot(jnp.concatenate([n[0] for n in normed_grad], axis=0), grad_pre, TN).astype(BF))
    cotangent = jnp.concatenate([g[1] for g in given], axis=0)
    put_matrix(out, 5, dot(cotangent, all_rows(lambda p: act_pre[p, :, 0:columns]), TN).astype(BF))


def merge_body(need, done, *refs):
    parts, out = refs[:-1], refs[-1]
    need(*range(len(parts)))
    value = parts[0][...].astype(F32)
    for part in parts[1:]:
        value = value + part[...].astype(F32)
    out[...] = value.astype(BF)


def input_body(n_head, n_vectors, need, done, *refs):
    parts, refs = refs[:n_head], refs[n_head:]
    me, rows, grad_hidden, vectors, sums, column_sums, pre_sums, input_grad, vector_rows, terms = refs
    need(*range(n_head), *range(n_head + 1, n_head + 7))
    grad_normed = parts[0][...].astype(F32)
    for part in parts[1:]:
        grad_normed = grad_normed + part[...].astype(F32)
    xhat, spread = norm_parts(rows[...].astype(F32))
    input_grad[...] = (grad_hidden[...] + norm_back(grad_normed * vectors[0:1, :], xhat, spread)).astype(BF)
    done(0)
    columns = column_sums.shape[2]
    terms[...] = jnp.zeros_like(terms)
    terms[0:1, :] = jnp.sum(grad_normed * xhat, axis=0, keepdims=True)
    terms[1:2, :] = jnp.sum(grad_normed, axis=0, keepdims=True)
    terms[2:4, :] = sums[0:2, :]
    terms[6:7, :] = sums[2:3, :]
    terms[8:9, :] = sums[3:4, :]
    for j in range(n_head):
        span = slice(j * columns, (j + 1) * columns)
        for i in range(2):
            terms[4 + i : 5 + i, span] = column_sums[i, j : j + 1, :]
        terms[7:8, span] = pre_sums[j : j + 1, :]
    inner, outer = vector_rows.shape[:2]
    lanes = vectors.shape[1] // (inner * outer)
    vector_rows[...] = jnp.zeros_like(vector_rows)
    for d in range(inner * outer):
        at = me[1] ^ d
        vector_rows[at % inner, at // inner, :, 0:lanes] = terms[:, d * lanes : (d + 1) * lanes].astype(BF)


def adamw_update(weight, first_moment, second_moment, gradient, learn_rate):
    first_new = BETA_FIRST * first_moment + (1.0 - BETA_FIRST) * gradient
    second_new = BETA_SECOND * second_moment + (1.0 - BETA_SECOND) * gradient * gradient
    first_hat = first_new / (1.0 - BETA_FIRST**ADAM_STEP)
    second_hat = second_new / (1.0 - BETA_SECOND**ADAM_STEP)
    weight_new = weight - learn_rate * (
        first_hat / (jnp.sqrt(second_hat) + ADAM_EPSILON) + WEIGHT_DECAY * weight
    )
    return (weight_new, first_new, second_new)


def told_body(need, done, arrived, *refs):
    parts, (shards, shard, told) = refs[:-3], refs[-3:]
    need(0)
    rest = arrived[0].astype(F32)
    for d in range(1, arrived.shape[0]):
        rest = rest + arrived[d].astype(F32)
    shards[...] = rest
    done(0)
    need(*range(1, len(parts) + 1))
    value = parts[0][...].astype(F32)
    for part in parts[1:]:
        value = value + part[...].astype(F32)
    table = value[VECTOR_ROWS:]
    shard[...] = table
    here = jnp.sum(table * table).reshape(1, 1) + jnp.sum(rest * rest).reshape(1, 1)
    tail = value[MESSAGE_ROWS : MESSAGE_ROWS + 1]
    free = LANES // 4
    gap = jnp.zeros((1, LANES - free), F32)
    spill = [jnp.concatenate([gap, tail[:, q * free : (q + 1) * free]], axis=1) for q in range(3)]
    spill = jnp.concatenate(spill + [jnp.zeros((MESSAGE_ROWS - 3, LANES), F32)], axis=0)
    message = jnp.where(corner_mask(), here, value[:MESSAGE_ROWS] + spill)
    told[...] = jnp.broadcast_to(message[None], told.shape)


def corner_mask():
    row = lax.broadcasted_iota(jnp.int32, (MESSAGE_ROWS, LANES), 0)
    lane = lax.broadcasted_iota(jnp.int32, (MESSAGE_ROWS, LANES), 1)
    return (row == MESSAGE_ROWS - 1) & (lane == LANES - 1)


def update_body(n_head, n_vectors, need, done, *refs):
    need(1)
    me, told, shards, out_shard, down_shard, table_shard = refs[:6]
    params, outs = refs[6:21], refs[21:36]
    norm_out = refs[36]
    n_dp = told.shape[0] // n_head

    def merged(d):
        value = told[d * n_head]
        for j in range(1, n_head):
            value = value + told[d * n_head + j]
        return value

    corner = corner_mask()

    def square(d, total):
        value = merged(d)
        return total + jnp.where(corner, value, value * value)

    total = lax.fori_loop(0, n_dp, square, jnp.zeros((MESSAGE_ROWS, LANES), F32))
    grad_norm = jnp.sqrt(jnp.sum(total).reshape(1, 1))
    norm_out[...] = jnp.broadcast_to(grad_norm, norm_out.shape)
    factor = CLIP_NORM / jnp.maximum(grad_norm, CLIP_NORM)

    def update(at, gradient, rate, pick=...):
        weight, first, second = (ref[pick] for ref in params[3 * at : 3 * at + 3])
        for ref, value in zip(outs[3 * at : 3 * at + 3], adamw_update(weight, first, second, gradient * factor, rate)):
            ref[pick] = value

    for k in range(3):
        update(0, shards[k], RATE_MATRIX, k)
    update(0, shards[4], RATE_MATRIX, 3)
    update(1, out_shard[...], RATE_OUTPUT)
    update(2, down_shard[...], RATE_MATRIX)
    mine, free = merged(me[1]), LANES // 4
    tail = jnp.concatenate([mine[q : q + 1, LANES - free :] for q in range(3)], axis=1)
    mine = jnp.concatenate([mine[:, : LANES - free], tail], axis=0)
    size = params[9].shape[1]
    gradient = jnp.zeros((n_vectors, size), F32)
    for j in range(n_head):
        gradient = jnp.where(me[0] == j, mine[:n_vectors, j * size : (j + 1) * size], gradient)
    update(3, gradient, RATE_VECTOR)
    heads = params[12].shape[0]
    for c in range(table_shard.shape[0] // heads):
        update(4, table_shard[c * heads : (c + 1) * heads, :], RATE_VECTOR, (slice(None), slice(c * LANES, (c + 1) * LANES)))


def exchange(value, axis):
    return lax.all_to_all(value, axis, split_axis=0, concat_axis=0, tiled=True)


def spread_all(value, axis):
    size = lax.axis_size(axis)
    return exchange(jnp.broadcast_to(value[None], (size, *value.shape)), axis)


def swap(values, n_head):
    return [values[0]] + [
        lax.ppermute(values[r], "head", [(i, i ^ r) for i in range(n_head)]) for r in range(1, n_head)
    ]


def struct(shape, dtype):
    return jax.ShapeDtypeStruct(shape, dtype)


def on_device(
    node_rows,
    output_grad,
    weight_in,
    first_in,
    second_in,
    weight_out,
    first_out,
    second_out,
    weight_down,
    first_down,
    second_down,
    vectors,
    first_vectors,
    second_vectors,
    bias_table,
    first_table,
    second_table,
    big_counts,
    small_counts,
    big_distance,
    small_distance,
    big_paths,
    small_paths,
    big_lengths,
    small_lengths,
):
    everyone = ("dp", "head")
    n_dp, n_head = lax.axis_size("dp"), lax.axis_size("head")
    head_index, dp_index = lax.axis_index("head"), lax.axis_index("dp")
    me = head_index.reshape(1).astype(jnp.int32)
    shard_rows, columns = weight_in.shape[1], weight_in.shape[2]
    model = shard_rows * n_dp
    my_rows = node_rows.shape[0]
    group_rows = my_rows * n_head
    heads = columns // HEAD_DIM
    width, narrow = big_distance.shape[1], small_distance.shape[1]
    pairs = small_distance.shape[0] // 2
    table_chunks = bias_table.shape[0] // LANES
    all_chunks = table_chunks * n_dp
    n_vectors, shard_width = vectors.shape
    stacked = shard_rows % 16 == 0
    big_ints = (big_distance, big_paths, big_lengths)
    small_ints = (small_distance, small_paths, small_lengths)
    inner = inner_of(n_dp)
    outer = n_dp // inner
    dp_pairs = lambda k: [(i, i ^ k) for i in range(n_dp)]
    us = jnp.stack([head_index, dp_index]).astype(jnp.int32)
    lanes_used = model // n_dp

    def far_shards(value):
        return [value] + [lax.ppermute(value, "dp", dp_pairs(k)) for k in range(inner, n_dp, inner)]

    def near_shards(values):
        value = jnp.stack(values)
        return [value] + [lax.ppermute(value, "dp", dp_pairs(k)) for k in range(1, inner)]

    def to_head(value, r):
        return lax.ppermute(value, "head", [(i, i ^ r) for i in range(n_head)])

    far = n_head // 2
    near_heads = range(1, far)

    rest_sent = jnp.stack([weight_out.astype(BF).T, weight_in[3].astype(BF), weight_down.astype(BF).T])
    rest_sent, my_table = lax.optimization_barrier((rest_sent, bias_table))
    with jax.named_scope("rest_far"):
        rest_far = far_shards(rest_sent)
    table_sent = my_table.astype(BF).T.reshape(heads, table_chunks, LANES).transpose(1, 0, 2)
    with jax.named_scope("table_all"):
        table_all = spread_all(table_sent, "dp").reshape(all_chunks * heads, LANES)
    given = {0: jnp.stack([node_rows, output_grad])}
    with jax.named_scope("rows_far"):
        given[far] = to_head(given[0], far)
    qkv_sent = weight_in[:3].astype(BF)
    with jax.named_scope("vectors_head"):
        own_vectors = lax.dynamic_update_slice_in_dim(
            jnp.zeros((n_vectors, lanes_used), F32), vectors, head_index * shard_width, 1
        )
        step = far
        while step:
            own_vectors = own_vectors + to_head(own_vectors, step)
            step //= 2
    rest, pieces = own_vectors, []
    for _ in range(PIECES):
        piece = lax.reduce_precision(rest, 8, 7)
        rest = rest - piece
        pieces.append(jnp.pad(piece.astype(BF), ((0, PIECE_ROWS - n_vectors), (0, columns - lanes_used))))
    qkv_sent = jnp.concatenate([qkv_sent.reshape(3 * shard_rows, columns), *pieces])
    qkv_sent, *rest_far = lax.optimization_barrier((qkv_sent, *rest_far))
    with jax.named_scope("rest_near"):
        rest_near = near_shards(rest_far)
    with jax.named_scope("qkv_far"):
        qkv_far = far_shards(qkv_sent)

    def pair_bias(part, table, ints):
        rows = width // sum(BIG_QUARTERS) * BIG_QUARTERS[part]
        big_range = struct((heads, width // LANES, rows, LANES), F32)
        return kernel_call(
            lambda *refs: bias_body(part, *refs),
            ([struct((heads, pairs, narrow, LANES), F32)] if part == 0 else []) + [big_range],
            "pair_bias",
            12 if part == 0 else 20,
            (table, *ints),
            [
                pltpu.VMEM((heads, all_chunks // 2, SUB, LANES), jnp.int32),
                pltpu.VMEM((len(PRODUCTS), max(CHUNKS) // 2 * heads, 2 * LANES), BF),
                pltpu.VMEM((len(PRODUCTS), heads * SUB, LANES), F32),
            ],
        )

    small_bias, *big_bias = pair_bias(0, table_all, (*small_ints, *big_ints))
    held = lax.optimization_barrier((small_bias, table_all, given[far], *rest_near, *qkv_far))
    (small_bias, table_all, given[far]), held = held[:3], held[3:]
    rest_near, qkv_far = held[:inner], held[inner:]
    weights_rest = jnp.concatenate(rest_near)
    with jax.named_scope("qkv_near"):
        qkv_near = near_shards(qkv_far)
    if not stacked:
        order = jnp.argsort(jnp.array(xor_order(n_dp), jnp.int32) ^ dp_index)
        weights_rest = weights_rest[order].transpose(1, 0, 2, 3).reshape(3, model, columns)
    weights_held = {0: weights_rest}
    with jax.named_scope("rest_far_head"):
        weights_held[far] = to_head(weights_rest, far)
    with jax.named_scope("rows_near"):
        for r in near_heads:
            given[r], given[far + r] = to_head(given[0], r), to_head(given[far], r)
    for part in range(1, BIG_PARTS):
        big_bias += pair_bias(part, table_all, big_ints)
    held = lax.optimization_barrier((big_bias[-1], *qkv_near, *[given[r] for r in range(n_head)]))
    big_bias[-1], qkv_near, given = held[0], held[1 : 1 + inner], held[1 + inner :]
    with jax.named_scope("rest_near_head"):
        for r in near_heads:
            weights_held[r] = to_head(weights_held[0], r)
    weights_attend = list(qkv_near)
    vector_row, vector_pieces = 3 * shard_rows, ()
    if not stacked:
        weights_attend = jnp.concatenate(qkv_near)[order]
        vector_row, vector_pieces = 0, (weights_attend[:, 3 * shard_rows :],)
        weights_attend = weights_attend[:, : 3 * shard_rows].reshape(n_dp, 3, shard_rows, columns)
        weights_attend = weights_attend.transpose(1, 0, 2, 3).reshape(3, model, columns)

    block = struct((my_rows, columns), BF)
    rows_block = struct((my_rows, model), BF)
    normed_one, qkv, big_probs, small_probs, all_vectors, hidden_bias, *mixed = kernel_call(
        lambda *refs: forward_body(n_head, vector_row, *refs),
        [
            struct((group_rows, model), BF),
            struct((3, group_rows, columns), BF),
            struct((heads, width, width), F32),
            struct((heads, pairs, 2 * narrow, 2 * narrow), F32),
            struct((n_vectors, model), F32),
            struct((n_head, columns), F32),
            *[block] * n_head,
        ],
        "attend_forward",
        12,
        (*given, us, big_counts, small_counts, weights_attend, small_bias, *big_bias, *vector_pieces),
        [
            pltpu.VMEM((group_rows, columns), BF),
            pltpu.VMEM((width, heads * width), BF),
            pltpu.VMEM((heads * width, columns), BF),
        ],
        range(n_head, n_head + 3),
        (n_head + 3,) if stacked else (),
        n_head,
    )
    with jax.named_scope("mixed_rows"):
        mixed_rows = swap(mixed, n_head)
    mixed_rows[0], *held = lax.optimization_barrier((mixed_rows[0], *[weights_held[r] for r in range(far + 1)]))
    weights_held.update(enumerate(held))
    with jax.named_scope("rest_near_head"):
        for r in near_heads:
            weights_held[far + r] = to_head(weights_held[far], r)
    weights_rest = [weights_held[r] for r in range(n_head)]

    layer_out, grad_hidden, sums, pre_sums, normed_grad, act_pre, *grad_heads = kernel_call(
        lambda *refs: middle_body(n_head, *refs),
        [
            rows_block,
            struct((my_rows, model), F32),
            struct((4, model), F32),
            struct((n_head, columns), F32),
            struct((2, my_rows, model), BF),
            struct((n_head, my_rows, 2 * parcel_slot(columns)), BF),
            *[block] * n_head,
        ],
        "feed_forward",
        6,
        (*mixed_rows, us, node_rows, output_grad, all_vectors, hidden_bias, *weights_rest),
        (),
        (n_head,),
        range(n_head + 5, 2 * n_head + 5) if stacked else (),
        n_head,
    )
    with jax.named_scope("grad_heads"):
        grad_heads = swap(grad_heads, n_head)
    with jax.named_scope("act_pre"):
        act_pre = exchange(act_pre, "head")
    with jax.named_scope("normed_grad"):
        rows_held = {0: normed_grad}
        for r in (far, *range(1, far)):
            rows_held[r] = lax.ppermute(normed_grad, "head", [(i, i ^ r) for i in range(n_head)])

    small_rows, big_rows, dqkv, column_sums, *rows_sent = kernel_call(
        lambda *refs: backward_body(n_head, *refs),
        [
            struct((pairs * narrow * SUB, LANES), F32),
            struct((width // LANES * width * SUB, LANES), F32),
            struct((3, group_rows, columns), BF),
            struct((2, n_head, columns), F32),
            *[rows_block] * n_head,
        ],
        "attend_backward",
        14,
        (*grad_heads, us, qkv, small_probs, big_probs, weights_attend),
        [
            pltpu.VMEM((group_rows, columns), BF),
            pltpu.VMEM((2, heads * width, width), BF),
            pltpu.VMEM((width, heads * width), BF),
            pltpu.VMEM((3, heads * width, columns), BF),
        ],
        (n_head,),
        (n_head + 4,) if stacked else (),
        n_head,
    )
    small_rows, *arrived = lax.optimization_barrier((small_rows, *[rows_held[r] for r in range(1, far + 1)]))
    rows_held.update(zip(range(1, far + 1), arrived))
    with jax.named_scope("normed_grad"):
        for r in range(1, far):
            rows_held[far + r] = lax.ppermute(rows_held[far], "head", [(i, i ^ r) for i in range(n_head)])
    (weight_grads,) = kernel_call(
        lambda *refs: weight_grads_body(n_head, *refs),
        [struct((n_dp, 6, shard_rows, columns) if stacked else (6, model, columns), BF)],
        "weight_grads",
        6,
        (*given, *mixed, us, act_pre, normed_one, dqkv, *[rows_held[r] for r in range(n_head)]),
        (),
        (2 * n_head,),
        early=(2 * n_head + 2, 2 * n_head + 3),
    )
    if not stacked:
        weight_grads = weight_grads.reshape(6, n_dp, shard_rows, columns).transpose(1, 0, 2, 3)
    with jax.named_scope("grad_normed_one"):
        rows_back = swap(rows_sent, n_head)
    _, *rows_back = lax.optimization_barrier((weight_grads, *rows_back))
    with jax.named_scope("weight_grads"):
        weights_arrived = exchange(weight_grads, "dp")
    input_grad, vector_rows = kernel_call(
        lambda *refs: input_body(n_head, n_vectors, *refs),
        [rows_block, struct((inner, outer, VECTOR_ROWS, LANES), BF)],
        "input_grad",
        3,
        (*rows_back, us, node_rows, grad_hidden, all_vectors, sums, column_sums, pre_sums),
        [pltpu.VMEM((VECTOR_ROWS, model), F32)],
        (n_head,),
    )
    table_rows = table_chunks * heads
    block = struct((outer, VECTOR_ROWS + table_rows, LANES), BF)
    inner_sent = kernel_call(
        scatter_body,
        [(inner, block)],
        "table_scatter",
        40,
        (small_rows, *small_ints, big_rows, *big_ints, us, vector_rows),
        [pltpu.VMEM((LOOKUPS, SPLIT, SUB * max(HIGHS)), F32)],
        (8,),
    )
    with jax.named_scope("table_inner"):
        arrived = [inner_sent[0]] + [lax.ppermute(inner_sent[k], "dp", dp_pairs(k)) for k in range(1, inner)]
    outer_sent = kernel_call(
        merge_body,
        [(outer, struct(block.shape[1:], BF))],
        "merge_table",
        1,
        tuple(arrived),
    )
    with jax.named_scope("table_outer"):
        parts = [outer_sent[0]] + [
            lax.ppermute(outer_sent[k], "dp", dp_pairs(k * inner)) for k in range(1, outer)
        ]
    weights_arrived, *parts = lax.optimization_barrier((weights_arrived, *parts))
    shards, table_shard, told = kernel_call(
        told_body,
        [
            struct((6, shard_rows, columns), F32),
            struct((table_rows, LANES), F32),
            struct((n_dp * n_head, MESSAGE_ROWS, LANES), F32),
        ],
        "shard_sums",
        4,
        (weights_arrived, *parts),
    )
    with jax.named_scope("squares"):
        told = exchange(told, everyone)
    params = (weight_in, first_in, second_in, weight_out, first_out, second_out)
    params += (weight_down, first_down, second_down, vectors, first_vectors, second_vectors)
    params += (bias_table.T, first_table.T, second_table.T)
    *updated, grad_norm = kernel_call(
        lambda *refs: update_body(n_head, n_vectors, *refs),
        [*[struct(p.shape, F32) for p in params], struct((1, LANES), F32)],
        "update",
        3,
        (us, told, shards, shards[3].T, shards[5].T, table_shard, *params),
        (),
        (0,),
        ready=range(2, 21),
        limit=16 << 20,
    )
    updated = updated[:12] + [value.T for value in updated[12:]]
    return (layer_out, input_grad, grad_norm[0, 0], *updated)


def solution(mesh):
    rows = P(("dp", "head"), None)
    square = P(None, "dp", "head")
    across = P("head", "dp")
    thin = P(None, ("dp", "head"))
    table = P("dp", "head")
    return jax.shard_map(
        on_device,
        mesh=mesh,
        in_specs=(rows, rows)
        + (square,) * 3
        + (across,) * 6
        + (thin,) * 3
        + (table,) * 3
        + (P("dp"), P("dp", None))
        + (P("dp", None, None),) * 2
        + (P(None, "dp", None, None),) * 2
        + (P("dp", None, None),) * 2,
        out_specs=(rows, rows, P()) + (square,) * 3 + (across,) * 6 + (thin,) * 3 + (table,) * 3,
        check_vma=False,
    )
```

```python
import jax
import jax.numpy as jnp
from jax import lax
from jax.experimental import pallas as pl
from jax.experimental.pallas import tpu as pltpu
from jax.sharding import PartitionSpec as P

HEAD_DIM = 24
NDIST = 512
NTYPE = 1536
STEPS = 5
ADAM_STEP = 10

NORM_EPSILON = 1e-05
NEGATIVE_FILL = -1e30
BETA_FIRST = 0.9
BETA_SECOND = 0.95
ADAM_EPSILON = 1e-08
RATE_MATRIX = 0.02
RATE_OUTPUT = 0.05
RATE_VECTOR = 0.15
WEIGHT_DECAY = 0.01
CLIP_NORM = 1.0

LANES = 128
SUB = 8
FIRST = [0] + [(NDIST + n * NTYPE) // LANES for n in range(STEPS)]
CHUNKS = [NDIST // LANES] + [NTYPE // LANES] * STEPS
LOOKUPS = STEPS + 1
VECTOR_ROWS = 16
BIG_QUARTERS = (1, 3)
BIG_PARTS = len(BIG_QUARTERS)
MESSAGE_ROWS = 8
PRODUCTS = (STEPS - 1, STEPS)
PIECES = 3
PIECE_ROWS = 16
FIXED = 8192.0
SPLIT = 112
SPLIT_RECIPROCAL, SPLIT_SHIFT = 4682, 19
HIGHS = [-(-(n * LANES) // (2 * SPLIT)) * 2 for n in CHUNKS]
NOWHERE = 4095
SCALE = HEAD_DIM**-0.5
BF = jnp.bfloat16
F32 = jnp.float32
VMEM_BYTES = 56 << 20

NN = (((1,), (0,)), ((), ()))
NT = (((1,), (1,)), ((), ()))
TN = (((0,), (0,)), ((), ()))


def dot(left, right, dims):
    return lax.dot_general(left, right, dims, preferred_element_type=F32)


def inner_of(size):
    return 1 << ((size.bit_length() - 1) // 2)


def xor_order(size):
    inner = inner_of(size)
    return [a * inner + b for b in range(inner) for a in range(size // inner)]


def kernel_call(body, outs, name, micros, args, scratch=(), smem_in=(), placed=(), us_at=None, ready=(), limit=VMEM_BYTES, early=()):
    groups = [arg if isinstance(arg, list) else [arg] for arg in args]
    args = [struct((sum(a.shape[0] for a in g), *g[0].shape[1:]), g[0].dtype) if len(g) > 1 else g[0] for g in groups]
    starts = [sum(len(g) for g in groups[:i]) for i in range(len(groups) + 1)]
    n_in, n_out = len(args), len(outs)
    moved = [i for i in range(n_in) if i not in smem_in and i not in ready]
    blocks = [out[0] if isinstance(out, tuple) else 0 for out in outs]
    shapes = [out[1] if isinstance(out, tuple) else out for out in outs]
    flat = [(i, k) for i in range(n_out) for k in range(max(blocks[i], 1))]
    n_sems = sum(args[i].shape[0] if i in placed else 1 for i in moved)

    def wrapped(*refs):
        parts = [refs[starts[i] : starts[i + 1]] for i in range(n_in)]
        given, results = [p[0] for p in parts], refs[starts[-1] : starts[-1] + len(flat)]
        refs = refs[starts[-1] + len(flat) :]
        held = dict(zip(moved, refs))
        made, refs = refs[len(moved) : len(moved) + n_out], refs[len(moved) + n_out :]
        rest, (in_sems, out_sems) = refs[:-2], refs[-2:]
        arriving, sem = {}, 0
        for i in moved:
            pieces = [(given[i], held[i])]
            if i in placed:
                size = args[i].shape[0]
                each = size // len(parts[i])
                pieces = [
                    (parts[i][k // each].at[k % each], held[i].at[given[us_at][1] ^ other])
                    for k, other in enumerate(xor_order(size))
                ]
            arriving[i] = [pltpu.make_async_copy(a, b, in_sems.at[sem + n]) for n, (a, b) in enumerate(pieces)]
            sem += len(pieces)
        leaving = [
            pltpu.make_async_copy(made[i].at[k] if blocks[i] else made[i], results[at], out_sems.at[at])
            for at, (i, k) in enumerate(flat)
        ]
        for i in [*early, *[i for i in moved if i not in early]]:
            for copy in arriving[i]:
                copy.start()
        waiting, unsent = list(moved), list(range(n_out))

        def need(*which):
            for i in which:
                if i in waiting:
                    waiting.remove(i)
                    for copy in arriving[i]:
                        copy.wait()

        def done(*which):
            for i in which:
                if i in unsent:
                    unsent.remove(i)
                    for at, (j, _) in enumerate(flat):
                        if i == j:
                            leaving[at].start()

        body(need, done, *[held.get(i, given[i]) for i in range(n_in)], *made, *rest)
        need(*moved)
        done(*range(n_out))
        for copy in leaving:
            copy.wait()

    anywhere, smem = pl.BlockSpec(memory_space=pl.ANY), pl.BlockSpec(memory_space=pltpu.SMEM)
    vmem = pl.BlockSpec(memory_space=pltpu.VMEM)
    return pl.pallas_call(
        wrapped,
        out_shape=tuple(shapes[i] for i, _ in flat),
        in_specs=[
            smem if i in smem_in else vmem if i in ready else anywhere for i in range(n_in) for _ in groups[i]
        ],
        out_specs=tuple([anywhere] * len(flat)),
        scratch_shapes=[pltpu.VMEM(args[i].shape, args[i].dtype) for i in moved]
        + [pltpu.VMEM((n, *o.shape) if n else o.shape, o.dtype) for n, o in zip(blocks, shapes)]
        + list(scratch)
        + [pltpu.SemaphoreType.DMA((n_sems,)), pltpu.SemaphoreType.DMA((len(flat),))],
        name=name,
        compiler_params=pltpu.CompilerParams(vmem_limit_bytes=limit),
        cost_estimate=pl.CostEstimate(flops=int(micros * 1e9), bytes_accessed=1 << 20, transcendentals=0),
    )(*[part for group in groups for part in group])


def big_block(refs, block, half):
    distance, paths, lengths = refs
    rows, lanes = pl.ds(SUB * block, SUB), slice(LANES * half, LANES * half + LANES)
    return [distance[0, rows, lanes]] + [paths[n, 0, rows, lanes] for n in range(STEPS)], lengths[0, rows, lanes]


def small_block(refs, block, pair):
    distance, paths, lengths = refs
    rows = pl.ds(SUB * block, SUB)

    def two(ref, *lead):
        return jnp.concatenate([ref[(*lead, 2 * pair, rows)], ref[(*lead, 2 * pair + 1, rows)]], axis=1)

    return [two(distance)] + [two(paths, n) for n in range(STEPS)], two(lengths)


def each_block(load, refs, first, count, sides, group, step):
    def some(at, carry):
        blocks = [first + at * group + u for u in range(group)]
        step([(*load(refs, block, side), block, side) for block in blocks for side in range(sides)])
        return carry

    lax.fori_loop(0, count // group, some, 0)


def pick(items, high):
    bit = 1
    while len(items) > 1:
        odd = (high & bit) != 0
        items = [
            jnp.where(odd, items[k + 1], items[k]) if k + 1 < len(items) else items[k]
            for k in range(0, len(items), 2)
        ]
        bit *= 2
    return items[0]


def bias_body(part, need, done, table, *refs):
    small, refs = (refs[:3], refs[3:]) if part == 0 else (None, refs)
    big, outs, (words, rows_of, found_rows) = refs[:3], refs[3:-3], refs[-3:]
    need(0)
    heads, count = words.shape[:2]
    for k in range(count):
        low = jnp.round(table[SUB * 2 * k : SUB * (2 * k + 1), :].astype(F32) * FIXED).astype(jnp.int32)
        high = jnp.round(table[SUB * (2 * k + 1) : SUB * (2 * k + 2), :].astype(F32) * FIXED).astype(jnp.int32)
        word = (high << 16) | (low & 0xFFFF)
        for h in range(heads):
            words[h, k] = jnp.broadcast_to(word[h : h + 1], (SUB, LANES))

    for i, t in enumerate(PRODUCTS):
        rows_of[i] = table[SUB * FIRST[t] : SUB * (FIRST[t] + CHUNKS[t]), :]
    sub = lax.broadcasted_iota(jnp.int32, (2 * SUB, LANES), 0)
    patterns = [(sub + 2 * SUB * k).astype(F32).astype(BF) for k in range(LANES // (2 * SUB))]
    zero, one = jnp.zeros((2 * SUB, LANES), BF), jnp.ones((2 * SUB, LANES), BF)

    def product(i, code):
        spread = [jnp.broadcast_to(code[s : s + 1], (SUB, LANES)) for s in range(SUB)]
        hot = []
        for s in range(SUB):
            low = (spread[s] & (LANES - 1)).astype(F32)
            low = jnp.concatenate([low, low], axis=0).astype(BF)
            hot.append(jnp.concatenate([jnp.where(low == p, one, zero) for p in patterns], axis=0))
        values = dot(rows_of[i], jnp.concatenate(hot, axis=1), NN)
        for s in range(SUB):
            lanes = slice(LANES * s, LANES * (s + 1))
            items = [values[heads * c : heads * (c + 1), lanes] for c in range(values.shape[0] // heads)]
            found_rows[i, pl.ds(s, heads, stride=SUB), :] = pick(items, spread[s] >> 7)

    def step(store):
        def run(parts):
            for index, lengths, block, side in parts:
                share = 1.0 / lengths.astype(F32)
                first, edges = [None] * heads, [None] * heads
                for i, t in enumerate(PRODUCTS):
                    product(i, index[t])
                for t in range(LOOKUPS):
                    if t in PRODUCTS:
                        continue
                    code = index[t]
                    lane = code & (LANES - 1)
                    odd = [(code & bit) != 0 for bit in (256, 512, 1024)]
                    shift = ((code >> 3) & 16) ^ 16
                    live = lengths > t - 1
                    for h in range(heads):
                        found = [
                            jnp.take_along_axis(words[h, FIRST[t] // 2 + k], lane, axis=1, mode="promise_in_bounds")
                            for k in range(CHUNKS[t] // 2)
                        ]
                        level = 0
                        while len(found) > 1:
                            found = [
                                jnp.where(odd[level], found[k + 1], found[k]) if k + 1 < len(found) else found[k]
                                for k in range(0, len(found), 2)
                            ]
                            level += 1
                        value = (found[0] << shift) >> 16
                        if t == 0:
                            first[h] = value
                        else:
                            value = jnp.where(live, value, 0)
                            edges[h] = value if edges[h] is None else edges[h] + value
                for h in range(heads):
                    edge = edges[h].astype(F32) * (1.0 / FIXED)
                    for i, t in enumerate(PRODUCTS):
                        edge = edge + jnp.where(lengths > t - 1, found_rows[i, SUB * h : SUB * (h + 1), :], 0.0)
                    store(h, side, block, first[h].astype(F32) * (1.0 / FIXED) + edge * share)

        return run

    if small:

        def store_small(h, side, block, value):
            outs[0][h, side, pl.ds(SUB * block, SUB), :] = value

        need(1, 2, 3)
        each_block(small_block, small, 0, small[0].shape[1] // SUB, small[0].shape[0] // 2, 1, step(store_small))
        done(0)
    need(*range(1, 7 if small else 4))
    out = outs[-1]
    count = out.shape[2] // SUB
    first_block = big[0].shape[1] // SUB // sum(BIG_QUARTERS) * sum(BIG_QUARTERS[:part])

    def store_big(h, side, block, value):
        out[h, side, pl.ds(SUB * (block - first_block), SUB), :] = value

    each_block(big_block, big, first_block, count, big[0].shape[2] // LANES, 1, step(store_big))


def scatter_body(need, done, small_grads, sd, sp, sl, big_grads, bd, bp, bl, me, vector_rows, parcel, total):
    total[...] = jnp.zeros_like(total)
    sub = lax.broadcasted_iota(jnp.int32, (2 * SUB, LANES), 0)
    low_pattern = [(sub + 2 * SUB * k).astype(F32).astype(BF) for k in range(SPLIT // (2 * SUB))]
    upper = (sub >= SUB).astype(jnp.int32)
    high_pattern = [(2 * k + upper).astype(F32).astype(BF) for k in range(max(HIGHS) // 2)]
    zero, one = jnp.zeros((2 * SUB, LANES), BF), jnp.ones((2 * SUB, LANES), BF)

    def twice(value):
        return jnp.concatenate([value, value], axis=0).astype(BF)

    def step(grads, side_rows):
        def run(parts):
            whole, shared = [], []
            for index, lengths, block, side in parts:
                inverse = 1.0 / lengths.astype(F32)
                for s in range(SUB):
                    g = grads[pl.ds((side * side_rows + SUB * block + s) * SUB, SUB), :]
                    whole.append(twice(g))
                    shared.append(twice(g * jnp.broadcast_to(inverse[s : s + 1], (SUB, LANES))))
            for t in range(LOOKUPS):
                left, right = [], []
                for part, (index, lengths, _, _) in enumerate(parts):
                    high = index[t] * SPLIT_RECIPROCAL >> SPLIT_SHIFT
                    code = (high << 7) | (index[t] - high * SPLIT)
                    if t > 0:
                        code = jnp.where(lengths > t - 1, code, NOWHERE)
                    for s in range(SUB):
                        spread = jnp.broadcast_to(code[s : s + 1], (SUB, LANES))
                        low = twice((spread & (LANES - 1)).astype(F32))
                        high = twice((spread >> 7).astype(F32))
                        source = (whole if t == 0 else shared)[SUB * part + s]
                        left.append(jnp.concatenate([jnp.where(low == p, one, zero) for p in low_pattern], axis=0))
                        right.append(
                            jnp.concatenate(
                                [jnp.where(high == p, source, zero) for p in high_pattern[: HIGHS[t] // 2]], axis=0
                            )
                        )
                span = slice(0, SUB * HIGHS[t])
                total[t, :, span] += dot(jnp.concatenate(left, axis=1), jnp.concatenate(right, axis=1), NT)

        return run

    need(0, 1, 2, 3)
    narrow, width = sd.shape[1], bd.shape[1]
    each_block(small_block, (sd, sp, sl), 0, narrow // SUB, sd.shape[0] // 2, 4, step(small_grads, narrow))
    need(4, 5, 6, 7)
    each_block(big_block, (bd, bp, bl), 0, width // SUB, width // LANES, 4, step(big_grads, width))
    need(9)
    inner, outer, height, _ = parcel.shape
    height -= VECTOR_ROWS
    parcel[:, :, :VECTOR_ROWS, :] = vector_rows[...]
    chunks = []
    for t in range(LOOKUPS):
        rows = total[t, :, 0 : SUB * HIGHS[t]].T
        for c in range(CHUNKS[t]):
            first, last = c * LANES, (c + 1) * LANES
            pieces = []
            for high in range(first // SPLIT, (last - 1) // SPLIT + 1):
                start, end = max(first - high * SPLIT, 0), min(last - high * SPLIT, SPLIT)
                pieces.append(rows[SUB * high : SUB * (high + 1), start:end])
            chunks.append(jnp.concatenate(pieces, axis=1))
    table = jnp.concatenate(chunks, axis=0).astype(BF)
    for d in range(inner * outer):
        at = me[1] ^ d
        parcel[at % inner, at // inner, VECTOR_ROWS:, :] = table[d * height : (d + 1) * height]


def attend_matrix(ref, k, model):
    if ref.shape[1] == model:
        return ref[k]
    rows = model // ref.shape[0]
    return ref[:, k * rows : (k + 1) * rows, :].reshape(model, ref.shape[2])


def whole_matrix(ref, k):
    if len(ref.shape) == 3:
        return ref[k]
    value = ref[:, k]
    return value.reshape(value.shape[0] * value.shape[1], value.shape[2])


def norm_parts(values):
    center = values - jnp.mean(values, axis=-1, keepdims=True)
    spread = lax.rsqrt(jnp.mean(center * center, axis=-1, keepdims=True) + NORM_EPSILON)
    return center * spread, spread


def norm_back(scaled, xhat, spread):
    return spread * (
        scaled
        - jnp.mean(scaled, axis=-1, keepdims=True)
        - xhat * jnp.mean(scaled * xhat, axis=-1, keepdims=True)
    )


def head_lanes(head, width):
    lane = lax.broadcasted_iota(jnp.int32, (1, width), 1)
    return (lane >= head * HEAD_DIM) & (lane < (head + 1) * HEAD_DIM)


def peer_block(me, r, rows):
    return pl.ds(pl.multiple_of((me[0] ^ r) * rows, rows), rows)


def forward_body(n_head, vector_row, need, done, *refs):
    rows_in, refs = refs[:n_head], refs[n_head:]
    me, big_counts, small_counts, weights, small_bias = refs[:5]
    big_bias, refs = refs[5 : 5 + BIG_PARTS], refs[5 + BIG_PARTS :]
    pieces = weights
    if vector_row == 0:
        pieces, refs = refs[0], refs[1:]
    normed, qkv, big_probs, small_probs, vectors, hidden_bias = refs[:6]
    mixed_out, (mixed, flat, stack) = refs[6 : 6 + n_head], refs[6 + n_head :]
    block = rows_in[0].shape[1]
    need(*range(n_head), n_head + 3)
    if vector_row == 0:
        need(n_head + 5 + BIG_PARTS)
    n_vectors, size = vectors.shape[0], vectors.shape[1] // pieces.shape[0]
    for d in range(pieces.shape[0]):
        parts = [pieces[d, pl.ds(vector_row + p * PIECE_ROWS, PIECE_ROWS), 0:size].astype(F32) for p in range(PIECES)]
        vectors[:, d * size : (d + 1) * size] = sum(parts[1:], parts[0])[:n_vectors]
    heads, width = big_probs.shape[:2]
    pairs, wide = small_probs.shape[1:3]
    narrow = wide // 2
    columns = qkv.shape[2]
    halves = width // LANES
    biases = [None] * 2
    for j in range(n_head):
        span = slice(j * columns, (j + 1) * columns)
        hidden_bias[j : j + 1, :] = vectors[7:8, span]
        for i in range(2):
            value = jnp.where(me[0] == j, vectors[4 + i : 5 + i, span], 0.0)
            biases[i] = value if j == 0 else biases[i] + value
    for r in range(n_head):
        xhat, _ = norm_parts(rows_in[r][0].astype(F32))
        normed[peer_block(me, r, block), :] = (xhat * vectors[0:1, :] + vectors[1:2, :]).astype(BF)
    done(0, 4, 5)
    for k in range(3):
        value = dot(normed[...], attend_matrix(weights, k, normed.shape[1]), NN)
        if k != 1:
            value = value + biases[k // 2]
        qkv[k] = value.astype(BF)
    done(1)
    need(*range(n_head + 4, n_head + 5 + BIG_PARTS))
    big_live = lax.broadcasted_iota(jnp.int32, (1, width), 1) < big_counts[0]
    small_live = []
    row = lax.broadcasted_iota(jnp.int32, (wide, wide), 0)
    lane = lax.broadcasted_iota(jnp.int32, (wide, wide), 1)
    for pair in range(pairs):
        first = (row < narrow) & (lane < small_counts[0, 2 * pair])
        second = (row >= narrow) & (lane >= narrow) & (lane < narrow + small_counts[0, 2 * pair + 1])
        small_live.append(first | second)

    def attend(span, extra, live, store):
        for head in range(heads):
            mine = head_lanes(head, columns)
            query = jnp.where(mine, qkv[0, span, :], 0.0)
            size = query.shape[0]
            scores = dot(query, qkv[1, span, :], NT) * SCALE + extra(head)
            scores = jnp.where(live, scores, NEGATIVE_FILL)
            power = jnp.exp(scores - jnp.max(scores, axis=-1, keepdims=True))
            probs = power * (1.0 / jnp.sum(power, axis=-1, keepdims=True))
            store(head, probs)
            rows = slice(head * size, (head + 1) * size)
            flat[:size, rows] = probs.astype(BF)
            stack[rows, :] = jnp.where(mine, qkv[2, span, :], 0.0)
        every = slice(0, heads * size)
        mixed[span, :] = dot(flat[:size, every], stack[every, :], NN).astype(BF)

    def big_extra(head):
        return jnp.concatenate(
            [jnp.concatenate([part[head, half] for part in big_bias], axis=0) for half in range(halves)], axis=1
        )

    def store_big(head, probs):
        big_probs[head] = probs

    attend(slice(0, width), big_extra, big_live, store_big)
    done(2)
    for pair in range(pairs):

        def small_extra(head, pair=pair):
            extra = small_bias[head, pair]
            return jnp.concatenate([extra, extra], axis=0)

        def store_small(head, probs, pair=pair):
            small_probs[head, pair] = probs

        span = slice(width + pair * wide, width + (pair + 1) * wide)
        attend(span, small_extra, small_live[pair], store_small)
    done(3)
    for r in range(n_head):
        mixed_out[r][...] = mixed[peer_block(me, r, block), :]


def put_matrix(ref, k, value):
    if len(ref.shape) == 3:
        ref[k] = value
        return
    rows, columns = ref.shape[2], value.shape[1]
    side = slice(k % 2 * columns, (k % 2 + 1) * columns)
    for d in range(ref.shape[0]):
        ref[d, k // 2, :, side] = value[d * rows : (d + 1) * rows]


def backward_body(n_head, need, done, *refs):
    need(*range(n_head), n_head + 1, n_head + 2)
    grads_in, refs = refs[:n_head], refs[n_head:]
    me, qkv, small_probs, big_probs, weights, small_rows, big_rows, dqkv, column_sums = refs[:9]
    rows_out, (grad_heads, tall, flat, stacks) = refs[9 : 9 + n_head], refs[9 + n_head :]
    heads, width = big_probs.shape[:2]
    pairs, wide = small_probs.shape[1:3]
    narrow = wide // 2
    columns = qkv.shape[2]
    halves = width // LANES
    block = grads_in[0].shape[0]
    for r in range(n_head):
        grad_heads[peer_block(me, r, block), :] = grads_in[r][...]

    need(n_head + 3)

    def attend(span, all_probs, store):
        for head in range(heads):
            mine = head_lanes(head, columns)
            probs = all_probs(head)
            upper = jnp.where(mine, grad_heads[span, :], 0.0)
            size = upper.shape[0]
            grad_probs = dot(upper, qkv[2, span, :], NT)
            inner = jnp.sum(probs * grad_probs, axis=-1, keepdims=True)
            grad_scores = (probs * (grad_probs - inner)).astype(BF)
            rows = slice(head * size, (head + 1) * size)
            tall[0, rows, :size] = grad_scores
            tall[1, rows, :size] = probs.astype(BF)
            flat[:size, rows] = grad_scores
            stacks[0, rows, :] = jnp.where(mine, qkv[0, span, :], 0.0)
            stacks[1, rows, :] = jnp.where(mine, qkv[1, span, :], 0.0)
            stacks[2, rows, :] = upper
            store(head, grad_scores.astype(F32))
        every = slice(0, heads * size)
        dqkv[0, span, :] = (dot(flat[:size, every], stacks[1, every, :], NN) * SCALE).astype(BF)
        dqkv[1, span, :] = (dot(tall[0, every, :size], stacks[0, every, :], TN) * SCALE).astype(BF)
        dqkv[2, span, :] = dot(tall[1, every, :size], stacks[2, every, :], TN).astype(BF)

    for pair in range(pairs):

        def store_small(head, value, at=pair * narrow * SUB):
            small_rows[pl.ds(at + head, narrow, stride=SUB), :] = value[:narrow] + value[narrow:]

        span = slice(width + pair * wide, width + (pair + 1) * wide)
        attend(span, lambda head, pair=pair: small_probs[head, pair], store_small)
    done(0)

    def store_big(head, value):
        for half in range(halves):
            big_rows[pl.ds(half * width * SUB + head, width, stride=SUB), :] = value[
                :, LANES * half : LANES * (half + 1)
            ]

    attend(slice(0, width), lambda head: big_probs[head], store_big)
    done(1, 2)
    need(n_head + 4)
    column_sums[...] = jnp.zeros_like(column_sums)
    for i, k in enumerate((0, 2)):
        column_sums[i, pl.ds(me[0], 1), :] = jnp.sum(dqkv[k].astype(F32), axis=0, keepdims=True)
    for r in range(n_head):
        rows = peer_block(me, r, block)
        model = rows_out[r].shape[1]
        total = dot(dqkv[0, rows, :], attend_matrix(weights, 0, model), NT)
        total = total + dot(dqkv[1, rows, :], attend_matrix(weights, 1, model), NT)
        total = total + dot(dqkv[2, rows, :], attend_matrix(weights, 2, model), NT)
        rows_out[r][...] = total.astype(BF)


def middle_body(n_head, need, done, *refs):
    mixed, refs = refs[:n_head], refs[n_head:]
    me, rows, upper, vectors, hidden_bias = refs[:5]
    weights, refs = refs[5 : 5 + n_head], refs[5 + n_head :]
    layer_out, grad_hidden, sums, pre_sums, normed_grad, act_pre = refs[:6]
    grad_heads = refs[6:]
    need(*range(n_head + 5))
    columns = mixed[0].shape[1]
    slot = parcel_slot(columns)
    hidden = rows[...].astype(F32) + vectors[6:7, :]
    for r in range(n_head):
        need(n_head + 5 + r)
        hidden = hidden + dot(mixed[r][...], whole_matrix(weights[r], 0), NT)
    xhat, spread = norm_parts(hidden)
    low = (xhat * vectors[2:3, :] + vectors[3:4, :]).astype(BF)
    normed_grad[0] = low
    cotangent = upper[...]
    final = hidden + vectors[8:9, :]
    grad_normed = jnp.zeros_like(hidden)
    for r in range(n_head):
        peer = me[0] ^ r
        into, down = whole_matrix(weights[r], 1), whole_matrix(weights[r], 2)
        pre = dot(low, into, NN) + hidden_bias[pl.ds(peer, 1), :]
        phi = 0.5 * (1.0 + lax.erf(pre * (0.5**0.5)))
        active = (pre * phi).astype(BF)
        final = final + dot(active, down, NT)
        slope = phi + pre * jnp.exp(-0.5 * pre * pre) * (0.5 / jnp.pi) ** 0.5
        low_grad = (dot(cotangent, down, NN) * slope).astype(BF)
        pre_sums[pl.ds(peer, 1), :] = jnp.sum(low_grad.astype(F32), axis=0, keepdims=True)
        grad_normed = grad_normed + dot(low_grad, into, NT)
        act_pre[peer, :, 0:columns] = active
        act_pre[peer, :, slot : slot + columns] = low_grad
    layer_out[...] = final.astype(BF)
    wide = cotangent.astype(F32)
    grad = wide + norm_back(grad_normed * vectors[2:3, :], xhat, spread)
    grad_hidden[...] = grad
    grad_small = grad.astype(BF)
    normed_grad[1] = grad_small
    for r in range(n_head):
        grad_heads[r][...] = dot(grad_small, whole_matrix(weights[r], 0), NN).astype(BF)
    sums[0:1, :] = jnp.sum(grad_normed * xhat, axis=0, keepdims=True)
    sums[1:2, :] = jnp.sum(grad_normed, axis=0, keepdims=True)
    sums[2:3, :] = jnp.sum(grad, axis=0, keepdims=True)
    sums[3:4, :] = jnp.sum(wide, axis=0, keepdims=True)


def parcel_slot(columns):
    return (columns + LANES - 1) // LANES * LANES


def weight_grads_body(n_head, need, done, *refs):
    given, mixed, refs = refs[:n_head], refs[n_head : 2 * n_head], refs[2 * n_head :]
    me, act_pre, normed_one, dqkv = refs[:4]
    normed_grad, out = refs[4 : 4 + n_head], refs[-1]
    columns = mixed[0].shape[1]
    slot = parcel_slot(columns)

    def all_rows(pick):
        return jnp.concatenate([pick(me[0] ^ r) for r in range(n_head)], axis=0)

    need(2 * n_head + 2, 2 * n_head + 3)
    for k in range(3):
        put_matrix(out, k, dot(normed_one[...], dqkv[k], TN).astype(BF))
    need(*range(2 * n_head), 2 * n_head + 1, *range(2 * n_head + 4, 3 * n_head + 4))
    heads_out = jnp.concatenate([m[...] for m in mixed], axis=0)
    put_matrix(out, 3, dot(jnp.concatenate([n[1] for n in normed_grad], axis=0), heads_out, TN).astype(BF))
    grad_pre = all_rows(lambda p: act_pre[p, :, slot : slot + columns])
    put_matrix(out, 4, dot(jnp.concatenate([n[0] for n in normed_grad], axis=0), grad_pre, TN).astype(BF))
    cotangent = jnp.concatenate([g[1] for g in given], axis=0)
    put_matrix(out, 5, dot(cotangent, all_rows(lambda p: act_pre[p, :, 0:columns]), TN).astype(BF))


def merge_body(need, done, *refs):
    parts, out = refs[:-1], refs[-1]
    need(*range(len(parts)))
    value = parts[0][...].astype(F32)
    for part in parts[1:]:
        value = value + part[...].astype(F32)
    out[...] = value.astype(BF)


def input_body(n_head, n_vectors, need, done, *refs):
    parts, refs = refs[:n_head], refs[n_head:]
    me, rows, grad_hidden, vectors, sums, column_sums, pre_sums, input_grad, vector_rows, terms = refs
    need(*range(n_head), *range(n_head + 1, n_head + 7))
    grad_normed = parts[0][...].astype(F32)
    for part in parts[1:]:
        grad_normed = grad_normed + part[...].astype(F32)
    xhat, spread = norm_parts(rows[...].astype(F32))
    input_grad[...] = (grad_hidden[...] + norm_back(grad_normed * vectors[0:1, :], xhat, spread)).astype(BF)
    done(0)
    columns = column_sums.shape[2]
    terms[...] = jnp.zeros_like(terms)
    terms[0:1, :] = jnp.sum(grad_normed * xhat, axis=0, keepdims=True)
    terms[1:2, :] = jnp.sum(grad_normed, axis=0, keepdims=True)
    terms[2:4, :] = sums[0:2, :]
    terms[6:7, :] = sums[2:3, :]
    terms[8:9, :] = sums[3:4, :]
    for j in range(n_head):
        span = slice(j * columns, (j + 1) * columns)
        for i in range(2):
            terms[4 + i : 5 + i, span] = column_sums[i, j : j + 1, :]
        terms[7:8, span] = pre_sums[j : j + 1, :]
    inner, outer = vector_rows.shape[:2]
    lanes = vectors.shape[1] // (inner * outer)
    vector_rows[...] = jnp.zeros_like(vector_rows)
    for d in range(inner * outer):
        at = me[1] ^ d
        vector_rows[at % inner, at // inner, :, 0:lanes] = terms[:, d * lanes : (d + 1) * lanes].astype(BF)


def adamw_update(weight, first_moment, second_moment, gradient, learn_rate):
    first_new = BETA_FIRST * first_moment + (1.0 - BETA_FIRST) * gradient
    second_new = BETA_SECOND * second_moment + (1.0 - BETA_SECOND) * gradient * gradient
    first_hat = first_new / (1.0 - BETA_FIRST**ADAM_STEP)
    second_hat = second_new / (1.0 - BETA_SECOND**ADAM_STEP)
    weight_new = weight - learn_rate * (
        first_hat / (jnp.sqrt(second_hat) + ADAM_EPSILON) + WEIGHT_DECAY * weight
    )
    return (weight_new, first_new, second_new)


def told_body(need, done, arrived, *refs):
    parts, (shards, shard, told) = refs[:-3], refs[-3:]
    need(0)
    rest = arrived[0].astype(F32)
    for d in range(1, arrived.shape[0]):
        rest = rest + arrived[d].astype(F32)
    columns = shards.shape[2]
    for k in range(shards.shape[0]):
        shards[k] = rest[k // 2, :, k % 2 * columns : (k % 2 + 1) * columns]
    done(0)
    need(*range(1, len(parts) + 1))
    value = parts[0][...].astype(F32)
    for part in parts[1:]:
        value = value + part[...].astype(F32)
    table = value[VECTOR_ROWS:]
    shard[...] = table
    here = jnp.sum(table * table).reshape(1, 1) + jnp.sum(rest * rest).reshape(1, 1)
    tail = value[MESSAGE_ROWS : MESSAGE_ROWS + 1]
    free = LANES // 4
    gap = jnp.zeros((1, LANES - free), F32)
    spill = [jnp.concatenate([gap, tail[:, q * free : (q + 1) * free]], axis=1) for q in range(3)]
    spill = jnp.concatenate(spill + [jnp.zeros((MESSAGE_ROWS - 3, LANES), F32)], axis=0)
    message = jnp.where(corner_mask(), here, value[:MESSAGE_ROWS] + spill)
    told[...] = jnp.broadcast_to(message[None], told.shape)


def corner_mask():
    row = lax.broadcasted_iota(jnp.int32, (MESSAGE_ROWS, LANES), 0)
    lane = lax.broadcasted_iota(jnp.int32, (MESSAGE_ROWS, LANES), 1)
    return (row == MESSAGE_ROWS - 1) & (lane == LANES - 1)


def update_body(n_head, n_vectors, need, done, *refs):
    need(1)
    me, told, shards, out_shard, down_shard, table_shard = refs[:6]
    params, outs = refs[6:21], refs[21:36]
    norm_out = refs[36]
    n_dp = told.shape[0] // n_head

    def merged(d):
        value = told[d * n_head]
        for j in range(1, n_head):
            value = value + told[d * n_head + j]
        return value

    corner = corner_mask()

    def square(d, total):
        value = merged(d)
        return total + jnp.where(corner, value, value * value)

    total = lax.fori_loop(0, n_dp, square, jnp.zeros((MESSAGE_ROWS, LANES), F32))
    grad_norm = jnp.sqrt(jnp.sum(total).reshape(1, 1))
    norm_out[...] = jnp.broadcast_to(grad_norm, norm_out.shape)
    factor = CLIP_NORM / jnp.maximum(grad_norm, CLIP_NORM)

    def update(at, gradient, rate, pick=...):
        weight, first, second = (ref[pick] for ref in params[3 * at : 3 * at + 3])
        for ref, value in zip(outs[3 * at : 3 * at + 3], adamw_update(weight, first, second, gradient * factor, rate)):
            ref[pick] = value

    for k in range(3):
        update(0, shards[k], RATE_MATRIX, k)
    update(0, shards[4], RATE_MATRIX, 3)
    update(1, out_shard[...], RATE_OUTPUT)
    update(2, down_shard[...], RATE_MATRIX)
    mine, free = merged(me[1]), LANES // 4
    tail = jnp.concatenate([mine[q : q + 1, LANES - free :] for q in range(3)], axis=1)
    mine = jnp.concatenate([mine[:, : LANES - free], tail], axis=0)
    size = params[9].shape[1]
    gradient = jnp.zeros((n_vectors, size), F32)
    for j in range(n_head):
        gradient = jnp.where(me[0] == j, mine[:n_vectors, j * size : (j + 1) * size], gradient)
    update(3, gradient, RATE_VECTOR)
    heads = params[12].shape[0]
    for c in range(table_shard.shape[0] // heads):
        update(4, table_shard[c * heads : (c + 1) * heads, :], RATE_VECTOR, (slice(None), slice(c * LANES, (c + 1) * LANES)))


def exchange(value, axis):
    return lax.all_to_all(value, axis, split_axis=0, concat_axis=0, tiled=True)


def spread_all(value, axis):
    size = lax.axis_size(axis)
    return exchange(jnp.broadcast_to(value[None], (size, *value.shape)), axis)


def swap(values, n_head):
    return [values[0]] + [
        lax.ppermute(values[r], "head", [(i, i ^ r) for i in range(n_head)]) for r in range(1, n_head)
    ]


def struct(shape, dtype):
    return jax.ShapeDtypeStruct(shape, dtype)


def on_device(
    node_rows,
    output_grad,
    weight_in,
    first_in,
    second_in,
    weight_out,
    first_out,
    second_out,
    weight_down,
    first_down,
    second_down,
    vectors,
    first_vectors,
    second_vectors,
    bias_table,
    first_table,
    second_table,
    big_counts,
    small_counts,
    big_distance,
    small_distance,
    big_paths,
    small_paths,
    big_lengths,
    small_lengths,
):
    everyone = ("dp", "head")
    n_dp, n_head = lax.axis_size("dp"), lax.axis_size("head")
    head_index, dp_index = lax.axis_index("head"), lax.axis_index("dp")
    me = head_index.reshape(1).astype(jnp.int32)
    shard_rows, columns = weight_in.shape[1], weight_in.shape[2]
    model = shard_rows * n_dp
    my_rows = node_rows.shape[0]
    group_rows = my_rows * n_head
    heads = columns // HEAD_DIM
    width, narrow = big_distance.shape[1], small_distance.shape[1]
    pairs = small_distance.shape[0] // 2
    table_chunks = bias_table.shape[0] // LANES
    all_chunks = table_chunks * n_dp
    n_vectors, shard_width = vectors.shape
    stacked = shard_rows % 16 == 0
    big_ints = (big_distance, big_paths, big_lengths)
    small_ints = (small_distance, small_paths, small_lengths)
    inner = inner_of(n_dp)
    outer = n_dp // inner
    dp_pairs = lambda k: [(i, i ^ k) for i in range(n_dp)]
    us = jnp.stack([head_index, dp_index]).astype(jnp.int32)
    lanes_used = model // n_dp

    def far_shards(value):
        return [value] + [lax.ppermute(value, "dp", dp_pairs(k)) for k in range(inner, n_dp, inner)]

    def near_shards(values):
        value = jnp.stack(values)
        return [value] + [lax.ppermute(value, "dp", dp_pairs(k)) for k in range(1, inner)]

    def to_head(value, r):
        return lax.ppermute(value, "head", [(i, i ^ r) for i in range(n_head)])

    far = n_head // 2
    near_heads = range(1, far)

    rest_sent = jnp.stack([weight_out.astype(BF).T, weight_in[3].astype(BF), weight_down.astype(BF).T])
    rest_sent, my_table = lax.optimization_barrier((rest_sent, bias_table))
    with jax.named_scope("rest_far"):
        rest_far = far_shards(rest_sent)
    table_sent = my_table.astype(BF).T.reshape(heads, table_chunks, LANES).transpose(1, 0, 2)
    with jax.named_scope("table_all"):
        table_all = spread_all(table_sent, "dp").reshape(all_chunks * heads, LANES)
    given = {0: jnp.stack([node_rows, output_grad])}
    with jax.named_scope("rows_far"):
        given[far] = to_head(given[0], far)
    qkv_sent = weight_in[:3].astype(BF)
    with jax.named_scope("vectors_head"):
        own_vectors = lax.dynamic_update_slice_in_dim(
            jnp.zeros((n_vectors, lanes_used), F32), vectors, head_index * shard_width, 1
        )
        step = far
        while step:
            own_vectors = own_vectors + to_head(own_vectors, step)
            step //= 2
    rest, pieces = own_vectors, []
    for _ in range(PIECES):
        piece = lax.reduce_precision(rest, 8, 7)
        rest = rest - piece
        pieces.append(jnp.pad(piece.astype(BF), ((0, PIECE_ROWS - n_vectors), (0, columns - lanes_used))))
    qkv_sent = jnp.concatenate([qkv_sent.reshape(3 * shard_rows, columns), *pieces])
    qkv_sent, *rest_far = lax.optimization_barrier((qkv_sent, *rest_far))
    with jax.named_scope("rest_near"):
        rest_near = near_shards(rest_far)
    with jax.named_scope("qkv_far"):
        qkv_far = far_shards(qkv_sent)

    def pair_bias(part, table, ints):
        rows = width // sum(BIG_QUARTERS) * BIG_QUARTERS[part]
        big_range = struct((heads, width // LANES, rows, LANES), F32)
        return kernel_call(
            lambda *refs: bias_body(part, *refs),
            ([struct((heads, pairs, narrow, LANES), F32)] if part == 0 else []) + [big_range],
            "pair_bias",
            12 if part == 0 else 20,
            (table, *ints),
            [
                pltpu.VMEM((heads, all_chunks // 2, SUB, LANES), jnp.int32),
                pltpu.VMEM((len(PRODUCTS), max(CHUNKS) * heads, LANES), BF),
                pltpu.VMEM((len(PRODUCTS), heads * SUB, LANES), F32),
            ],
        )

    small_bias, *big_bias = pair_bias(0, table_all, (*small_ints, *big_ints))
    held = lax.optimization_barrier((small_bias, table_all, given[far], *rest_near, *qkv_far))
    (small_bias, table_all, given[far]), held = held[:3], held[3:]
    rest_near, qkv_far = held[:inner], held[inner:]
    weights_rest = jnp.concatenate(rest_near)
    with jax.named_scope("qkv_near"):
        qkv_near = near_shards(qkv_far)
    if not stacked:
        order = jnp.argsort(jnp.array(xor_order(n_dp), jnp.int32) ^ dp_index)
        weights_rest = weights_rest[order].transpose(1, 0, 2, 3).reshape(3, model, columns)
    weights_held = {0: weights_rest}
    with jax.named_scope("rest_far_head"):
        weights_held[far] = to_head(weights_rest, far)
    with jax.named_scope("rows_near"):
        for r in near_heads:
            given[r], given[far + r] = to_head(given[0], r), to_head(given[far], r)
    for part in range(1, BIG_PARTS):
        big_bias += pair_bias(part, table_all, big_ints)
    held = lax.optimization_barrier((big_bias[-1], *qkv_near, *[given[r] for r in range(n_head)]))
    big_bias[-1], qkv_near, given = held[0], held[1 : 1 + inner], held[1 + inner :]
    with jax.named_scope("rest_near_head"):
        for r in near_heads:
            weights_held[r] = to_head(weights_held[0], r)
    weights_attend = list(qkv_near)
    vector_row, vector_pieces = 3 * shard_rows, ()
    if not stacked:
        weights_attend = jnp.concatenate(qkv_near)[order]
        vector_row, vector_pieces = 0, (weights_attend[:, 3 * shard_rows :],)
        weights_attend = weights_attend[:, : 3 * shard_rows].reshape(n_dp, 3, shard_rows, columns)
        weights_attend = weights_attend.transpose(1, 0, 2, 3).reshape(3, model, columns)

    block = struct((my_rows, columns), BF)
    rows_block = struct((my_rows, model), BF)
    normed_one, qkv, big_probs, small_probs, all_vectors, hidden_bias, *mixed = kernel_call(
        lambda *refs: forward_body(n_head, vector_row, *refs),
        [
            struct((group_rows, model), BF),
            struct((3, group_rows, columns), BF),
            struct((heads, width, width), F32),
            struct((heads, pairs, 2 * narrow, 2 * narrow), F32),
            struct((n_vectors, model), F32),
            struct((n_head, columns), F32),
            *[block] * n_head,
        ],
        "attend_forward",
        12,
        (*given, us, big_counts, small_counts, weights_attend, small_bias, *big_bias, *vector_pieces),
        [
            pltpu.VMEM((group_rows, columns), BF),
            pltpu.VMEM((width, heads * width), BF),
            pltpu.VMEM((heads * width, columns), BF),
        ],
        range(n_head, n_head + 3),
        (n_head + 3,) if stacked else (),
        n_head,
    )
    with jax.named_scope("mixed_rows"):
        mixed_rows = swap(mixed, n_head)
    mixed_rows[0], *held = lax.optimization_barrier((mixed_rows[0], *[weights_held[r] for r in range(far + 1)]))
    weights_held.update(enumerate(held))
    with jax.named_scope("rest_near_head"):
        for r in near_heads:
            weights_held[far + r] = to_head(weights_held[far], r)
    weights_rest = [weights_held[r] for r in range(n_head)]

    layer_out, grad_hidden, sums, pre_sums, normed_grad, act_pre, *grad_heads = kernel_call(
        lambda *refs: middle_body(n_head, *refs),
        [
            rows_block,
            struct((my_rows, model), F32),
            struct((4, model), F32),
            struct((n_head, columns), F32),
            struct((2, my_rows, model), BF),
            struct((n_head, my_rows, 2 * parcel_slot(columns)), BF),
            *[block] * n_head,
        ],
        "feed_forward",
        6,
        (*mixed_rows, us, node_rows, output_grad, all_vectors, hidden_bias, *weights_rest),
        (),
        (n_head,),
        range(n_head + 5, 2 * n_head + 5) if stacked else (),
        n_head,
    )
    with jax.named_scope("grad_heads"):
        grad_heads = swap(grad_heads, n_head)
    with jax.named_scope("act_pre"):
        act_pre = exchange(act_pre, "head")
    with jax.named_scope("normed_grad"):
        rows_held = {0: normed_grad}
        for r in (far, *range(1, far)):
            rows_held[r] = lax.ppermute(normed_grad, "head", [(i, i ^ r) for i in range(n_head)])

    small_rows, big_rows, dqkv, column_sums, *rows_sent = kernel_call(
        lambda *refs: backward_body(n_head, *refs),
        [
            struct((pairs * narrow * SUB, LANES), F32),
            struct((width // LANES * width * SUB, LANES), F32),
            struct((3, group_rows, columns), BF),
            struct((2, n_head, columns), F32),
            *[rows_block] * n_head,
        ],
        "attend_backward",
        14,
        (*grad_heads, us, qkv, small_probs, big_probs, weights_attend),
        [
            pltpu.VMEM((group_rows, columns), BF),
            pltpu.VMEM((2, heads * width, width), BF),
            pltpu.VMEM((width, heads * width), BF),
            pltpu.VMEM((3, heads * width, columns), BF),
        ],
        (n_head,),
        (n_head + 4,) if stacked else (),
        n_head,
    )
    small_rows, *arrived = lax.optimization_barrier((small_rows, *[rows_held[r] for r in range(1, far + 1)]))
    rows_held.update(zip(range(1, far + 1), arrived))
    with jax.named_scope("normed_grad"):
        for r in range(1, far):
            rows_held[far + r] = lax.ppermute(rows_held[far], "head", [(i, i ^ r) for i in range(n_head)])
    (weight_grads,) = kernel_call(
        lambda *refs: weight_grads_body(n_head, *refs),
        [struct((n_dp, 3, shard_rows, 2 * columns) if stacked else (6, model, columns), BF)],
        "weight_grads",
        6,
        (*given, *mixed, us, act_pre, normed_one, dqkv, *[rows_held[r] for r in range(n_head)]),
        (),
        (2 * n_head,),
        early=(2 * n_head + 2, 2 * n_head + 3),
    )
    if not stacked:
        weight_grads = weight_grads.reshape(3, 2, n_dp, shard_rows, columns).transpose(2, 0, 3, 1, 4)
        weight_grads = weight_grads.reshape(n_dp, 3, shard_rows, 2 * columns)
    with jax.named_scope("grad_normed_one"):
        rows_back = swap(rows_sent, n_head)
    _, *rows_back = lax.optimization_barrier((weight_grads, *rows_back))
    with jax.named_scope("weight_grads"):
        weights_arrived = exchange(weight_grads, "dp")
    input_grad, vector_rows = kernel_call(
        lambda *refs: input_body(n_head, n_vectors, *refs),
        [rows_block, struct((inner, outer, VECTOR_ROWS, LANES), BF)],
        "input_grad",
        3,
        (*rows_back, us, node_rows, grad_hidden, all_vectors, sums, column_sums, pre_sums),
        [pltpu.VMEM((VECTOR_ROWS, model), F32)],
        (n_head,),
    )
    table_rows = table_chunks * heads
    block = struct((outer, VECTOR_ROWS + table_rows, LANES), BF)
    inner_sent = kernel_call(
        scatter_body,
        [(inner, block)],
        "table_scatter",
        40,
        (small_rows, *small_ints, big_rows, *big_ints, us, vector_rows),
        [pltpu.VMEM((LOOKUPS, SPLIT, SUB * max(HIGHS)), F32)],
        (8,),
    )
    with jax.named_scope("table_inner"):
        arrived = [inner_sent[0]] + [lax.ppermute(inner_sent[k], "dp", dp_pairs(k)) for k in range(1, inner)]
    outer_sent = kernel_call(
        merge_body,
        [(outer, struct(block.shape[1:], BF))],
        "merge_table",
        1,
        tuple(arrived),
    )
    with jax.named_scope("table_outer"):
        parts = [outer_sent[0]] + [
            lax.ppermute(outer_sent[k], "dp", dp_pairs(k * inner)) for k in range(1, outer)
        ]
    weights_arrived, *parts = lax.optimization_barrier((weights_arrived, *parts))
    shards, table_shard, told = kernel_call(
        told_body,
        [
            struct((6, shard_rows, columns), F32),
            struct((table_rows, LANES), F32),
            struct((n_dp * n_head, MESSAGE_ROWS, LANES), F32),
        ],
        "shard_sums",
        4,
        (weights_arrived, *parts),
    )
    with jax.named_scope("squares"):
        told = exchange(told, everyone)
    params = (weight_in, first_in, second_in, weight_out, first_out, second_out)
    params += (weight_down, first_down, second_down, vectors, first_vectors, second_vectors)
    params += (bias_table.T, first_table.T, second_table.T)
    *updated, grad_norm = kernel_call(
        lambda *refs: update_body(n_head, n_vectors, *refs),
        [*[struct(p.shape, F32) for p in params], struct((1, LANES), F32)],
        "update",
        3,
        (us, told, shards, shards[3].T, shards[5].T, table_shard, *params),
        (),
        (0,),
        ready=range(2, 21),
        limit=16 << 20,
    )
    updated = updated[:12] + [value.T for value in updated[12:]]
    return (layer_out, input_grad, grad_norm[0, 0], *updated)


def solution(mesh):
    rows = P(("dp", "head"), None)
    square = P(None, "dp", "head")
    across = P("head", "dp")
    thin = P(None, ("dp", "head"))
    table = P("dp", "head")
    return jax.shard_map(
        on_device,
        mesh=mesh,
        in_specs=(rows, rows)
        + (square,) * 3
        + (across,) * 6
        + (thin,) * 3
        + (table,) * 3
        + (P("dp"), P("dp", None))
        + (P("dp", None, None),) * 2
        + (P(None, "dp", None, None),) * 2
        + (P("dp", None, None),) * 2,
        out_specs=(rows, rows, P()) + (square,) * 3 + (across,) * 6 + (thin,) * 3 + (table,) * 3,
        check_vma=False,
    )
```

```python
import jax
import jax.numpy as jnp
from jax import lax
from jax.experimental import pallas as pl
from jax.experimental.pallas import tpu as pltpu
from jax.sharding import PartitionSpec as P

HEAD_DIM = 24
NDIST = 512
NTYPE = 1536
STEPS = 5
ADAM_STEP = 10

NORM_EPSILON = 1e-05
NEGATIVE_FILL = -1e30
BETA_FIRST = 0.9
BETA_SECOND = 0.95
ADAM_EPSILON = 1e-08
RATE_MATRIX = 0.02
RATE_OUTPUT = 0.05
RATE_VECTOR = 0.15
WEIGHT_DECAY = 0.01
CLIP_NORM = 1.0

LANES = 128
SUB = 8
FIRST = [0] + [(NDIST + n * NTYPE) // LANES for n in range(STEPS)]
CHUNKS = [NDIST // LANES] + [NTYPE // LANES] * STEPS
LOOKUPS = STEPS + 1
VECTOR_ROWS = 16
BIG_QUARTERS = (1, 3)
BIG_PARTS = len(BIG_QUARTERS)
MESSAGE_ROWS = 8
PRODUCTS = (STEPS - 1, STEPS)
PIECES = 3
PIECE_ROWS = 16
FIXED = 8192.0
SPLIT = 112
SPLIT_RECIPROCAL, SPLIT_SHIFT = 4682, 19
HIGHS = [-(-(n * LANES) // (2 * SPLIT)) * 2 for n in CHUNKS]
NOWHERE = 4095
SCALE = HEAD_DIM**-0.5
BF = jnp.bfloat16
F32 = jnp.float32
VMEM_BYTES = 56 << 20

NN = (((1,), (0,)), ((), ()))
NT = (((1,), (1,)), ((), ()))
TN = (((0,), (0,)), ((), ()))


def dot(left, right, dims):
    return lax.dot_general(left, right, dims, preferred_element_type=F32)


def inner_of(size):
    return 1 << ((size.bit_length() - 1) // 2)


def xor_order(size):
    inner = inner_of(size)
    return [a * inner + b for b in range(inner) for a in range(size // inner)]


def kernel_call(body, outs, name, micros, args, scratch=(), smem_in=(), placed=(), us_at=None, ready=(), limit=VMEM_BYTES, early=()):
    groups = [arg if isinstance(arg, list) else [arg] for arg in args]
    args = [struct((sum(a.shape[0] for a in g), *g[0].shape[1:]), g[0].dtype) if len(g) > 1 else g[0] for g in groups]
    starts = [sum(len(g) for g in groups[:i]) for i in range(len(groups) + 1)]
    n_in, n_out = len(args), len(outs)
    moved = [i for i in range(n_in) if i not in smem_in and i not in ready]
    blocks = [out[0] if isinstance(out, tuple) else 0 for out in outs]
    shapes = [out[1] if isinstance(out, tuple) else out for out in outs]
    flat = [(i, k) for i in range(n_out) for k in range(max(blocks[i], 1))]
    n_sems = sum(args[i].shape[0] if i in placed else 1 for i in moved)

    def wrapped(*refs):
        parts = [refs[starts[i] : starts[i + 1]] for i in range(n_in)]
        given, results = [p[0] for p in parts], refs[starts[-1] : starts[-1] + len(flat)]
        refs = refs[starts[-1] + len(flat) :]
        held = dict(zip(moved, refs))
        made, refs = refs[len(moved) : len(moved) + n_out], refs[len(moved) + n_out :]
        rest, (in_sems, out_sems) = refs[:-2], refs[-2:]
        arriving, sem = {}, 0
        for i in moved:
            pieces = [(given[i], held[i])]
            if i in placed:
                size = args[i].shape[0]
                each = size // len(parts[i])
                pieces = [
                    (parts[i][k // each].at[k % each], held[i].at[given[us_at][1] ^ other])
                    for k, other in enumerate(xor_order(size))
                ]
            arriving[i] = [pltpu.make_async_copy(a, b, in_sems.at[sem + n]) for n, (a, b) in enumerate(pieces)]
            sem += len(pieces)
        leaving = [
            pltpu.make_async_copy(made[i].at[k] if blocks[i] else made[i], results[at], out_sems.at[at])
            for at, (i, k) in enumerate(flat)
        ]
        for i in [*early, *[i for i in moved if i not in early]]:
            for copy in arriving[i]:
                copy.start()
        waiting, unsent = list(moved), list(range(n_out))

        def need(*which):
            for i in which:
                if i in waiting:
                    waiting.remove(i)
                    for copy in arriving[i]:
                        copy.wait()

        def done(*which):
            for i in which:
                if i in unsent:
                    unsent.remove(i)
                    for at, (j, _) in enumerate(flat):
                        if i == j:
                            leaving[at].start()

        body(need, done, *[held.get(i, given[i]) for i in range(n_in)], *made, *rest)
        need(*moved)
        done(*range(n_out))
        for copy in leaving:
            copy.wait()

    anywhere, smem = pl.BlockSpec(memory_space=pl.ANY), pl.BlockSpec(memory_space=pltpu.SMEM)
    vmem = pl.BlockSpec(memory_space=pltpu.VMEM)
    return pl.pallas_call(
        wrapped,
        out_shape=tuple(shapes[i] for i, _ in flat),
        in_specs=[
            smem if i in smem_in else vmem if i in ready else anywhere for i in range(n_in) for _ in groups[i]
        ],
        out_specs=tuple([anywhere] * len(flat)),
        scratch_shapes=[pltpu.VMEM(args[i].shape, args[i].dtype) for i in moved]
        + [pltpu.VMEM((n, *o.shape) if n else o.shape, o.dtype) for n, o in zip(blocks, shapes)]
        + list(scratch)
        + [pltpu.SemaphoreType.DMA((n_sems,)), pltpu.SemaphoreType.DMA((len(flat),))],
        name=name,
        compiler_params=pltpu.CompilerParams(vmem_limit_bytes=limit),
        cost_estimate=pl.CostEstimate(flops=int(micros * 1e9), bytes_accessed=1 << 20, transcendentals=0),
    )(*[part for group in groups for part in group])


def big_block(refs, block, half):
    distance, paths, lengths = refs
    rows, lanes = pl.ds(SUB * block, SUB), slice(LANES * half, LANES * half + LANES)
    return [distance[0, rows, lanes]] + [paths[n, 0, rows, lanes] for n in range(STEPS)], lengths[0, rows, lanes]


def small_block(refs, block, pair):
    distance, paths, lengths = refs
    rows = pl.ds(SUB * block, SUB)

    def two(ref, *lead):
        return jnp.concatenate([ref[(*lead, 2 * pair, rows)], ref[(*lead, 2 * pair + 1, rows)]], axis=1)

    return [two(distance)] + [two(paths, n) for n in range(STEPS)], two(lengths)


def each_block(load, refs, first, count, sides, group, step):
    def some(at, carry):
        blocks = [first + at * group + u for u in range(group)]
        step([(*load(refs, block, side), block, side) for block in blocks for side in range(sides)])
        return carry

    lax.fori_loop(0, count // group, some, 0)


def pick(items, high):
    bit = 1
    while len(items) > 1:
        odd = (high & bit) != 0
        items = [
            jnp.where(odd, items[k + 1], items[k]) if k + 1 < len(items) else items[k]
            for k in range(0, len(items), 2)
        ]
        bit *= 2
    return items[0]


def bias_body(part, need, done, table, *refs):
    small, refs = (refs[:3], refs[3:]) if part == 0 else (None, refs)
    big, outs, (words, rows_of, found_rows) = refs[:3], refs[3:-3], refs[-3:]
    need(0)
    heads, count = words.shape[:2]
    for k in range(count):
        low = jnp.round(table[SUB * 2 * k : SUB * (2 * k + 1), :].astype(F32) * FIXED).astype(jnp.int32)
        high = jnp.round(table[SUB * (2 * k + 1) : SUB * (2 * k + 2), :].astype(F32) * FIXED).astype(jnp.int32)
        word = (high << 16) | (low & 0xFFFF)
        for h in range(heads):
            words[h, k] = jnp.broadcast_to(word[h : h + 1], (SUB, LANES))

    for i, t in enumerate(PRODUCTS):
        rows_of[i] = table[SUB * FIRST[t] : SUB * (FIRST[t] + CHUNKS[t]), :]
    sub = lax.broadcasted_iota(jnp.int32, (2 * SUB, LANES), 0)
    patterns = [(sub + 2 * SUB * k).astype(F32).astype(BF) for k in range(LANES // (2 * SUB))]
    zero, one = jnp.zeros((2 * SUB, LANES), BF), jnp.ones((2 * SUB, LANES), BF)

    def product(i, code):
        spread = [jnp.broadcast_to(code[s : s + 1], (SUB, LANES)) for s in range(SUB)]
        hot = []
        for s in range(SUB):
            low = (spread[s] & (LANES - 1)).astype(F32)
            low = jnp.concatenate([low, low], axis=0).astype(BF)
            hot.append(jnp.concatenate([jnp.where(low == p, one, zero) for p in patterns], axis=0))
        values = dot(rows_of[i], jnp.concatenate(hot, axis=1), NN)
        for s in range(SUB):
            lanes = slice(LANES * s, LANES * (s + 1))
            items = [values[heads * c : heads * (c + 1), lanes] for c in range(values.shape[0] // heads)]
            found_rows[i, pl.ds(s, heads, stride=SUB), :] = pick(items, spread[s] >> 7)

    def step(store):
        def run(parts):
            for index, lengths, block, side in parts:
                share = 1.0 / lengths.astype(F32)
                first, edges = [None] * heads, [None] * heads
                for i, t in enumerate(PRODUCTS):
                    product(i, index[t])
                for t in range(LOOKUPS):
                    if t in PRODUCTS:
                        continue
                    code = index[t]
                    lane = code & (LANES - 1)
                    odd = [(code & bit) != 0 for bit in (256, 512, 1024)]
                    shift = ((code >> 3) & 16) ^ 16
                    live = lengths > t - 1
                    for h in range(heads):
                        found = [
                            jnp.take_along_axis(words[h, FIRST[t] // 2 + k], lane, axis=1, mode="promise_in_bounds")
                            for k in range(CHUNKS[t] // 2)
                        ]
                        level = 0
                        while len(found) > 1:
                            found = [
                                jnp.where(odd[level], found[k + 1], found[k]) if k + 1 < len(found) else found[k]
                                for k in range(0, len(found), 2)
                            ]
                            level += 1
                        value = (found[0] << shift) >> 16
                        if t == 0:
                            first[h] = value
                        else:
                            value = jnp.where(live, value, 0)
                            edges[h] = value if edges[h] is None else edges[h] + value
                for h in range(heads):
                    edge = edges[h].astype(F32) * (1.0 / FIXED)
                    for i, t in enumerate(PRODUCTS):
                        edge = edge + jnp.where(lengths > t - 1, found_rows[i, SUB * h : SUB * (h + 1), :], 0.0)
                    store(h, side, block, first[h].astype(F32) * (1.0 / FIXED) + edge * share)

        return run

    if small:

        def store_small(h, side, block, value):
            outs[0][h, side, pl.ds(SUB * block, SUB), :] = value

        need(1, 2, 3)
        each_block(small_block, small, 0, small[0].shape[1] // SUB, small[0].shape[0] // 2, 1, step(store_small))
        done(0)
    need(*range(1, 7 if small else 4))
    out = outs[-1]
    count = out.shape[2] // SUB
    first_block = big[0].shape[1] // SUB // sum(BIG_QUARTERS) * sum(BIG_QUARTERS[:part])

    def store_big(h, side, block, value):
        out[h, side, pl.ds(SUB * (block - first_block), SUB), :] = value

    each_block(big_block, big, first_block, count, big[0].shape[2] // LANES, 1, step(store_big))


def scatter_body(need, done, small_grads, sd, sp, sl, big_grads, bd, bp, bl, me, vector_rows, parcel, total):
    total[...] = jnp.zeros_like(total)
    sub = lax.broadcasted_iota(jnp.int32, (2 * SUB, LANES), 0)
    low_pattern = [(sub + 2 * SUB * k).astype(F32).astype(BF) for k in range(SPLIT // (2 * SUB))]
    upper = (sub >= SUB).astype(jnp.int32)
    high_pattern = [(2 * k + upper).astype(F32).astype(BF) for k in range(max(HIGHS) // 2)]
    zero, one = jnp.zeros((2 * SUB, LANES), BF), jnp.ones((2 * SUB, LANES), BF)

    def twice(value):
        return jnp.concatenate([value, value], axis=0).astype(BF)

    def step(grads, side_rows):
        def run(parts):
            whole, shared = [], []
            for index, lengths, block, side in parts:
                inverse = 1.0 / lengths.astype(F32)
                for s in range(SUB):
                    g = grads[pl.ds((side * side_rows + SUB * block + s) * SUB, SUB), :]
                    whole.append(twice(g))
                    shared.append(twice(g * jnp.broadcast_to(inverse[s : s + 1], (SUB, LANES))))
            for t in range(LOOKUPS):
                left, right = [], []
                for part, (index, lengths, _, _) in enumerate(parts):
                    high = index[t] * SPLIT_RECIPROCAL >> SPLIT_SHIFT
                    code = (high << 7) | (index[t] - high * SPLIT)
                    if t > 0:
                        code = jnp.where(lengths > t - 1, code, NOWHERE)
                    for s in range(SUB):
                        spread = jnp.broadcast_to(code[s : s + 1], (SUB, LANES))
                        low = twice((spread & (LANES - 1)).astype(F32))
                        high = twice((spread >> 7).astype(F32))
                        source = (whole if t == 0 else shared)[SUB * part + s]
                        left.append(jnp.concatenate([jnp.where(low == p, one, zero) for p in low_pattern], axis=0))
                        right.append(
                            jnp.concatenate(
                                [jnp.where(high == p, source, zero) for p in high_pattern[: HIGHS[t] // 2]], axis=0
                            )
                        )
                span = slice(0, SUB * HIGHS[t])
                total[t, :, span] += dot(jnp.concatenate(left, axis=1), jnp.concatenate(right, axis=1), NT)

        return run

    need(0, 1, 2, 3)
    narrow, width = sd.shape[1], bd.shape[1]
    each_block(small_block, (sd, sp, sl), 0, narrow // SUB, sd.shape[0] // 2, 8, step(small_grads, narrow))
    need(4, 5, 6, 7)
    each_block(big_block, (bd, bp, bl), 0, width // SUB, width // LANES, 8, step(big_grads, width))
    need(9)
    inner, outer, height, _ = parcel.shape
    height -= VECTOR_ROWS
    parcel[:, :, :VECTOR_ROWS, :] = vector_rows[...]
    chunks = []
    for t in range(LOOKUPS):
        rows = total[t, :, 0 : SUB * HIGHS[t]].T
        for c in range(CHUNKS[t]):
            first, last = c * LANES, (c + 1) * LANES
            pieces = []
            for high in range(first // SPLIT, (last - 1) // SPLIT + 1):
                start, end = max(first - high * SPLIT, 0), min(last - high * SPLIT, SPLIT)
                pieces.append(rows[SUB * high : SUB * (high + 1), start:end])
            chunks.append(jnp.concatenate(pieces, axis=1))
    table = jnp.concatenate(chunks, axis=0).astype(BF)
    for d in range(inner * outer):
        at = me[1] ^ d
        parcel[at % inner, at // inner, VECTOR_ROWS:, :] = table[d * height : (d + 1) * height]


def attend_matrix(ref, k, model):
    if ref.shape[1] == model:
        return ref[k]
    rows = model // ref.shape[0]
    return ref[:, k * rows : (k + 1) * rows, :].reshape(model, ref.shape[2])


def whole_matrix(ref, k):
    if len(ref.shape) == 3:
        return ref[k]
    value = ref[:, k]
    return value.reshape(value.shape[0] * value.shape[1], value.shape[2])


def norm_parts(values):
    center = values - jnp.mean(values, axis=-1, keepdims=True)
    spread = lax.rsqrt(jnp.mean(center * center, axis=-1, keepdims=True) + NORM_EPSILON)
    return center * spread, spread


def norm_back(scaled, xhat, spread):
    return spread * (
        scaled
        - jnp.mean(scaled, axis=-1, keepdims=True)
        - xhat * jnp.mean(scaled * xhat, axis=-1, keepdims=True)
    )


def head_lanes(head, width):
    lane = lax.broadcasted_iota(jnp.int32, (1, width), 1)
    return (lane >= head * HEAD_DIM) & (lane < (head + 1) * HEAD_DIM)


def peer_block(me, r, rows):
    return pl.ds(pl.multiple_of((me[0] ^ r) * rows, rows), rows)


def pack_rows(ref, value):
    half, columns = ref.shape[0], value.shape[1]
    ref[:, 0:columns] = value[:half]
    ref[:, columns:] = value[half:]


def unpack_rows(ref):
    columns = ref.shape[1] // 2
    return jnp.concatenate([ref[:, 0:columns], ref[:, columns:]], axis=0)


def forward_body(n_head, vector_row, need, done, *refs):
    rows_in, refs = refs[:n_head], refs[n_head:]
    me, big_counts, small_counts, weights, small_bias = refs[:5]
    big_bias, refs = refs[5 : 5 + BIG_PARTS], refs[5 + BIG_PARTS :]
    pieces = weights
    if vector_row == 0:
        pieces, refs = refs[0], refs[1:]
    normed, qkv, big_probs, small_probs, vectors, hidden_bias = refs[:6]
    mixed_out, (mixed, flat, stack) = refs[6 : 6 + n_head], refs[6 + n_head :]
    block = rows_in[0].shape[1]
    need(*range(n_head), n_head + 3)
    if vector_row == 0:
        need(n_head + 5 + BIG_PARTS)
    n_vectors, size = vectors.shape[0], vectors.shape[1] // pieces.shape[0]
    for d in range(pieces.shape[0]):
        parts = [pieces[d, pl.ds(vector_row + p * PIECE_ROWS, PIECE_ROWS), 0:size].astype(F32) for p in range(PIECES)]
        vectors[:, d * size : (d + 1) * size] = sum(parts[1:], parts[0])[:n_vectors]
    heads, width = big_probs.shape[:2]
    pairs, wide = small_probs.shape[1:3]
    narrow = wide // 2
    columns = qkv.shape[2]
    halves = width // LANES
    biases = [None] * 2
    for j in range(n_head):
        span = slice(j * columns, (j + 1) * columns)
        hidden_bias[j : j + 1, :] = vectors[7:8, span]
        for i in range(2):
            value = jnp.where(me[0] == j, vectors[4 + i : 5 + i, span], 0.0)
            biases[i] = value if j == 0 else biases[i] + value
    for r in range(n_head):
        xhat, _ = norm_parts(rows_in[r][0].astype(F32))
        normed[peer_block(me, r, block), :] = (xhat * vectors[0:1, :] + vectors[1:2, :]).astype(BF)
    done(0, 4, 5)
    for k in range(3):
        value = dot(normed[...], attend_matrix(weights, k, normed.shape[1]), NN)
        if k != 1:
            value = value + biases[k // 2]
        qkv[k] = value.astype(BF)
    done(1)
    need(*range(n_head + 4, n_head + 5 + BIG_PARTS))
    big_live = lax.broadcasted_iota(jnp.int32, (1, width), 1) < big_counts[0]
    small_live = []
    row = lax.broadcasted_iota(jnp.int32, (wide, wide), 0)
    lane = lax.broadcasted_iota(jnp.int32, (wide, wide), 1)
    for pair in range(pairs):
        first = (row < narrow) & (lane < small_counts[0, 2 * pair])
        second = (row >= narrow) & (lane >= narrow) & (lane < narrow + small_counts[0, 2 * pair + 1])
        small_live.append(first | second)

    def attend(span, extra, live, store):
        for head in range(heads):
            mine = head_lanes(head, columns)
            query = jnp.where(mine, qkv[0, span, :], 0.0)
            size = query.shape[0]
            scores = dot(query, qkv[1, span, :], NT) * SCALE + extra(head)
            scores = jnp.where(live, scores, NEGATIVE_FILL)
            power = jnp.exp(scores - jnp.max(scores, axis=-1, keepdims=True))
            probs = power * (1.0 / jnp.sum(power, axis=-1, keepdims=True))
            store(head, probs)
            rows = slice(head * size, (head + 1) * size)
            flat[:size, rows] = probs.astype(BF)
            stack[rows, :] = jnp.where(mine, qkv[2, span, :], 0.0)
        every = slice(0, heads * size)
        mixed[span, :] = dot(flat[:size, every], stack[every, :], NN).astype(BF)

    def big_extra(head):
        return jnp.concatenate(
            [jnp.concatenate([part[head, half] for part in big_bias], axis=0) for half in range(halves)], axis=1
        )

    def store_big(head, probs):
        big_probs[head] = probs

    attend(slice(0, width), big_extra, big_live, store_big)
    done(2)
    for pair in range(pairs):

        def small_extra(head, pair=pair):
            extra = small_bias[head, pair]
            return jnp.concatenate([extra, extra], axis=0)

        def store_small(head, probs, pair=pair):
            small_probs[head, pair] = probs

        span = slice(width + pair * wide, width + (pair + 1) * wide)
        attend(span, small_extra, small_live[pair], store_small)
    done(3)
    for r in range(n_head):
        pack_rows(mixed_out[r], mixed[peer_block(me, r, block), :])


def put_matrix(ref, k, value):
    if len(ref.shape) == 3:
        ref[k] = value
        return
    rows, columns = ref.shape[2], value.shape[1]
    side = slice(k % 2 * columns, (k % 2 + 1) * columns)
    for d in range(ref.shape[0]):
        ref[d, k // 2, :, side] = value[d * rows : (d + 1) * rows]


def backward_body(n_head, need, done, *refs):
    need(*range(n_head), n_head + 1, n_head + 2)
    grads_in, refs = refs[:n_head], refs[n_head:]
    me, qkv, small_probs, big_probs, weights, small_rows, big_rows, dqkv, column_sums = refs[:9]
    rows_out, (grad_heads, tall, flat, stacks) = refs[9 : 9 + n_head], refs[9 + n_head :]
    heads, width = big_probs.shape[:2]
    pairs, wide = small_probs.shape[1:3]
    narrow = wide // 2
    columns = qkv.shape[2]
    halves = width // LANES
    block = 2 * grads_in[0].shape[0]
    for r in range(n_head):
        grad_heads[peer_block(me, r, block), :] = unpack_rows(grads_in[r])

    need(n_head + 3)

    def attend(span, all_probs, store):
        for head in range(heads):
            mine = head_lanes(head, columns)
            probs = all_probs(head)
            upper = jnp.where(mine, grad_heads[span, :], 0.0)
            size = upper.shape[0]
            grad_probs = dot(upper, qkv[2, span, :], NT)
            inner = jnp.sum(probs * grad_probs, axis=-1, keepdims=True)
            grad_scores = (probs * (grad_probs - inner)).astype(BF)
            rows = slice(head * size, (head + 1) * size)
            tall[0, rows, :size] = grad_scores
            tall[1, rows, :size] = probs.astype(BF)
            flat[:size, rows] = grad_scores
            stacks[0, rows, :] = jnp.where(mine, qkv[0, span, :], 0.0)
            stacks[1, rows, :] = jnp.where(mine, qkv[1, span, :], 0.0)
            stacks[2, rows, :] = upper
            store(head, grad_scores.astype(F32))
        every = slice(0, heads * size)
        dqkv[0, span, :] = (dot(flat[:size, every], stacks[1, every, :], NN) * SCALE).astype(BF)
        dqkv[1, span, :] = (dot(tall[0, every, :size], stacks[0, every, :], TN) * SCALE).astype(BF)
        dqkv[2, span, :] = dot(tall[1, every, :size], stacks[2, every, :], TN).astype(BF)

    for pair in range(pairs):

        def store_small(head, value, at=pair * narrow * SUB):
            small_rows[pl.ds(at + head, narrow, stride=SUB), :] = value[:narrow] + value[narrow:]

        span = slice(width + pair * wide, width + (pair + 1) * wide)
        attend(span, lambda head, pair=pair: small_probs[head, pair], store_small)
    done(0)

    def store_big(head, value):
        for half in range(halves):
            big_rows[pl.ds(half * width * SUB + head, width, stride=SUB), :] = value[
                :, LANES * half : LANES * (half + 1)
            ]

    attend(slice(0, width), lambda head: big_probs[head], store_big)
    done(1, 2)
    need(n_head + 4)
    column_sums[...] = jnp.zeros_like(column_sums)
    for i, k in enumerate((0, 2)):
        column_sums[i, pl.ds(me[0], 1), :] = jnp.sum(dqkv[k].astype(F32), axis=0, keepdims=True)
    for r in range(n_head):
        rows = peer_block(me, r, block)
        model = rows_out[r].shape[1]
        total = dot(dqkv[0, rows, :], attend_matrix(weights, 0, model), NT)
        total = total + dot(dqkv[1, rows, :], attend_matrix(weights, 1, model), NT)
        total = total + dot(dqkv[2, rows, :], attend_matrix(weights, 2, model), NT)
        rows_out[r][...] = total.astype(BF)


def middle_body(n_head, need, done, *refs):
    mixed, refs = refs[:n_head], refs[n_head:]
    me, rows, upper, vectors, hidden_bias = refs[:5]
    weights, refs = refs[5 : 5 + n_head], refs[5 + n_head :]
    layer_out, grad_hidden, sums, pre_sums, normed_grad, act_pre = refs[:6]
    grad_heads = refs[6:]
    need(*range(n_head + 5))
    columns = mixed[0].shape[1] // 2
    hidden = rows[...].astype(F32) + vectors[6:7, :]
    for r in range(n_head):
        need(n_head + 5 + r)
        hidden = hidden + dot(unpack_rows(mixed[r]), whole_matrix(weights[r], 0), NT)
    xhat, spread = norm_parts(hidden)
    low = (xhat * vectors[2:3, :] + vectors[3:4, :]).astype(BF)
    normed_grad[0] = low
    cotangent = upper[...]
    final = hidden + vectors[8:9, :]
    grad_normed = jnp.zeros_like(hidden)
    for r in range(n_head):
        peer = me[0] ^ r
        into, down = whole_matrix(weights[r], 1), whole_matrix(weights[r], 2)
        pre = dot(low, into, NN) + hidden_bias[pl.ds(peer, 1), :]
        phi = 0.5 * (1.0 + lax.erf(pre * (0.5**0.5)))
        active = (pre * phi).astype(BF)
        final = final + dot(active, down, NT)
        slope = phi + pre * jnp.exp(-0.5 * pre * pre) * (0.5 / jnp.pi) ** 0.5
        low_grad = (dot(cotangent, down, NN) * slope).astype(BF)
        pre_sums[pl.ds(peer, 1), :] = jnp.sum(low_grad.astype(F32), axis=0, keepdims=True)
        grad_normed = grad_normed + dot(low_grad, into, NT)
        act_pre[peer, :, 0:columns] = active
        act_pre[peer, :, columns : 2 * columns] = low_grad
    layer_out[...] = final.astype(BF)
    wide = cotangent.astype(F32)
    grad = wide + norm_back(grad_normed * vectors[2:3, :], xhat, spread)
    grad_hidden[...] = grad
    grad_small = grad.astype(BF)
    normed_grad[1] = grad_small
    for r in range(n_head):
        pack_rows(grad_heads[r], dot(grad_small, whole_matrix(weights[r], 0), NN).astype(BF))
    sums[0:1, :] = jnp.sum(grad_normed * xhat, axis=0, keepdims=True)
    sums[1:2, :] = jnp.sum(grad_normed, axis=0, keepdims=True)
    sums[2:3, :] = jnp.sum(grad, axis=0, keepdims=True)
    sums[3:4, :] = jnp.sum(wide, axis=0, keepdims=True)


def weight_grads_body(n_head, need, done, *refs):
    given, mixed, refs = refs[:n_head], refs[n_head : 2 * n_head], refs[2 * n_head :]
    me, act_pre, normed_one, dqkv = refs[:4]
    normed_grad, out = refs[4 : 4 + n_head], refs[-1]
    columns = mixed[0].shape[1] // 2

    def all_rows(pick):
        return jnp.concatenate([pick(me[0] ^ r) for r in range(n_head)], axis=0)

    need(2 * n_head + 2, 2 * n_head + 3)
    for k in range(3):
        put_matrix(out, k, dot(normed_one[...], dqkv[k], TN).astype(BF))
    need(*range(2 * n_head), 2 * n_head + 1, *range(2 * n_head + 4, 3 * n_head + 4))
    heads_out = jnp.concatenate([unpack_rows(m) for m in mixed], axis=0)
    put_matrix(out, 3, dot(jnp.concatenate([n[1] for n in normed_grad], axis=0), heads_out, TN).astype(BF))
    grad_pre = all_rows(lambda p: act_pre[p, :, columns : 2 * columns])
    put_matrix(out, 4, dot(jnp.concatenate([n[0] for n in normed_grad], axis=0), grad_pre, TN).astype(BF))
    cotangent = jnp.concatenate([g[1] for g in given], axis=0)
    put_matrix(out, 5, dot(cotangent, all_rows(lambda p: act_pre[p, :, 0:columns]), TN).astype(BF))


def merge_body(need, done, *refs):
    parts, out = refs[:-1], refs[-1]
    need(*range(len(parts)))
    value = parts[0][...].astype(F32)
    for part in parts[1:]:
        value = value + part[...].astype(F32)
    out[...] = value.astype(BF)


def input_body(n_head, n_vectors, need, done, *refs):
    parts, refs = refs[:n_head], refs[n_head:]
    me, rows, grad_hidden, vectors, sums, column_sums, pre_sums, input_grad, vector_rows, terms = refs
    need(*range(n_head), *range(n_head + 1, n_head + 7))
    grad_normed = parts[0][...].astype(F32)
    for part in parts[1:]:
        grad_normed = grad_normed + part[...].astype(F32)
    xhat, spread = norm_parts(rows[...].astype(F32))
    input_grad[...] = (grad_hidden[...] + norm_back(grad_normed * vectors[0:1, :], xhat, spread)).astype(BF)
    done(0)
    columns = column_sums.shape[2]
    terms[...] = jnp.zeros_like(terms)
    terms[0:1, :] = jnp.sum(grad_normed * xhat, axis=0, keepdims=True)
    terms[1:2, :] = jnp.sum(grad_normed, axis=0, keepdims=True)
    terms[2:4, :] = sums[0:2, :]
    terms[6:7, :] = sums[2:3, :]
    terms[8:9, :] = sums[3:4, :]
    for j in range(n_head):
        span = slice(j * columns, (j + 1) * columns)
        for i in range(2):
            terms[4 + i : 5 + i, span] = column_sums[i, j : j + 1, :]
        terms[7:8, span] = pre_sums[j : j + 1, :]
    inner, outer = vector_rows.shape[:2]
    lanes = vectors.shape[1] // (inner * outer)
    vector_rows[...] = jnp.zeros_like(vector_rows)
    for d in range(inner * outer):
        at = me[1] ^ d
        vector_rows[at % inner, at // inner, :, 0:lanes] = terms[:, d * lanes : (d + 1) * lanes].astype(BF)


def adamw_update(weight, first_moment, second_moment, gradient, learn_rate):
    first_new = BETA_FIRST * first_moment + (1.0 - BETA_FIRST) * gradient
    second_new = BETA_SECOND * second_moment + (1.0 - BETA_SECOND) * gradient * gradient
    first_hat = first_new / (1.0 - BETA_FIRST**ADAM_STEP)
    second_hat = second_new / (1.0 - BETA_SECOND**ADAM_STEP)
    weight_new = weight - learn_rate * (
        first_hat / (jnp.sqrt(second_hat) + ADAM_EPSILON) + WEIGHT_DECAY * weight
    )
    return (weight_new, first_new, second_new)


def told_body(need, done, arrived, *refs):
    parts, (shards, shard, told) = refs[:-3], refs[-3:]
    need(0)
    rest = arrived[0].astype(F32)
    for d in range(1, arrived.shape[0]):
        rest = rest + arrived[d].astype(F32)
    columns = shards.shape[2]
    for k in range(shards.shape[0]):
        shards[k] = rest[k // 2, :, k % 2 * columns : (k % 2 + 1) * columns]
    done(0)
    need(*range(1, len(parts) + 1))
    value = parts[0][...].astype(F32)
    for part in parts[1:]:
        value = value + part[...].astype(F32)
    table = value[VECTOR_ROWS:]
    shard[...] = table
    here = jnp.sum(table * table).reshape(1, 1) + jnp.sum(rest * rest).reshape(1, 1)
    tail = value[MESSAGE_ROWS : MESSAGE_ROWS + 1]
    free = LANES // 4
    gap = jnp.zeros((1, LANES - free), F32)
    spill = [jnp.concatenate([gap, tail[:, q * free : (q + 1) * free]], axis=1) for q in range(3)]
    spill = jnp.concatenate(spill + [jnp.zeros((MESSAGE_ROWS - 3, LANES), F32)], axis=0)
    message = jnp.where(corner_mask(), here, value[:MESSAGE_ROWS] + spill)
    told[...] = jnp.broadcast_to(message[None], told.shape)


def corner_mask():
    row = lax.broadcasted_iota(jnp.int32, (MESSAGE_ROWS, LANES), 0)
    lane = lax.broadcasted_iota(jnp.int32, (MESSAGE_ROWS, LANES), 1)
    return (row == MESSAGE_ROWS - 1) & (lane == LANES - 1)


def update_body(n_head, n_vectors, need, done, *refs):
    need(1)
    me, told, shards, out_shard, down_shard, table_shard = refs[:6]
    params, outs = refs[6:21], refs[21:36]
    norm_out = refs[36]
    n_dp = told.shape[0] // n_head

    def merged(d):
        value = told[d * n_head]
        for j in range(1, n_head):
            value = value + told[d * n_head + j]
        return value

    corner = corner_mask()

    def square(d, total):
        value = merged(d)
        return total + jnp.where(corner, value, value * value)

    total = lax.fori_loop(0, n_dp, square, jnp.zeros((MESSAGE_ROWS, LANES), F32))
    grad_norm = jnp.sqrt(jnp.sum(total).reshape(1, 1))
    norm_out[...] = jnp.broadcast_to(grad_norm, norm_out.shape)
    factor = CLIP_NORM / jnp.maximum(grad_norm, CLIP_NORM)

    def update(at, gradient, rate, pick=...):
        weight, first, second = (ref[pick] for ref in params[3 * at : 3 * at + 3])
        for ref, value in zip(outs[3 * at : 3 * at + 3], adamw_update(weight, first, second, gradient * factor, rate)):
            ref[pick] = value

    for k in range(3):
        update(0, shards[k], RATE_MATRIX, k)
    update(0, shards[4], RATE_MATRIX, 3)
    update(1, out_shard[...], RATE_OUTPUT)
    update(2, down_shard[...], RATE_MATRIX)
    mine, free = merged(me[1]), LANES // 4
    tail = jnp.concatenate([mine[q : q + 1, LANES - free :] for q in range(3)], axis=1)
    mine = jnp.concatenate([mine[:, : LANES - free], tail], axis=0)
    size = params[9].shape[1]
    gradient = jnp.zeros((n_vectors, size), F32)
    for j in range(n_head):
        gradient = jnp.where(me[0] == j, mine[:n_vectors, j * size : (j + 1) * size], gradient)
    update(3, gradient, RATE_VECTOR)
    heads = params[12].shape[0]
    for c in range(table_shard.shape[0] // heads):
        update(4, table_shard[c * heads : (c + 1) * heads, :], RATE_VECTOR, (slice(None), slice(c * LANES, (c + 1) * LANES)))


def exchange(value, axis):
    return lax.all_to_all(value, axis, split_axis=0, concat_axis=0, tiled=True)


def spread_all(value, axis):
    size = lax.axis_size(axis)
    return exchange(jnp.broadcast_to(value[None], (size, *value.shape)), axis)


def swap(values, n_head):
    return [values[0]] + [
        lax.ppermute(values[r], "head", [(i, i ^ r) for i in range(n_head)]) for r in range(1, n_head)
    ]


def struct(shape, dtype):
    return jax.ShapeDtypeStruct(shape, dtype)


def on_device(
    node_rows,
    output_grad,
    weight_in,
    first_in,
    second_in,
    weight_out,
    first_out,
    second_out,
    weight_down,
    first_down,
    second_down,
    vectors,
    first_vectors,
    second_vectors,
    bias_table,
    first_table,
    second_table,
    big_counts,
    small_counts,
    big_distance,
    small_distance,
    big_paths,
    small_paths,
    big_lengths,
    small_lengths,
):
    everyone = ("dp", "head")
    n_dp, n_head = lax.axis_size("dp"), lax.axis_size("head")
    head_index, dp_index = lax.axis_index("head"), lax.axis_index("dp")
    me = head_index.reshape(1).astype(jnp.int32)
    shard_rows, columns = weight_in.shape[1], weight_in.shape[2]
    model = shard_rows * n_dp
    my_rows = node_rows.shape[0]
    group_rows = my_rows * n_head
    heads = columns // HEAD_DIM
    width, narrow = big_distance.shape[1], small_distance.shape[1]
    pairs = small_distance.shape[0] // 2
    table_chunks = bias_table.shape[0] // LANES
    all_chunks = table_chunks * n_dp
    n_vectors, shard_width = vectors.shape
    stacked = shard_rows % 16 == 0
    big_ints = (big_distance, big_paths, big_lengths)
    small_ints = (small_distance, small_paths, small_lengths)
    inner = inner_of(n_dp)
    outer = n_dp // inner
    dp_pairs = lambda k: [(i, i ^ k) for i in range(n_dp)]
    us = jnp.stack([head_index, dp_index]).astype(jnp.int32)
    lanes_used = model // n_dp

    def far_shards(value):
        return [value] + [lax.ppermute(value, "dp", dp_pairs(k)) for k in range(inner, n_dp, inner)]

    def near_shards(values):
        value = jnp.stack(values)
        return [value] + [lax.ppermute(value, "dp", dp_pairs(k)) for k in range(1, inner)]

    def to_head(value, r):
        return lax.ppermute(value, "head", [(i, i ^ r) for i in range(n_head)])

    far = n_head // 2
    near_heads = range(1, far)

    rest_sent = jnp.stack([weight_out.astype(BF).T, weight_in[3].astype(BF), weight_down.astype(BF).T])
    rest_sent, my_table = lax.optimization_barrier((rest_sent, bias_table))
    with jax.named_scope("rest_far"):
        rest_far = far_shards(rest_sent)
    table_sent = my_table.astype(BF).T.reshape(heads, table_chunks, LANES).transpose(1, 0, 2)
    with jax.named_scope("table_all"):
        table_all = spread_all(table_sent, "dp").reshape(all_chunks * heads, LANES)
    given = {0: jnp.stack([node_rows, output_grad])}
    with jax.named_scope("rows_far"):
        given[far] = to_head(given[0], far)
    qkv_sent = weight_in[:3].astype(BF)
    with jax.named_scope("vectors_head"):
        own_vectors = lax.dynamic_update_slice_in_dim(
            jnp.zeros((n_vectors, lanes_used), F32), vectors, head_index * shard_width, 1
        )
        step = far
        while step:
            own_vectors = own_vectors + to_head(own_vectors, step)
            step //= 2
    rest, pieces = own_vectors, []
    for _ in range(PIECES):
        piece = lax.reduce_precision(rest, 8, 7)
        rest = rest - piece
        pieces.append(jnp.pad(piece.astype(BF), ((0, PIECE_ROWS - n_vectors), (0, columns - lanes_used))))
    qkv_sent = jnp.concatenate([qkv_sent.reshape(3 * shard_rows, columns), *pieces])
    qkv_sent, *rest_far = lax.optimization_barrier((qkv_sent, *rest_far))
    with jax.named_scope("rest_near"):
        rest_near = near_shards(rest_far)
    with jax.named_scope("qkv_far"):
        qkv_far = far_shards(qkv_sent)

    def pair_bias(part, table, ints):
        rows = width // sum(BIG_QUARTERS) * BIG_QUARTERS[part]
        big_range = struct((heads, width // LANES, rows, LANES), F32)
        return kernel_call(
            lambda *refs: bias_body(part, *refs),
            ([struct((heads, pairs, narrow, LANES), F32)] if part == 0 else []) + [big_range],
            "pair_bias",
            12 if part == 0 else 20,
            (table, *ints),
            [
                pltpu.VMEM((heads, all_chunks // 2, SUB, LANES), jnp.int32),
                pltpu.VMEM((len(PRODUCTS), max(CHUNKS) * heads, LANES), BF),
                pltpu.VMEM((len(PRODUCTS), heads * SUB, LANES), F32),
            ],
        )

    small_bias, *big_bias = pair_bias(0, table_all, (*small_ints, *big_ints))
    held = lax.optimization_barrier((small_bias, table_all, given[far], *rest_near, *qkv_far))
    (small_bias, table_all, given[far]), held = held[:3], held[3:]
    rest_near, qkv_far = held[:inner], held[inner:]
    weights_rest = jnp.concatenate(rest_near)
    with jax.named_scope("qkv_near"):
        qkv_near = near_shards(qkv_far)
    if not stacked:
        order = jnp.argsort(jnp.array(xor_order(n_dp), jnp.int32) ^ dp_index)
        weights_rest = weights_rest[order].transpose(1, 0, 2, 3).reshape(3, model, columns)
    weights_held = {0: weights_rest}
    with jax.named_scope("rest_far_head"):
        weights_held[far] = to_head(weights_rest, far)
    with jax.named_scope("rows_near"):
        for r in near_heads:
            given[r], given[far + r] = to_head(given[0], r), to_head(given[far], r)
    for part in range(1, BIG_PARTS):
        big_bias += pair_bias(part, table_all, big_ints)
    held = lax.optimization_barrier((big_bias[-1], *qkv_near, *[given[r] for r in range(n_head)]))
    big_bias[-1], qkv_near, given = held[0], held[1 : 1 + inner], held[1 + inner :]
    with jax.named_scope("rest_near_head"):
        for r in near_heads:
            weights_held[r] = to_head(weights_held[0], r)
    weights_attend = list(qkv_near)
    vector_row, vector_pieces = 3 * shard_rows, ()
    if not stacked:
        weights_attend = jnp.concatenate(qkv_near)[order]
        vector_row, vector_pieces = 0, (weights_attend[:, 3 * shard_rows :],)
        weights_attend = weights_attend[:, : 3 * shard_rows].reshape(n_dp, 3, shard_rows, columns)
        weights_attend = weights_attend.transpose(1, 0, 2, 3).reshape(3, model, columns)

    block = struct((my_rows // 2, 2 * columns), BF)
    rows_block = struct((my_rows, model), BF)
    normed_one, qkv, big_probs, small_probs, all_vectors, hidden_bias, *mixed = kernel_call(
        lambda *refs: forward_body(n_head, vector_row, *refs),
        [
            struct((group_rows, model), BF),
            struct((3, group_rows, columns), BF),
            struct((heads, width, width), F32),
            struct((heads, pairs, 2 * narrow, 2 * narrow), F32),
            struct((n_vectors, model), F32),
            struct((n_head, columns), F32),
            *[block] * n_head,
        ],
        "attend_forward",
        12,
        (*given, us, big_counts, small_counts, weights_attend, small_bias, *big_bias, *vector_pieces),
        [
            pltpu.VMEM((group_rows, columns), BF),
            pltpu.VMEM((width, heads * width), BF),
            pltpu.VMEM((heads * width, columns), BF),
        ],
        range(n_head, n_head + 3),
        (n_head + 3,) if stacked else (),
        n_head,
    )
    with jax.named_scope("mixed_rows"):
        mixed_rows = swap(mixed, n_head)
    mixed_rows[0], *held = lax.optimization_barrier((mixed_rows[0], *[weights_held[r] for r in range(far + 1)]))
    weights_held.update(enumerate(held))
    with jax.named_scope("rest_near_head"):
        for r in near_heads:
            weights_held[far + r] = to_head(weights_held[far], r)
    weights_rest = [weights_held[r] for r in range(n_head)]

    layer_out, grad_hidden, sums, pre_sums, normed_grad, act_pre, *grad_heads = kernel_call(
        lambda *refs: middle_body(n_head, *refs),
        [
            rows_block,
            struct((my_rows, model), F32),
            struct((4, model), F32),
            struct((n_head, columns), F32),
            struct((2, my_rows, model), BF),
            struct((n_head, my_rows, 2 * columns), BF),
            *[block] * n_head,
        ],
        "feed_forward",
        6,
        (*mixed_rows, us, node_rows, output_grad, all_vectors, hidden_bias, *weights_rest),
        (),
        (n_head,),
        range(n_head + 5, 2 * n_head + 5) if stacked else (),
        n_head,
    )
    with jax.named_scope("grad_heads"):
        grad_heads = swap(grad_heads, n_head)
    with jax.named_scope("act_pre"):
        act_pre = exchange(act_pre, "head")
    with jax.named_scope("normed_grad"):
        rows_held = {0: normed_grad}
        for r in (far, *range(1, far)):
            rows_held[r] = lax.ppermute(normed_grad, "head", [(i, i ^ r) for i in range(n_head)])

    small_rows, big_rows, dqkv, column_sums, *rows_sent = kernel_call(
        lambda *refs: backward_body(n_head, *refs),
        [
            struct((pairs * narrow * SUB, LANES), F32),
            struct((width // LANES * width * SUB, LANES), F32),
            struct((3, group_rows, columns), BF),
            struct((2, n_head, columns), F32),
            *[rows_block] * n_head,
        ],
        "attend_backward",
        14,
        (*grad_heads, us, qkv, small_probs, big_probs, weights_attend),
        [
            pltpu.VMEM((group_rows, columns), BF),
            pltpu.VMEM((2, heads * width, width), BF),
            pltpu.VMEM((width, heads * width), BF),
            pltpu.VMEM((3, heads * width, columns), BF),
        ],
        (n_head,),
        (n_head + 4,) if stacked else (),
        n_head,
    )
    small_rows, act_pre, *arrived = lax.optimization_barrier(
        (small_rows, act_pre, *[rows_held[r] for r in range(1, far + 1)])
    )
    rows_held.update(zip(range(1, far + 1), arrived))
    with jax.named_scope("normed_grad"):
        for r in range(1, far):
            rows_held[far + r] = lax.ppermute(rows_held[far], "head", [(i, i ^ r) for i in range(n_head)])
    (weight_grads,) = kernel_call(
        lambda *refs: weight_grads_body(n_head, *refs),
        [struct((n_dp, 3, shard_rows, 2 * columns) if stacked else (6, model, columns), BF)],
        "weight_grads",
        6,
        (*given, *mixed, us, act_pre, normed_one, dqkv, *[rows_held[r] for r in range(n_head)]),
        (),
        (2 * n_head,),
        early=(2 * n_head + 2, 2 * n_head + 3),
    )
    if not stacked:
        weight_grads = weight_grads.reshape(3, 2, n_dp, shard_rows, columns).transpose(2, 0, 3, 1, 4)
        weight_grads = weight_grads.reshape(n_dp, 3, shard_rows, 2 * columns)
    with jax.named_scope("grad_normed_one"):
        rows_back = swap(rows_sent, n_head)
    _, *rows_back = lax.optimization_barrier((weight_grads, *rows_back))
    with jax.named_scope("weight_grads"):
        weights_arrived = exchange(weight_grads, "dp")
    input_grad, vector_rows = kernel_call(
        lambda *refs: input_body(n_head, n_vectors, *refs),
        [rows_block, struct((inner, outer, VECTOR_ROWS, LANES), BF)],
        "input_grad",
        3,
        (*rows_back, us, node_rows, grad_hidden, all_vectors, sums, column_sums, pre_sums),
        [pltpu.VMEM((VECTOR_ROWS, model), F32)],
        (n_head,),
    )
    table_rows = table_chunks * heads
    block = struct((outer, VECTOR_ROWS + table_rows, LANES), BF)
    inner_sent = kernel_call(
        scatter_body,
        [(inner, block)],
        "table_scatter",
        40,
        (small_rows, *small_ints, big_rows, *big_ints, us, vector_rows),
        [pltpu.VMEM((LOOKUPS, SPLIT, SUB * max(HIGHS)), F32)],
        (8,),
    )
    with jax.named_scope("table_inner"):
        arrived = [inner_sent[0]] + [lax.ppermute(inner_sent[k], "dp", dp_pairs(k)) for k in range(1, inner)]
    outer_sent = kernel_call(
        merge_body,
        [(outer, struct(block.shape[1:], BF))],
        "merge_table",
        1,
        tuple(arrived),
    )
    with jax.named_scope("table_outer"):
        parts = [outer_sent[0]] + [
            lax.ppermute(outer_sent[k], "dp", dp_pairs(k * inner)) for k in range(1, outer)
        ]
    weights_arrived, *parts = lax.optimization_barrier((weights_arrived, *parts))
    shards, table_shard, told = kernel_call(
        told_body,
        [
            struct((6, shard_rows, columns), F32),
            struct((table_rows, LANES), F32),
            struct((n_dp * n_head, MESSAGE_ROWS, LANES), F32),
        ],
        "shard_sums",
        4,
        (weights_arrived, *parts),
    )
    with jax.named_scope("squares"):
        told = exchange(told, everyone)
    params = (weight_in, first_in, second_in, weight_out, first_out, second_out)
    params += (weight_down, first_down, second_down, vectors, first_vectors, second_vectors)
    params += (bias_table.T, first_table.T, second_table.T)
    *updated, grad_norm = kernel_call(
        lambda *refs: update_body(n_head, n_vectors, *refs),
        [*[struct(p.shape, F32) for p in params], struct((1, LANES), F32)],
        "update",
        3,
        (us, told, shards, shards[3].T, shards[5].T, table_shard, *params),
        (),
        (0,),
        ready=range(2, 21),
        limit=16 << 20,
    )
    updated = updated[:12] + [value.T for value in updated[12:]]
    return (layer_out, input_grad, grad_norm[0, 0], *updated)


def solution(mesh):
    rows = P(("dp", "head"), None)
    square = P(None, "dp", "head")
    across = P("head", "dp")
    thin = P(None, ("dp", "head"))
    table = P("dp", "head")
    return jax.shard_map(
        on_device,
        mesh=mesh,
        in_specs=(rows, rows)
        + (square,) * 3
        + (across,) * 6
        + (thin,) * 3
        + (table,) * 3
        + (P("dp"), P("dp", None))
        + (P("dp", None, None),) * 2
        + (P(None, "dp", None, None),) * 2
        + (P("dp", None, None),) * 2,
        out_specs=(rows, rows, P()) + (square,) * 3 + (across,) * 6 + (thin,) * 3 + (table,) * 3,
        check_vma=False,
    )
```
